32 devices in a mesh: rep: 4 (over x, core), shard: 8 (over z, y).
Axes of the slice: x: 2, y: 2, z: 4, core: 2. Of those that a mesh axis runs over, the one named last changes fastest.
Arguments:
- tokens: bfloat16 [16384, 1024], P(('rep', 'shard')), may hold values from -6 to 6
- cotangent: bfloat16 [16384, 1024], P(('rep', 'shard')), may hold values from -6 to 6
- seq_lengths: int32 [32, 8], P(('rep', 'shard')), may hold values from 0 to 512, as said below
- mixer_in: float32 [1024, 4120], P('shard'), may hold values from -0.1875 to 0.1875
- mixer_in_mean: float32 [1024, 4120], P('shard'), may hold values from -20 to 20
- mixer_in_square: float32 [1024, 4120], P('shard'), may hold values from 52.4288 to 206.4384
- mixer_out: float32 [2048, 1024], P('shard'), may hold values from -0.1875 to 0.1875
- mixer_out_mean: float32 [2048, 1024], P('shard'), may hold values from -64 to 64
- mixer_out_square: float32 [2048, 1024], P('shard'), may hold values from 573.44 to 2293.76
- swiglu_in: float32 [1024, 4096], P('shard'), may hold values from -0.1875 to 0.1875
- swiglu_in_mean: float32 [1024, 4096], P('shard'), may hold values from -32 to 32
- swiglu_in_square: float32 [1024, 4096], P('shard'), may hold values from 144.1792 to 573.44
- swiglu_out: float32 [2048, 1024], P('shard'), may hold values from -0.125 to 0.125
- swiglu_out_mean: float32 [2048, 1024], P('shard'), may hold values from -40 to 40
- swiglu_out_square: float32 [2048, 1024], P('shard'), may hold values from 206.4384 to 819.2
- gains: float32 [3584], P('shard'), may hold values from 0.5 to 1.5
- gains_mean: float32 [3584], P('shard'), may hold values from -64 to 64
- gains_square: float32 [3584], P('shard'), may hold values from 573.44 to 2293.76
- conv_kernel: float32 [5, 1792], P(None, 'shard'), may hold values from -3 to 3
- conv_kernel_mean: float32 [5, 1792], P(None, 'shard'), may hold values from -32 to 32
- conv_kernel_square: float32 [5, 1792], P(None, 'shard'), may hold values from 144.1792 to 573.44
- head_params: float32 [3, 24], replicated, may hold values from -4 to 2.7, as said below
- head_params_mean: float32 [3, 24], replicated, may hold values from -224 to 224
- head_params_square: float32 [3, 24], replicated, may hold values from 5242.88 to 20643.84
Outputs:
- block_out: bfloat16 [16384, 1024], P(('rep', 'shard'))
- tokens_grad: float32 [16384, 1024], P(('rep', 'shard'))
- mixer_in_new: float32 [1024, 4120], P('shard')
- mixer_in_mean_new: float32 [1024, 4120], P('shard')
- mixer_in_square_new: float32 [1024, 4120], P('shard')
- mixer_out_new: float32 [2048, 1024], P('shard')
- mixer_out_mean_new: float32 [2048, 1024], P('shard')
- mixer_out_square_new: float32 [2048, 1024], P('shard')
- swiglu_in_new: float32 [1024, 4096], P('shard')
- swiglu_in_mean_new: float32 [1024, 4096], P('shard')
- swiglu_in_square_new: float32 [1024, 4096], P('shard')
- swiglu_out_new: float32 [2048, 1024], P('shard')
- swiglu_out_mean_new: float32 [2048, 1024], P('shard')
- swiglu_out_square_new: float32 [2048, 1024], P('shard')
- gains_new: float32 [3584], P('shard')
- gains_mean_new: float32 [3584], P('shard')
- gains_square_new: float32 [3584], P('shard')
- conv_kernel_new: float32 [5, 1792], P(None, 'shard')
- conv_kernel_mean_new: float32 [5, 1792], P(None, 'shard')
- conv_kernel_square_new: float32 [5, 1792], P(None, 'shard')
- head_params_new: float32 [3, 24], replicated
- head_params_mean_new: float32 [3, 24], replicated
- head_params_square_new: float32 [3, 24], replicated
The draws below stay inside these ranges and needn't reach their ends.
Inputs may be any that keep to these rules, and one draw needn't show every extreme that they name: `seq_lengths`: row b gives the lengths of the sequences of block b in order, 0 for unused entries; a row sums to 128 or more and 512 or less; some block holds one sequence of 512 tokens. `head_params`: row 0 within -4 to -1, row 1 within -0.5 to 2.7, row 2 within 0.5 to 1.5.
All inputs are finite; a program needn't handle non-finite values.
Results may differ from the reference program's by a relative error of at most 0.012.
The reference program's roundings to bfloat16 on the way count: a program that leaves them out, or rounds other values in their place, can miss the bound.
Values may be sent and summed in bfloat16 or wider, within the bound.
No kernel may reach another device: no remote copies, remote signals or barrier semaphores. Data moves between devices by JAX's collectives and lax.ppermute only.
A program may use at most 256 MiB of HBM per device.

```python
import math
import jax
import jax.numpy as jnp
from jax import lax

D = 1024
FF = 2048
QUERY_HEADS = 8
KEY_VALUE_HEADS = 2
HEAD_SIZE = 64
MH = 24
MP = 64
NS = 128
KC = 4
CAP = 512
SEQ_DEV = 8
STEP = 10
BLOCKS = 32
TOKENS = 16384
DIN = 4120
DOUT = 2048
GAINS = 3584
CONVW = 1792


def draw_seq_lengths(key, part):
    key = jax.random.fold_in(key, 11)
    block_index = jnp.arange(BLOCKS, dtype=jnp.int32)
    lowest = CAP // 3
    base_total = lowest + block_index * (CAP - lowest) // max(BLOCKS - 1, 1)
    jitter = jax.random.randint(jax.random.fold_in(key, 1), (BLOCKS,), 0, CAP // 8 + 1)
    totals = jnp.maximum(base_total - jitter, CAP // 4)
    totals = jnp.where(block_index == BLOCKS - 1, CAP, totals).astype(jnp.int32)
    cut_points = jax.random.randint(jax.random.fold_in(key, 2), (BLOCKS, SEQ_DEV - 1), 0, CAP + 1)
    cut_points = jnp.sort(cut_points, axis=1)
    scaled = cut_points * totals[:, None] // CAP
    bounds = jnp.concatenate([jnp.zeros((BLOCKS, 1), jnp.int32), scaled.astype(jnp.int32), totals[:, None]], axis=1)
    lengths = bounds[:, 1:] - bounds[:, :-1]
    single = jnp.zeros((SEQ_DEV,), jnp.int32).at[0].set(CAP)
    lengths = jnp.where((block_index == BLOCKS - 1)[:, None], single[None, :], lengths)
    return lengths.astype(jnp.int32)


def draw_head_params(key, part):
    key = jax.random.fold_in(key, 7)
    step_shift = jax.random.uniform(jax.random.fold_in(key, 1), (MH,), jnp.float32, -4.0, -1.0)
    decay_logs = jax.random.uniform(jax.random.fold_in(key, 2), (MH,), jnp.float32, -0.5, 2.7)
    skip_weight = jax.random.uniform(jax.random.fold_in(key, 3), (MH,), jnp.float32, 0.5, 1.5)
    return jnp.stack([step_shift, decay_logs, skip_weight])


def block_levels(own_key, dims, pieces, least, largest):
    level, own = 1.0, jax.random.fold_in(own_key, 6)
    for axis_at, parts in pieces:
        draws = jnp.exp(jax.random.uniform(jax.random.fold_in(own, axis_at), (parts,), jnp.float32, least / len(pieces), largest / len(pieces)))
        level = level * jnp.repeat(draws, dims[axis_at] // parts).reshape([-1 if axis == axis_at else 1 for axis in range(len(dims))])
    return level


def gaussian(rng, extent, deviation, reach, cuts=(), kind=jnp.bfloat16):
    array = jax.random.normal(rng, extent, jnp.float32) * deviation
    if len(cuts) > 0:
        array = block_levels(rng, extent, cuts, -0.22, 0.18) * array
    return jnp.clip(array, min=-reach, max=reach).astype(kind)


def setup_inputs(seed: int = 0) -> dict:
    splits = jax.random.split(jax.random.key(seed), 25)
    tokens = gaussian(splits[0], (TOKENS, D), 1.0, 6.0, ((0, 32),))
    cotangent = gaussian(splits[1], (TOKENS, D), 1.0, 6.0, ((0, 32),))
    seq_lengths = draw_seq_lengths(jax.random.fold_in(splits[24], 71), 0)
    mixer_in = gaussian(splits[3], (D, DIN), D ** -0.5, 0.1875, ((0, 8),), jnp.float32)
    mixer_in_mean = gaussian(splits[4], (D, DIN), (0.027 * (CAP * BLOCKS) ** 0.5), 20.0, ((0, 8),), jnp.float32)
    mixer_in_square = jnp.clip(jnp.exp(math.log(206.4384) - 1.370546 * jax.random.uniform(splits[5], (D, DIN), jnp.float32) ** block_levels(splits[5], (D, DIN), ((0, 8),), -0.2, 0.2)), 52.4288, 206.4384)
    mixer_out = gaussian(splits[6], (DOUT, D), D ** -0.5, 0.1875, ((0, 8),), jnp.float32)
    mixer_out_mean = gaussian(splits[7], (DOUT, D), (0.091 * (CAP * BLOCKS) ** 0.5), 64.0, ((0, 8),), jnp.float32)
    mixer_out_square = jnp.clip(jnp.exp(math.log(2293.76) - 1.3862944 * jax.random.uniform(splits[8], (DOUT, D), jnp.float32) ** block_levels(splits[8], (DOUT, D), ((0, 8),), -0.2, 0.2)), 573.44, 2293.76)
    swiglu_in = gaussian(splits[9], (D, 2 * FF), D ** -0.5, 0.1875, ((0, 8),), jnp.float32)
    swiglu_in_mean = gaussian(splits[10], (D, 2 * FF), (0.045 * (CAP * BLOCKS) ** 0.5), 32.0, ((0, 8),), jnp.float32)
    swiglu_in_square = jnp.clip(jnp.exp(math.log(573.44) - 1.38059635 * jax.random.uniform(splits[11], (D, 2 * FF), jnp.float32) ** block_levels(splits[11], (D, 2 * FF), ((0, 8),), -0.2, 0.2)), 144.1792, 573.44)
    swiglu_out = gaussian(splits[12], (FF, D), FF ** -0.5, 0.125, ((0, 8),), jnp.float32)
    swiglu_out_mean = gaussian(splits[13], (FF, D), (0.054 * (CAP * BLOCKS) ** 0.5), 40.0, ((0, 8),), jnp.float32)
    swiglu_out_square = jnp.clip(jnp.exp(math.log(819.2) - 1.3783262 * jax.random.uniform(splits[14], (FF, D), jnp.float32) ** block_levels(splits[14], (FF, D), ((0, 8),), -0.2, 0.2)), 206.4384, 819.2)
    gains = jnp.clip(1.0 + 0.1 * jax.random.normal(splits[15], (GAINS,), jnp.float32), 0.5, 1.5)
    gains_mean = gaussian(splits[16], (GAINS,), (0.091 * (CAP * BLOCKS) ** 0.5), 64.0, ((0, 8),), jnp.float32)
    gains_square = jnp.clip(jnp.exp(math.log(2293.76) - 1.3862944 * jax.random.uniform(splits[17], (GAINS,), jnp.float32) ** block_levels(splits[17], (GAINS,), ((0, 8),), -0.2, 0.2)), 573.44, 2293.76)
    conv_kernel = gaussian(splits[18], (KC + 1, CONVW), 0.5, 3.0, ((1, 8),), jnp.float32)
    conv_kernel_mean = gaussian(splits[19], (KC + 1, CONVW), (0.045 * (CAP * BLOCKS) ** 0.5), 32.0, ((1, 8),), jnp.float32)
    conv_kernel_square = jnp.clip(jnp.exp(math.log(573.44) - 1.38059635 * jax.random.uniform(splits[20], (KC + 1, CONVW), jnp.float32) ** block_levels(splits[20], (KC + 1, CONVW), ((1, 8),), -0.2, 0.2)), 144.1792, 573.44)
    head_params = draw_head_params(jax.random.fold_in(splits[24], 71), 0)
    head_params_mean = gaussian(splits[22], (3, MH), (0.27 * (CAP * BLOCKS) ** 0.5), 224.0, (), jnp.float32)
    head_params_square = jnp.clip(jnp.exp(jax.random.uniform(splits[23], (3, MH), jnp.float32, math.log(5242.88), math.log(20643.84))), 5242.88, 20643.84)
    return {"tokens": tokens, "cotangent": cotangent, "seq_lengths": seq_lengths, "mixer_in": mixer_in, "mixer_in_mean": mixer_in_mean, "mixer_in_square": mixer_in_square, "mixer_out": mixer_out, "mixer_out_mean": mixer_out_mean, "mixer_out_square": mixer_out_square, "swiglu_in": swiglu_in, "swiglu_in_mean": swiglu_in_mean, "swiglu_in_square": swiglu_in_square, "swiglu_out": swiglu_out, "swiglu_out_mean": swiglu_out_mean, "swiglu_out_square": swiglu_out_square, "gains": gains, "gains_mean": gains_mean, "gains_square": gains_square, "conv_kernel": conv_kernel, "conv_kernel_mean": conv_kernel_mean, "conv_kernel_square": conv_kernel_square, "head_params": head_params, "head_params_mean": head_params_mean, "head_params_square": head_params_square}


NORM_EPS = 1e-05
ROPE_BASE = 100000000000.0
BETA_MEAN = 0.9
BETA_SQUARE = 0.95
ADAM_EPS = 1e-08
DECAY = 0.1
MATRIX_RATE = 0.03
VECTOR_RATE = 0.5

@jax.custom_vjp
def low(v):
    return lax.optimization_barrier(v.astype(jnp.bfloat16)).astype(jnp.float32)

@jax.custom_vjp
def low_back(v):
    return v

def low_keep(v):
    return (low(v), None)

def low_pass(kept, grad):
    return (grad,)

def back_keep(v):
    return (v, None)

def back_low(kept, grad):
    return (low(grad),)
low.defvjp(low_keep, low_pass)
low_back.defvjp(back_keep, back_low)

def normalize(values, gain):
    return values * lax.rsqrt(lax.optimization_barrier(jnp.mean(values * values, axis=-1, keepdims=True)) + NORM_EPS) * gain

def layout(seq_row, span_length):
    count = seq_row.shape[0]
    ends = jnp.cumsum(seq_row).astype(jnp.int32)
    starts = (ends - seq_row).astype(jnp.int32)
    slots = jnp.arange(span_length, dtype=jnp.int32)
    segment = lax.optimization_barrier(jnp.sum((slots[:, None] >= ends[None, :]).astype(jnp.int32), axis=1)).astype(jnp.int32)
    valid = slots < ends[count - 1]
    segment = jnp.where(valid, segment, count + slots).astype(jnp.int32)
    match = segment[:, None] == jnp.arange(count, dtype=jnp.int32)[None, :]
    first = lax.optimization_barrier(jnp.sum(jnp.where(match, starts[None, :], 0), axis=1)).astype(jnp.int32)
    token_position = jnp.where(valid, slots - first, 0).astype(jnp.int32)
    return (segment, token_position, valid)

def apply_rotary(values, token_position):
    half = HEAD_SIZE // 2
    freq = ROPE_BASE ** (-(jnp.arange(half, dtype=jnp.float32) * 2.0 / HEAD_SIZE))
    angle = token_position.astype(jnp.float32)[:, None] * freq[None, :]
    cosine = jnp.cos(angle)[:, None, :]
    sine = jnp.sin(angle)[:, None, :]
    first_half = values[..., :half]
    second_half = values[..., half:]
    return jnp.concatenate([first_half * cosine - second_half * sine, second_half * cosine + first_half * sine], axis=-1)

def block_forward(block_tokens, weights, head_params, segment, token_position, precision):
    w_in, w_out, w_up, w_down, gain_all, kernel = weights
    span_length = block_tokens.shape[0]
    normed = low(normalize(block_tokens, gain_all[:D]))
    projected_input = low_back(jnp.dot(normed, w_in, precision=precision))
    key_offset = QUERY_HEADS * HEAD_SIZE
    value_offset = key_offset + KEY_VALUE_HEADS * HEAD_SIZE
    gate_offset = value_offset + KEY_VALUE_HEADS * HEAD_SIZE
    offset_c = gate_offset + MH * MP
    offset_t = offset_c + MH * MP + 2 * NS
    query_matrix = projected_input[:, :key_offset].reshape(span_length, QUERY_HEADS, HEAD_SIZE)
    key_matrix = projected_input[:, key_offset:value_offset].reshape(span_length, KEY_VALUE_HEADS, HEAD_SIZE)
    value_matrix = low(projected_input[:, value_offset:gate_offset].reshape(span_length, KEY_VALUE_HEADS, HEAD_SIZE))
    query_matrix = low(apply_rotary(query_matrix, token_position)).reshape(span_length, KEY_VALUE_HEADS, QUERY_HEADS // KEY_VALUE_HEADS, HEAD_SIZE)
    key_matrix = low(apply_rotary(key_matrix, token_position))
    slots = jnp.arange(span_length, dtype=jnp.int32)
    allowed = (segment[:, None] == segment[None, :]) & (slots[None, :] <= slots[:, None])
    scores = jnp.einsum('tagd,sad->agts', query_matrix, key_matrix, precision=precision) * HEAD_SIZE ** (-0.5)
    scores = low_back(scores)
    scores = jnp.where(allowed[None, None], scores, -1000000000.0)
    probs = low(jax.nn.softmax(scores, axis=-1))
    context = low_back(jnp.einsum('agts,sad->tagd', probs, value_matrix, precision=precision))
    context = low(context.reshape(span_length, QUERY_HEADS * HEAD_SIZE))
    gate_z = projected_input[:, gate_offset:offset_c]
    conv_in = projected_input[:, offset_c:offset_t]
    step_raw = projected_input[:, offset_t:]
    width = conv_in.shape[1]
    summed = jnp.zeros_like(conv_in) + kernel[KC][None, :]
    for lag in range(KC):
        shifted = jnp.concatenate([jnp.zeros((lag, width), jnp.float32), conv_in[:span_length - lag]], axis=0)
        earlier = jnp.concatenate([jnp.full((lag,), -1, jnp.int32), segment[:span_length - lag]], axis=0)
        keep = earlier == segment
        summed = summed + kernel[KC - 1 - lag][None, :] * jnp.where(keep[:, None], shifted, 0.0)
    conv_out = jax.nn.silu(summed)
    scan_x = low(conv_out[:, :MH * MP]).reshape(span_length, MH, MP)
    scan_b = low(conv_out[:, MH * MP:MH * MP + NS])
    scan_c = low(conv_out[:, MH * MP + NS:])
    step_size = jax.nn.softplus(step_raw + head_params[0][None, :])
    cumulative = jnp.cumsum(-step_size * jnp.exp(head_params[1])[None, :], axis=0)
    intersection = low_back(jnp.dot(scan_c, scan_b.T, precision=precision))
    cum_heads = cumulative.T
    spread = cum_heads[:, :, None] - cum_heads[:, None, :]
    decay_matrix = jnp.exp(jnp.where(allowed[None], spread, -10000.0))
    mixing = low(intersection[None] * decay_matrix * step_size.T[:, None, :])
    scan_out = low_back(jnp.einsum('hts,shp->thp', mixing, scan_x, precision=precision))
    scan_out = scan_out + head_params[2][None, :, None] * scan_x
    gated = scan_out.reshape(span_length, MH * MP) * jax.nn.silu(gate_z)
    mamba_out = low(normalize(gated, gain_all[2 * D:]))
    joined = jnp.concatenate([context, mamba_out], axis=1)
    hidden = block_tokens + low_back(jnp.dot(joined, w_out, precision=precision))
    normed_ff = low(normalize(hidden, gain_all[D:2 * D]))
    gate_up = low_back(jnp.dot(normed_ff, w_up, precision=precision))
    activated = low(jax.nn.silu(gate_up[:, :FF]) * gate_up[:, FF:])
    return hidden + low_back(jnp.dot(activated, w_down, precision=precision))

def adamw(weight, mean, square, grad, rate):
    mean_new = BETA_MEAN * mean + (1.0 - BETA_MEAN) * grad
    square_new = BETA_SQUARE * square + (1.0 - BETA_SQUARE) * grad * grad
    corrected = mean_new / (1.0 - BETA_MEAN ** STEP) / (jnp.sqrt(square_new / (1.0 - BETA_SQUARE ** STEP)) + ADAM_EPS)
    return (weight - rate * (corrected + DECAY * weight), mean_new, square_new)

def reference(tokens, cotangent, seq_lengths, mixer_in, mixer_in_mean, mixer_in_square, mixer_out, mixer_out_mean, mixer_out_square, swiglu_in, swiglu_in_mean, swiglu_in_square, swiglu_out, swiglu_out_mean, swiglu_out_square, gains, gains_mean, gains_square, conv_kernel, conv_kernel_mean, conv_kernel_square, head_params, head_params_mean, head_params_square):
    masters = (mixer_in, mixer_out, swiglu_in, swiglu_out, gains, conv_kernel)
    rounded = tuple((low(master) for master in masters))
    token_blocks = tokens.astype(jnp.float32).reshape(BLOCKS, CAP, D)
    cot_blocks = cotangent.astype(jnp.float32).reshape(BLOCKS, CAP, D)

    def one_block(totals, inputs):
        block_tokens, block_cot, seq_row = inputs
        segment, token_position, valid = layout(seq_row, CAP)

        def forward(values, weights, params):
            return block_forward(values, weights, params, segment, token_position, lax.Precision.HIGHEST)
        output, pull = jax.vjp(jax.checkpoint(forward), block_tokens, rounded, head_params)
        token_grad, weight_grads, param_grad = pull(block_cot * valid[:, None].astype(jnp.float32))
        summed = tuple((left + right for left, right in zip(totals[0], weight_grads)))
        return ((summed, totals[1] + param_grad), (output.astype(jnp.bfloat16), token_grad))
    start = (tuple((jnp.zeros(master.shape, jnp.float32) for master in masters)), jnp.zeros(head_params.shape, jnp.float32))
    (weight_grads, param_grad), (outputs, token_grads) = lax.scan(one_block, start, (token_blocks, cot_blocks, seq_lengths))
    rates = (MATRIX_RATE, MATRIX_RATE, MATRIX_RATE, MATRIX_RATE, VECTOR_RATE, VECTOR_RATE)
    means = (mixer_in_mean, mixer_out_mean, swiglu_in_mean, swiglu_out_mean, gains_mean, conv_kernel_mean)
    squares = (mixer_in_square, mixer_out_square, swiglu_in_square, swiglu_out_square, gains_square, conv_kernel_square)
    updated = [adamw(masters[index], means[index], squares[index], weight_grads[index], rates[index]) for index in range(6)]
    head_new = adamw(head_params, head_params_mean, head_params_square, param_grad, VECTOR_RATE)
    return (outputs.reshape(TOKENS, D), token_grads.reshape(TOKENS, D), updated[0][0], updated[0][1], updated[0][2], updated[1][0], updated[1][1], updated[1][2], updated[2][0], updated[2][1], updated[2][2], updated[3][0], updated[3][1], updated[3][2], updated[4][0], updated[4][1], updated[4][2], updated[5][0], updated[5][1], updated[5][2], head_new[0], head_new[1], head_new[2])
```

```python
import jax
import jax.numpy as jnp
from jax import lax
from jax.sharding import PartitionSpec as P

D = 1024
FF = 2048
QUERY_HEADS = 8
KEY_VALUE_HEADS = 2
HEAD_SIZE = 64
MH = 24
MP = 64
NS = 128
KC = 4
STEP = 10


NORM_EPS = 1e-05
ROPE_BASE = 100000000000.0
BETA_MEAN = 0.9
BETA_SQUARE = 0.95
ADAM_EPS = 1e-08
DECAY = 0.1
MATRIX_RATE = 0.03
VECTOR_RATE = 0.5


def make_rounders():

    def round_value(values):
        return lax.optimization_barrier(values.astype(jnp.bfloat16)).astype(jnp.float32)

    def pass_value(values):
        return values

    value_rounder = jax.custom_vjp(round_value)
    grad_rounder = jax.custom_vjp(pass_value)

    def value_keep(values):
        return (round_value(values), None)

    def value_pass(kept, grad):
        return (grad,)

    def grad_keep(values):
        return (values, None)

    def grad_round(kept, grad):
        return (round_value(grad),)

    value_rounder.defvjp(value_keep, value_pass)
    grad_rounder.defvjp(grad_keep, grad_round)
    return (value_rounder, grad_rounder)


def normalize(values, gain):
    return values * lax.rsqrt(jnp.mean(values * values, axis=-1, keepdims=True) + NORM_EPS) * gain


def layout(seq_row, span_length):
    count = seq_row.shape[0]
    ends = jnp.cumsum(seq_row)
    starts = ends - seq_row
    slots = jnp.arange(span_length, dtype=jnp.int32)
    segment = jnp.sum((slots[:, None] >= ends[None, :]).astype(jnp.int32), axis=1)
    valid = slots < ends[count - 1]
    segment = jnp.where(valid, segment, count + slots)
    match = segment[:, None] == jnp.arange(count, dtype=jnp.int32)[None, :]
    first = jnp.sum(jnp.where(match, starts[None, :], 0), axis=1)
    token_position = jnp.where(valid, slots - first, 0)
    return (segment, token_position, valid)


def apply_rotary(values, token_position):
    half = HEAD_SIZE // 2
    freq = ROPE_BASE ** (-(jnp.arange(half, dtype=jnp.float32) * 2.0 / HEAD_SIZE))
    angle = token_position.astype(jnp.float32)[:, None] * freq[None, :]
    cosine = jnp.cos(angle)[:, None, :]
    sine = jnp.sin(angle)[:, None, :]
    first_half = values[..., :half]
    second_half = values[..., half:]
    return jnp.concatenate(
        [first_half * cosine - second_half * sine, second_half * cosine + first_half * sine],
        axis=-1,
    )


def block_forward(block_tokens, weights, head_params, segment, token_position, low, low_back):
    w_in, w_out, w_up, w_down, gain_all, kernel = weights
    span_length = block_tokens.shape[0]
    normed = low(normalize(block_tokens, gain_all[:D]))
    projected_input = low_back(jnp.dot(normed, w_in, precision=None))
    key_offset = QUERY_HEADS * HEAD_SIZE
    value_offset = key_offset + KEY_VALUE_HEADS * HEAD_SIZE
    gate_offset = value_offset + KEY_VALUE_HEADS * HEAD_SIZE
    offset_c = gate_offset + MH * MP
    offset_t = offset_c + MH * MP + 2 * NS
    query_matrix = projected_input[:, :key_offset].reshape(span_length, QUERY_HEADS, HEAD_SIZE)
    key_matrix = projected_input[:, key_offset:value_offset].reshape(
        span_length, KEY_VALUE_HEADS, HEAD_SIZE
    )
    value_matrix = low(
        projected_input[:, value_offset:gate_offset].reshape(
            span_length, KEY_VALUE_HEADS, HEAD_SIZE
        )
    )
    query_matrix = low(apply_rotary(query_matrix, token_position)).reshape(
        span_length, KEY_VALUE_HEADS, QUERY_HEADS // KEY_VALUE_HEADS, HEAD_SIZE
    )
    key_matrix = low(apply_rotary(key_matrix, token_position))
    slots = jnp.arange(span_length, dtype=jnp.int32)
    allowed = (segment[:, None] == segment[None, :]) & (slots[None, :] <= slots[:, None])
    scores = jnp.einsum("tagd,sad->agts", query_matrix, key_matrix, precision=None) * HEAD_SIZE ** (
        -0.5
    )
    scores = low_back(scores)
    scores = jnp.where(allowed[None, None], scores, -1000000000.0)
    probs = low(jax.nn.softmax(scores, axis=-1))
    context = low_back(jnp.einsum("agts,sad->tagd", probs, value_matrix, precision=None))
    context = low(context.reshape(span_length, QUERY_HEADS * HEAD_SIZE))
    gate_z = projected_input[:, gate_offset:offset_c]
    conv_in = projected_input[:, offset_c:offset_t]
    step_raw = projected_input[:, offset_t:]
    width = conv_in.shape[1]
    summed = jnp.zeros_like(conv_in) + kernel[KC][None, :]
    for lag in range(KC):
        shifted = jnp.concatenate(
            [jnp.zeros((lag, width), jnp.float32), conv_in[: span_length - lag]], axis=0
        )
        earlier = jnp.concatenate(
            [jnp.full((lag,), -1, jnp.int32), segment[: span_length - lag]], axis=0
        )
        keep = earlier == segment
        summed = summed + kernel[KC - 1 - lag][None, :] * jnp.where(keep[:, None], shifted, 0.0)
    conv_out = jax.nn.silu(summed)
    scan_x = low(conv_out[:, : MH * MP]).reshape(span_length, MH, MP)
    scan_b = low(conv_out[:, MH * MP : MH * MP + NS])
    scan_c = low(conv_out[:, MH * MP + NS :])
    step_size = jax.nn.softplus(step_raw + head_params[0][None, :])
    cumulative = jnp.cumsum(-step_size * jnp.exp(head_params[1])[None, :], axis=0)
    intersection = low_back(jnp.dot(scan_c, scan_b.T, precision=None))
    cum_heads = cumulative.T
    spread = cum_heads[:, :, None] - cum_heads[:, None, :]
    decay_matrix = jnp.exp(jnp.where(allowed[None], spread, -10000.0))
    mixing = low(intersection[None] * decay_matrix * step_size.T[:, None, :])
    scan_out = low_back(jnp.einsum("hts,shp->thp", mixing, scan_x, precision=None))
    scan_out = scan_out + head_params[2][None, :, None] * scan_x
    gated = scan_out.reshape(span_length, MH * MP) * jax.nn.silu(gate_z)
    mamba_out = low(normalize(gated, gain_all[2 * D :]))
    joined = jnp.concatenate([context, mamba_out], axis=1)
    hidden = block_tokens + low_back(jnp.dot(joined, w_out, precision=None))
    normed_ff = low(normalize(hidden, gain_all[D : 2 * D]))
    gate_up = low_back(jnp.dot(normed_ff, w_up, precision=None))
    activated = low(jax.nn.silu(gate_up[:, :FF]) * gate_up[:, FF:])
    return hidden + low_back(jnp.dot(activated, w_down, precision=None))


def adamw(weight, mean, square, grad, rate):
    mean_new = BETA_MEAN * mean + (1.0 - BETA_MEAN) * grad
    square_new = BETA_SQUARE * square + (1.0 - BETA_SQUARE) * grad * grad
    corrected = (
        mean_new
        / (1.0 - BETA_MEAN**STEP)
        / (jnp.sqrt(square_new / (1.0 - BETA_SQUARE**STEP)) + ADAM_EPS)
    )
    return (weight - rate * (corrected + DECAY * weight), mean_new, square_new)


BOTH = ("shard", "rep")


def gather_matrices(masters):
    copies = lax.axis_size("rep")
    copy = lax.axis_index("rep")
    pieces = []
    for master in masters:
        rows = master.shape[0] // copies
        own = lax.dynamic_slice_in_dim(master, copy * rows, rows, 0).astype(jnp.bfloat16)
        pieces.append(lax.all_gather(own, BOTH, axis=0, tiled=True))
    return tuple(pieces)


def gather_vectors(gains, conv_kernel):
    owners = lax.axis_size("shard")
    width = conv_kernel.shape[1]
    own = jnp.concatenate([gains, conv_kernel.reshape(-1)]).astype(jnp.bfloat16)
    every = lax.all_gather(own, "shard", axis=0, tiled=False)
    gains_all = every[:, : gains.shape[0]].reshape(-1)
    taps = every[:, gains.shape[0] :].reshape(owners, KC + 1, width)
    return (gains_all, jnp.swapaxes(taps, 0, 1).reshape(KC + 1, owners * width))


def reduce_matrices(grads):
    results = []
    for grad in grads:
        piece = lax.psum_scatter(
            grad.astype(jnp.bfloat16), BOTH, scatter_dimension=0, tiled=True
        )
        results.append(lax.all_gather(piece, "rep", axis=0, tiled=True).astype(jnp.float32))
    return tuple(results)


def reduce_vectors(gains_grad, conv_grad, head_grad):
    owners = lax.axis_size("shard")
    owner = lax.axis_index("shard")
    count, taps = gains_grad.shape[0], conv_grad.size
    flat = jnp.concatenate([gains_grad, conv_grad.reshape(-1), head_grad.reshape(-1)])
    total = lax.psum(flat, ("rep", "shard"))
    own_gains = lax.dynamic_slice_in_dim(total[:count], owner * (count // owners), count // owners)
    width = conv_grad.shape[1] // owners
    own_taps = lax.dynamic_slice_in_dim(
        total[count : count + taps].reshape(conv_grad.shape), owner * width, width, 1
    )
    return ((own_gains, own_taps), total[count + taps :].reshape(head_grad.shape))


def on_device(
    tokens,
    cotangent,
    seq_lengths,
    mixer_in,
    mixer_in_mean,
    mixer_in_square,
    mixer_out,
    mixer_out_mean,
    mixer_out_square,
    swiglu_in,
    swiglu_in_mean,
    swiglu_in_square,
    swiglu_out,
    swiglu_out_mean,
    swiglu_out_square,
    gains,
    gains_mean,
    gains_square,
    conv_kernel,
    conv_kernel_mean,
    conv_kernel_square,
    head_params,
    head_params_mean,
    head_params_square,
):
    value_rounder, grad_rounder = make_rounders()
    gathered = gather_matrices((mixer_in, mixer_out, swiglu_in, swiglu_out))
    gathered = gathered + gather_vectors(gains, conv_kernel)
    weights = tuple((piece.astype(jnp.float32) for piece in gathered))
    segment, token_position, valid = layout(seq_lengths[0], tokens.shape[0])
    cot_rows = cotangent.astype(jnp.float32) * valid[:, None].astype(jnp.float32)

    def forward(values, weight_set, params):
        return block_forward(
            values, weight_set, params, segment, token_position, value_rounder, grad_rounder
        )

    output, pull = jax.vjp(forward, tokens.astype(jnp.float32), weights, head_params)
    token_grad, weight_grads, param_grad = pull(cot_rows)
    owned = reduce_matrices(weight_grads[:4])
    vector_grads, head_grad = reduce_vectors(weight_grads[4], weight_grads[5], param_grad)
    owned = owned + vector_grads
    masters = (mixer_in, mixer_out, swiglu_in, swiglu_out, gains, conv_kernel)
    means = (
        mixer_in_mean,
        mixer_out_mean,
        swiglu_in_mean,
        swiglu_out_mean,
        gains_mean,
        conv_kernel_mean,
    )
    squares = (
        mixer_in_square,
        mixer_out_square,
        swiglu_in_square,
        swiglu_out_square,
        gains_square,
        conv_kernel_square,
    )
    rates = (MATRIX_RATE, MATRIX_RATE, MATRIX_RATE, MATRIX_RATE, VECTOR_RATE, VECTOR_RATE)
    updated = [
        adamw(masters[index], means[index], squares[index], owned[index], rates[index])
        for index in range(6)
    ]
    head_new = adamw(head_params, head_params_mean, head_params_square, head_grad, VECTOR_RATE)
    return (
        output.astype(jnp.bfloat16),
        token_grad,
        updated[0][0],
        updated[0][1],
        updated[0][2],
        updated[1][0],
        updated[1][1],
        updated[1][2],
        updated[2][0],
        updated[2][1],
        updated[2][2],
        updated[3][0],
        updated[3][1],
        updated[3][2],
        updated[4][0],
        updated[4][1],
        updated[4][2],
        updated[5][0],
        updated[5][1],
        updated[5][2],
        head_new[0],
        head_new[1],
        head_new[2],
    )


def solution(mesh):
    return jax.shard_map(
        on_device,
        mesh=mesh,
        in_specs=(
            P(("rep", "shard"), None),
            P(("rep", "shard"), None),
            P(("rep", "shard"), None),
            P("shard", None),
            P("shard", None),
            P("shard", None),
            P("shard", None),
            P("shard", None),
            P("shard", None),
            P("shard", None),
            P("shard", None),
            P("shard", None),
            P("shard", None),
            P("shard", None),
            P("shard", None),
            P("shard"),
            P("shard"),
            P("shard"),
            P(None, "shard"),
            P(None, "shard"),
            P(None, "shard"),
            P(),
            P(),
            P(),
        ),
        out_specs=(
            P(("rep", "shard"), None),
            P(("rep", "shard"), None),
            P("shard", None),
            P("shard", None),
            P("shard", None),
            P("shard", None),
            P("shard", None),
            P("shard", None),
            P("shard", None),
            P("shard", None),
            P("shard", None),
            P("shard", None),
            P("shard", None),
            P("shard", None),
            P("shard"),
            P("shard"),
            P("shard"),
            P(None, "shard"),
            P(None, "shard"),
            P(None, "shard"),
            P(),
            P(),
            P(),
        ),
        check_vma=False,
    )
```

```python
import jax
import jax.numpy as jnp
from jax import lax
from jax.experimental import pallas as pl
from jax.experimental.pallas import tpu as pltpu
from jax.sharding import PartitionSpec as P

D = 1024
FF = 2048
QUERY_HEADS = 8
KEY_VALUE_HEADS = 2
HEAD_SIZE = 64
MH = 24
MP = 64
NS = 128
KC = 4
STEP = 10


NORM_EPS = 1e-05
ROPE_BASE = 100000000000.0
BETA_MEAN = 0.9
BETA_SQUARE = 0.95
ADAM_EPS = 1e-08
DECAY = 0.1
MATRIX_RATE = 0.03
VECTOR_RATE = 0.5


def make_rounders():

    def round_value(values):
        return lax.optimization_barrier(values.astype(jnp.bfloat16)).astype(jnp.float32)

    def pass_value(values):
        return values

    value_rounder = jax.custom_vjp(round_value)
    grad_rounder = jax.custom_vjp(pass_value)

    def value_keep(values):
        return (round_value(values), None)

    def value_pass(kept, grad):
        return (grad,)

    def grad_keep(values):
        return (values, None)

    def grad_round(kept, grad):
        return (round_value(grad),)

    value_rounder.defvjp(value_keep, value_pass)
    grad_rounder.defvjp(grad_keep, grad_round)
    return (value_rounder, grad_rounder)


def normalize(values, gain):
    return values * lax.rsqrt(jnp.mean(values * values, axis=-1, keepdims=True) + NORM_EPS) * gain


def layout(seq_row, span_length):
    count = seq_row.shape[0]
    ends = jnp.cumsum(seq_row)
    starts = ends - seq_row
    slots = jnp.arange(span_length, dtype=jnp.int32)
    segment = jnp.sum((slots[:, None] >= ends[None, :]).astype(jnp.int32), axis=1)
    valid = slots < ends[count - 1]
    segment = jnp.where(valid, segment, count + slots)
    match = segment[:, None] == jnp.arange(count, dtype=jnp.int32)[None, :]
    first = jnp.sum(jnp.where(match, starts[None, :], 0), axis=1)
    token_position = jnp.where(valid, slots - first, 0)
    return (segment, token_position, valid)


def apply_rotary(values, token_position):
    half = HEAD_SIZE // 2
    freq = ROPE_BASE ** (-(jnp.arange(half, dtype=jnp.float32) * 2.0 / HEAD_SIZE))
    angle = token_position.astype(jnp.float32)[:, None] * freq[None, :]
    cosine = jnp.cos(angle)[:, None, :]
    sine = jnp.sin(angle)[:, None, :]
    first_half = values[..., :half]
    second_half = values[..., half:]
    return jnp.concatenate(
        [first_half * cosine - second_half * sine, second_half * cosine + first_half * sine],
        axis=-1,
    )


def block_forward(block_tokens, weights, head_params, segment, token_position, low, low_back):
    w_conv, w_qkv, w_gate, w_out, w_up, w_down, gain_all, kernel = weights
    span_length = block_tokens.shape[0]
    normed = low(normalize(block_tokens, gain_all[:D]))
    projected_qkv = low_back(jnp.dot(normed, w_qkv, precision=None))
    projected_conv = low_back(jnp.dot(normed, w_conv, precision=None))
    key_offset = QUERY_HEADS * HEAD_SIZE
    value_offset = key_offset + KEY_VALUE_HEADS * HEAD_SIZE
    conv_width = MH * MP + 2 * NS
    query_matrix = projected_qkv[:, :key_offset].reshape(span_length, QUERY_HEADS, HEAD_SIZE)
    key_matrix = projected_qkv[:, key_offset:value_offset].reshape(
        span_length, KEY_VALUE_HEADS, HEAD_SIZE
    )
    value_matrix = low(
        projected_qkv[:, value_offset:].reshape(
            span_length, KEY_VALUE_HEADS, HEAD_SIZE
        )
    )
    query_matrix = low(apply_rotary(query_matrix, token_position)).reshape(
        span_length, KEY_VALUE_HEADS, QUERY_HEADS // KEY_VALUE_HEADS, HEAD_SIZE
    )
    key_matrix = low(apply_rotary(key_matrix, token_position))
    slots = jnp.arange(span_length, dtype=jnp.int32)
    allowed = (segment[:, None] == segment[None, :]) & (slots[None, :] <= slots[:, None])
    scores = jnp.einsum("tagd,sad->agts", query_matrix, key_matrix, precision=None) * HEAD_SIZE ** (
        -0.5
    )
    scores = low_back(scores)
    scores = jnp.where(allowed[None, None], scores, -1000000000.0)
    probs = low(jax.nn.softmax(scores, axis=-1))
    context = low_back(jnp.einsum("agts,sad->tagd", probs, value_matrix, precision=None))
    context = low(context.reshape(span_length, QUERY_HEADS * HEAD_SIZE))
    gate_z = low_back(jnp.dot(normed, w_gate, precision=None))
    conv_in = projected_conv[:, :conv_width]
    step_raw = projected_conv[:, conv_width : conv_width + MH]
    width = conv_in.shape[1]
    summed = jnp.zeros_like(conv_in) + kernel[KC][None, :]
    for lag in range(KC):
        shifted = jnp.concatenate(
            [jnp.zeros((lag, width), jnp.float32), conv_in[: span_length - lag]], axis=0
        )
        earlier = jnp.concatenate(
            [jnp.full((lag,), -1, jnp.int32), segment[: span_length - lag]], axis=0
        )
        keep = earlier == segment
        summed = summed + kernel[KC - 1 - lag][None, :] * jnp.where(keep[:, None], shifted, 0.0)
    conv_out = jax.nn.silu(summed)
    scan_x = low(conv_out[:, : MH * MP]).reshape(span_length, MH, MP)
    scan_b = low(conv_out[:, MH * MP : MH * MP + NS])
    scan_c = low(conv_out[:, MH * MP + NS :])
    step_size = jax.nn.softplus(step_raw + head_params[0][None, :])
    cumulative = jnp.cumsum(-step_size * jnp.exp(head_params[1])[None, :], axis=0)
    intersection = low_back(jnp.dot(scan_c, scan_b.T, precision=None))
    cum_heads = cumulative.T
    spread = cum_heads[:, :, None] - cum_heads[:, None, :]
    decay_matrix = jnp.exp(jnp.where(allowed[None], spread, -10000.0))
    mixing = low(intersection[None] * decay_matrix * step_size.T[:, None, :])
    scan_out = low_back(jnp.einsum("hts,shp->thp", mixing, scan_x, precision=None))
    scan_out = scan_out + head_params[2][None, :, None] * scan_x
    gated = scan_out.reshape(span_length, MH * MP) * jax.nn.silu(gate_z)
    mamba_out = low(normalize(gated, gain_all[2 * D :]))
    joined = jnp.concatenate([context, mamba_out], axis=1)
    hidden = block_tokens + low_back(jnp.dot(joined, w_out, precision=None))
    normed_ff = low(normalize(hidden, gain_all[D : 2 * D]))
    gate_up = low_back(jnp.dot(normed_ff, w_up, precision=None))
    activated = low(jax.nn.silu(gate_up[:, :FF]) * gate_up[:, FF:])
    return hidden + low_back(jnp.dot(activated, w_down, precision=None))


def adamw(weight, mean, square, grad, rate):
    mean_new = BETA_MEAN * mean + (1.0 - BETA_MEAN) * grad
    square_new = BETA_SQUARE * square + (1.0 - BETA_SQUARE) * grad * grad
    corrected = (
        mean_new
        / (1.0 - BETA_MEAN**STEP)
        / (jnp.sqrt(square_new / (1.0 - BETA_SQUARE**STEP)) + ADAM_EPS)
    )
    return (weight - rate * (corrected + DECAY * weight), mean_new, square_new)


QKV = (QUERY_HEADS + 2 * KEY_VALUE_HEADS) * HEAD_SIZE
GATE = MH * MP
CONV = MH * MP + 2 * NS
STEP_LANES = 128
BOTH = ("shard", "rep")
ALL = ("rep", "shard")


def general_gather(own):
    copies = lax.axis_size("rep")
    rows = own.shape[0] // copies
    part = lax.dynamic_slice_in_dim(own, lax.axis_index("rep") * rows, rows, 0)
    return lax.all_gather(part, BOTH, axis=0, tiled=True)


def general_reduce(grad):
    piece = lax.psum_scatter(grad, BOTH, scatter_dimension=0, tiled=True)
    return lax.all_gather(piece, "rep", axis=0, tiled=True)


def place():
    rep, shard = lax.axis_index("rep"), lax.axis_index("shard")
    return (rep // 2, rep % 2, shard // 2, shard % 2)


def send(values, dx=0, dcore=0, dz=0, dy=0):
    pairs = []
    for x in range(2):
        for core in range(2):
            for z in range(4):
                for y in range(2):
                    start = (x * 2 + core) * 8 + z * 2 + y
                    end = ((x ^ dx) * 2 + (core ^ dcore)) * 8 + ((z + dz) % 4) * 2 + (y ^ dy)
                    pairs.append((start, end))
    return lax.ppermute(values, ALL, pairs)


def pick(values, index, axis):
    return lax.dynamic_index_in_dim(values, index, axis, keepdims=False)


def assemble(held, rows):
    quarter = rows // 8
    columns = held[0].shape[-1]

    def kernel(*refs):
        sources, target, sems = refs[:8], refs[8], refs[9]
        rep, shard = lax.axis_index("rep"), lax.axis_index("shard")
        x, core, z, y = rep // 2, rep % 2, shard // 2, shard % 2
        copies = []
        for other_core in range(2):
            half = core if other_core == 0 else 1 - core
            for other_y in range(2):
                row = y if other_y == 0 else 1 - y
                for turn in range(4):
                    owner = ((z + 4 - turn) % 4) * 2 + row
                    base = owner * rows + half * (rows // 2)
                    main = sources[other_core * 4 + other_y].at[turn]
                    cross = sources[other_core * 4 + 2 + other_y].at[turn]
                    for piece, start, count in (
                        (main.at[pl.ds(0, quarter)], base + x * quarter, quarter),
                        (main.at[pl.ds(quarter, 2 * quarter)], base + 2 * quarter, 2 * quarter),
                        (cross, base + (1 - x) * quarter, quarter),
                    ):
                        place_at = pl.ds(pl.multiple_of(start, 16), count)
                        copies.append(
                            pltpu.make_async_copy(piece, target.at[place_at], sems.at[len(copies)])
                        )
        for copy in copies:
            copy.start()
        for copy in copies:
            copy.wait()

    return pl.pallas_call(
        kernel,
        out_shape=jax.ShapeDtypeStruct((8 * rows, columns), jnp.bfloat16),
        in_specs=[pl.BlockSpec(memory_space=pl.ANY)] * 8,
        out_specs=pl.BlockSpec(memory_space=pl.ANY),
        scratch_shapes=[pltpu.SemaphoreType.DMA((48,))],
        name="assemble",
    )(*held)


def tuned_gather(own):
    rows = own.shape[0]
    quarter = rows // 8
    x, core, z, y = place()
    half = lax.dynamic_slice_in_dim(own, core * (rows // 2), rows // 2, 0)
    mine = jnp.concatenate(
        [lax.dynamic_slice_in_dim(half, x * quarter, quarter, 0), half[2 * quarter :]], axis=0
    )
    along_z = jnp.stack([mine] + [send(mine, dz=turn) for turn in range(1, 4)])
    across_y = send(along_z, dy=1)
    held = [along_z, across_y]
    held += [send(group[:, :quarter], dx=1) for group in held]
    held += [send(group, dcore=1) for group in held]
    return assemble(held, rows)


def add_low(left, right):
    return (left.astype(jnp.float32) + right.astype(jnp.float32)).astype(jnp.bfloat16)


def tuned_reduce(grad):
    rows, columns = grad.shape[0] // 8, grad.shape[1]
    quarter = rows // 8
    x, core, z, y = place()
    parts = grad.reshape(4, 2, 2, rows // 2, columns)
    half = add_low(pick(parts, core, 2), send(pick(parts, 1 - core, 2), dcore=1))
    far = lax.dynamic_slice_in_dim(half, (1 - x) * quarter, quarter, 2)
    near = add_low(lax.dynamic_slice_in_dim(half, x * quarter, quarter, 2), send(far, dx=1))
    both = half[:, :, 2 * quarter :]
    there = jnp.concatenate([pick(near, 1 - y, 1), pick(both, 1 - y, 1)], axis=1)
    here = jnp.concatenate([pick(near, y, 1), pick(both, y, 1)], axis=1)
    column = add_low(here, send(there, dy=1))
    total = pick(column, z, 0).astype(jnp.float32)
    for turn in range(1, 4):
        total = total + send(pick(column, (z + turn) % 4, 0), dz=turn).astype(jnp.float32)
    total = total.astype(jnp.bfloat16)
    across = send(total, dx=1)
    own_x, other_x = total[:quarter], across[:quarter]
    owned = jnp.concatenate(
        [
            jnp.where(x == 0, own_x, other_x),
            jnp.where(x == 0, other_x, own_x),
            add_low(total[quarter:], across[quarter:]),
        ],
        axis=0,
    )
    beside = send(owned, dcore=1)
    return jnp.concatenate(
        [jnp.where(core == 0, owned, beside), jnp.where(core == 0, beside, owned)], axis=0
    )


def tuned():
    return lax.axis_size("rep") == 4 and lax.axis_size("shard") == 8


def gather_weights(mixer_in, mixer_out, swiglu_in, swiglu_out, gains, conv_kernel):
    gather = tuned_gather if tuned() else general_gather
    rows = mixer_in.shape[0]
    owners = lax.axis_size("shard")
    width = conv_kernel.shape[1]
    count = gains.shape[0] + conv_kernel.size
    lanes = -(-count // rows)
    vector = jnp.concatenate([gains, conv_kernel.reshape(-1)])
    vector = jnp.pad(vector, (0, lanes * rows - count)).reshape(rows, lanes)
    low_in = mixer_in.astype(jnp.bfloat16)
    tail = STEP_LANES - MH - lanes
    conv_piece = jnp.concatenate(
        [low_in[:, QKV + GATE :], vector.astype(jnp.bfloat16), jnp.zeros((rows, tail), jnp.bfloat16)],
        axis=1,
    )
    w_conv = gather(conv_piece)
    w_qkv = gather(low_in[:, :QKV])
    w_gate = gather(low_in[:, QKV : QKV + GATE])
    w_out = gather(mixer_out.astype(jnp.bfloat16))
    w_up = gather(swiglu_in.astype(jnp.bfloat16))
    w_down = gather(swiglu_out.astype(jnp.bfloat16))
    every = w_conv[:, CONV + MH : CONV + MH + lanes].reshape(owners, rows * lanes)
    gains_all = every[:, : gains.shape[0]].reshape(-1)
    taps = every[:, gains.shape[0] : count].reshape(owners, KC + 1, width)
    taps = jnp.swapaxes(taps, 0, 1).reshape(KC + 1, owners * width)
    return (w_conv, w_qkv, w_gate, w_out, w_up, w_down, gains_all, taps)


def reduce_grads(grads, head_grad):
    reduce = tuned_reduce if tuned() else general_reduce
    owners = lax.axis_size("shard")
    conv_g, qkv_g, gate_g, out_g, up_g, down_g, gains_g, taps_g = grads
    down = reduce(down_g.astype(jnp.bfloat16))
    up = reduce(up_g.astype(jnp.bfloat16))
    out = reduce(out_g.astype(jnp.bfloat16))
    gate = reduce(gate_g.astype(jnp.bfloat16))
    qkv = reduce(qkv_g.astype(jnp.bfloat16))
    rows = conv_g.shape[0] // owners
    width = taps_g.shape[1] // owners
    vector = jnp.concatenate(
        [
            gains_g.reshape(owners, -1),
            jnp.swapaxes(taps_g.reshape(KC + 1, owners, width), 0, 1).reshape(owners, -1),
            jnp.broadcast_to(head_grad.reshape(1, -1), (owners, head_grad.size)),
        ],
        axis=1,
    )
    count = vector.shape[1]
    lanes = -(-count // rows)
    vector = jnp.pad(vector, ((0, 0), (0, lanes * rows - count))).reshape(owners * rows, lanes)
    used = CONV + MH
    conv_g = jnp.concatenate(
        [conv_g[:, :used], vector, jnp.zeros((owners * rows, STEP_LANES - MH - lanes), jnp.float32)],
        axis=1,
    )
    conv = reduce(conv_g.astype(jnp.bfloat16))
    flat = conv[:, used : used + lanes].astype(jnp.float32).reshape(-1)
    own_gains = gains_g.shape[0] // owners
    own_taps = (KC + 1) * width
    matrix = jnp.concatenate([qkv, gate, conv[:, :used]], axis=1)
    return (
        (
            matrix.astype(jnp.float32),
            out.astype(jnp.float32),
            up.astype(jnp.float32),
            down.astype(jnp.float32),
            flat[:own_gains],
            flat[own_gains : own_gains + own_taps].reshape(KC + 1, width),
        ),
        flat[own_gains + own_taps : count].reshape(head_grad.shape),
    )


def on_device(
    tokens,
    cotangent,
    seq_lengths,
    mixer_in,
    mixer_in_mean,
    mixer_in_square,
    mixer_out,
    mixer_out_mean,
    mixer_out_square,
    swiglu_in,
    swiglu_in_mean,
    swiglu_in_square,
    swiglu_out,
    swiglu_out_mean,
    swiglu_out_square,
    gains,
    gains_mean,
    gains_square,
    conv_kernel,
    conv_kernel_mean,
    conv_kernel_square,
    head_params,
    head_params_mean,
    head_params_square,
):
    value_rounder, grad_rounder = make_rounders()
    gathered = gather_weights(mixer_in, mixer_out, swiglu_in, swiglu_out, gains, conv_kernel)
    weights = tuple((piece.astype(jnp.float32) for piece in gathered))
    segment, token_position, valid = layout(seq_lengths[0], tokens.shape[0])
    cot_rows = cotangent.astype(jnp.float32) * valid[:, None].astype(jnp.float32)

    def forward(values, weight_set, params):
        return block_forward(
            values, weight_set, params, segment, token_position, value_rounder, grad_rounder
        )

    output, pull = jax.vjp(forward, tokens.astype(jnp.float32), weights, head_params)
    token_grad, weight_grads, param_grad = pull(cot_rows)
    owned, head_grad = reduce_grads(weight_grads, param_grad)
    masters = (mixer_in, mixer_out, swiglu_in, swiglu_out, gains, conv_kernel)
    means = (
        mixer_in_mean,
        mixer_out_mean,
        swiglu_in_mean,
        swiglu_out_mean,
        gains_mean,
        conv_kernel_mean,
    )
    squares = (
        mixer_in_square,
        mixer_out_square,
        swiglu_in_square,
        swiglu_out_square,
        gains_square,
        conv_kernel_square,
    )
    rates = (MATRIX_RATE, MATRIX_RATE, MATRIX_RATE, MATRIX_RATE, VECTOR_RATE, VECTOR_RATE)
    updated = [
        adamw(masters[index], means[index], squares[index], owned[index], rates[index])
        for index in range(6)
    ]
    head_new = adamw(head_params, head_params_mean, head_params_square, head_grad, VECTOR_RATE)
    return (
        output.astype(jnp.bfloat16),
        token_grad,
        updated[0][0],
        updated[0][1],
        updated[0][2],
        updated[1][0],
        updated[1][1],
        updated[1][2],
        updated[2][0],
        updated[2][1],
        updated[2][2],
        updated[3][0],
        updated[3][1],
        updated[3][2],
        updated[4][0],
        updated[4][1],
        updated[4][2],
        updated[5][0],
        updated[5][1],
        updated[5][2],
        head_new[0],
        head_new[1],
        head_new[2],
    )


def solution(mesh):
    return jax.shard_map(
        on_device,
        mesh=mesh,
        in_specs=(
            P(("rep", "shard"), None),
            P(("rep", "shard"), None),
            P(("rep", "shard"), None),
            P("shard", None),
            P("shard", None),
            P("shard", None),
            P("shard", None),
            P("shard", None),
            P("shard", None),
            P("shard", None),
            P("shard", None),
            P("shard", None),
            P("shard", None),
            P("shard", None),
            P("shard", None),
            P("shard"),
            P("shard"),
            P("shard"),
            P(None, "shard"),
            P(None, "shard"),
            P(None, "shard"),
            P(),
            P(),
            P(),
        ),
        out_specs=(
            P(("rep", "shard"), None),
            P(("rep", "shard"), None),
            P("shard", None),
            P("shard", None),
            P("shard", None),
            P("shard", None),
            P("shard", None),
            P("shard", None),
            P("shard", None),
            P("shard", None),
            P("shard", None),
            P("shard", None),
            P("shard", None),
            P("shard", None),
            P("shard"),
            P("shard"),
            P("shard"),
            P(None, "shard"),
            P(None, "shard"),
            P(None, "shard"),
            P(),
            P(),
            P(),
        ),
        check_vma=False,
    )
```

```python
import jax
import jax.numpy as jnp
from jax import lax
from jax.experimental import pallas as pl
from jax.experimental.pallas import tpu as pltpu
from jax.sharding import PartitionSpec as P

D = 1024
FF = 2048
QUERY_HEADS = 8
KEY_VALUE_HEADS = 2
HEAD_SIZE = 64
MH = 24
MP = 64
NS = 128
KC = 4
STEP = 10


NORM_EPS = 1e-05
ROPE_BASE = 100000000000.0
BETA_MEAN = 0.9
BETA_SQUARE = 0.95
ADAM_EPS = 1e-08
DECAY = 0.1
MATRIX_RATE = 0.03
VECTOR_RATE = 0.5


def make_rounders():

    def round_value(values):
        return lax.optimization_barrier(values.astype(jnp.bfloat16)).astype(jnp.float32)

    def pass_value(values):
        return values

    value_rounder = jax.custom_vjp(round_value)
    grad_rounder = jax.custom_vjp(pass_value)

    def value_keep(values):
        return (round_value(values), None)

    def value_pass(kept, grad):
        return (grad,)

    def grad_keep(values):
        return (values, None)

    def grad_round(kept, grad):
        return (round_value(grad),)

    value_rounder.defvjp(value_keep, value_pass)
    grad_rounder.defvjp(grad_keep, grad_round)
    return (value_rounder, grad_rounder)


def normalize(values, gain):
    return values * lax.rsqrt(jnp.mean(values * values, axis=-1, keepdims=True) + NORM_EPS) * gain


def layout(seq_row, span_length):
    count = seq_row.shape[0]
    ends = jnp.cumsum(seq_row)
    starts = ends - seq_row
    slots = jnp.arange(span_length, dtype=jnp.int32)
    segment = jnp.sum((slots[:, None] >= ends[None, :]).astype(jnp.int32), axis=1)
    valid = slots < ends[count - 1]
    segment = jnp.where(valid, segment, count + slots)
    match = segment[:, None] == jnp.arange(count, dtype=jnp.int32)[None, :]
    first = jnp.sum(jnp.where(match, starts[None, :], 0), axis=1)
    token_position = jnp.where(valid, slots - first, 0)
    return (segment, token_position, valid)


def apply_rotary(values, token_position):
    half = HEAD_SIZE // 2
    freq = ROPE_BASE ** (-(jnp.arange(half, dtype=jnp.float32) * 2.0 / HEAD_SIZE))
    angle = token_position.astype(jnp.float32)[:, None] * freq[None, :]
    cosine = jnp.cos(angle)[:, None, :]
    sine = jnp.sin(angle)[:, None, :]
    first_half = values[..., :half]
    second_half = values[..., half:]
    return jnp.concatenate(
        [first_half * cosine - second_half * sine, second_half * cosine + first_half * sine],
        axis=-1,
    )


def rows_of(matrix):
    return matrix.astype(jnp.bfloat16)


def dot(left, right):
    return jnp.dot(left, right, preferred_element_type=jnp.float32)


def dot_left(left, right):
    return lax.dot_general(left, right, (((0,), (0,)), ((), ())), preferred_element_type=jnp.float32)


def dot_right(left, right):
    return lax.dot_general(left, right, (((1,), (1,)), ((), ())), preferred_element_type=jnp.float32)


def attention(projected, segment, token_position, low, low_back):
    span_length = projected.shape[0]
    key_offset = QUERY_HEADS * HEAD_SIZE
    value_offset = key_offset + KEY_VALUE_HEADS * HEAD_SIZE
    query_matrix = projected[:, :key_offset].reshape(span_length, QUERY_HEADS, HEAD_SIZE)
    key_matrix = projected[:, key_offset:value_offset].reshape(
        span_length, KEY_VALUE_HEADS, HEAD_SIZE
    )
    value_matrix = low(
        projected[:, value_offset:].reshape(span_length, KEY_VALUE_HEADS, HEAD_SIZE)
    )
    query_matrix = low(apply_rotary(query_matrix, token_position)).reshape(
        span_length, KEY_VALUE_HEADS, QUERY_HEADS // KEY_VALUE_HEADS, HEAD_SIZE
    )
    key_matrix = low(apply_rotary(key_matrix, token_position))
    slots = jnp.arange(span_length, dtype=jnp.int32)
    allowed = (segment[:, None] == segment[None, :]) & (slots[None, :] <= slots[:, None])
    scores = jnp.einsum("tagd,sad->agts", query_matrix, key_matrix, precision=None) * HEAD_SIZE ** (
        -0.5
    )
    scores = low_back(scores)
    scores = jnp.where(allowed[None, None], scores, -1000000000.0)
    probs = low(jax.nn.softmax(scores, axis=-1))
    context = low_back(jnp.einsum("agts,sad->tagd", probs, value_matrix, precision=None))
    return low(context.reshape(span_length, QUERY_HEADS * HEAD_SIZE))


def state_space(projected, kernel, head_params, segment, low, low_back):
    span_length = projected.shape[0]
    conv_in = projected[:, :CONV]
    step_raw = projected[:, CONV : CONV + MH]
    slots = jnp.arange(span_length, dtype=jnp.int32)
    allowed = (segment[:, None] == segment[None, :]) & (slots[None, :] <= slots[:, None])
    summed = jnp.zeros_like(conv_in) + kernel[KC][None, :]
    for lag in range(KC):
        shifted = jnp.concatenate(
            [jnp.zeros((lag, CONV), jnp.float32), conv_in[: span_length - lag]], axis=0
        )
        earlier = jnp.concatenate(
            [jnp.full((lag,), -1, jnp.int32), segment[: span_length - lag]], axis=0
        )
        keep = earlier == segment
        summed = summed + kernel[KC - 1 - lag][None, :] * jnp.where(keep[:, None], shifted, 0.0)
    conv_out = jax.nn.silu(summed)
    scan_x = low(conv_out[:, : MH * MP]).reshape(span_length, MH, MP)
    scan_b = low(conv_out[:, MH * MP : MH * MP + NS])
    scan_c = low(conv_out[:, MH * MP + NS :])
    step_size = jax.nn.softplus(step_raw + head_params[0][None, :])
    cumulative = jnp.cumsum(-step_size * jnp.exp(head_params[1])[None, :], axis=0)
    intersection = low_back(jnp.dot(scan_c, scan_b.T, precision=None))
    cum_heads = cumulative.T
    spread = cum_heads[:, :, None] - cum_heads[:, None, :]
    decay_matrix = jnp.exp(jnp.where(allowed[None], spread, -10000.0))
    mixing = low(intersection[None] * decay_matrix * step_size.T[:, None, :])
    scan_out = low_back(jnp.einsum("hts,shp->thp", mixing, scan_x, precision=None))
    scan_out = scan_out + head_params[2][None, :, None] * scan_x
    return scan_out.reshape(span_length, MH * MP)


def gating(scan_out, gate_z, gain, low):
    return low(normalize(scan_out * jax.nn.silu(gate_z), gain))


def activation(gate_up, low):
    return low(jax.nn.silu(gate_up[:, :FF]) * gate_up[:, FF:])


def adamw(weight, mean, square, grad, rate):
    mean_new = BETA_MEAN * mean + (1.0 - BETA_MEAN) * grad
    square_new = BETA_SQUARE * square + (1.0 - BETA_SQUARE) * grad * grad
    corrected = (
        mean_new
        / (1.0 - BETA_MEAN**STEP)
        / (jnp.sqrt(square_new / (1.0 - BETA_SQUARE**STEP)) + ADAM_EPS)
    )
    return (weight - rate * (corrected + DECAY * weight), mean_new, square_new)


QKV = (QUERY_HEADS + 2 * KEY_VALUE_HEADS) * HEAD_SIZE
GATE = MH * MP
CONV = MH * MP + 2 * NS
STEP_LANES = 128
BOTH = ("shard", "rep")
ALL = ("rep", "shard")


def general_gather(own):
    copies = lax.axis_size("rep")
    rows = own.shape[0] // copies
    part = lax.dynamic_slice_in_dim(own, lax.axis_index("rep") * rows, rows, 0)
    return lax.all_gather(part, BOTH, axis=0, tiled=True)


def general_reduce(grad):
    piece = lax.psum_scatter(grad, BOTH, scatter_dimension=0, tiled=True)
    return lax.all_gather(piece, "rep", axis=0, tiled=True)


def place():
    rep, shard = lax.axis_index("rep"), lax.axis_index("shard")
    return (rep // 2, rep % 2, shard // 2, shard % 2)


def send(values, dx=0, dcore=0, dz=0, dy=0):
    pairs = []
    for x in range(2):
        for core in range(2):
            for z in range(4):
                for y in range(2):
                    start = (x * 2 + core) * 8 + z * 2 + y
                    end = ((x ^ dx) * 2 + (core ^ dcore)) * 8 + ((z + dz) % 4) * 2 + (y ^ dy)
                    pairs.append((start, end))
    return lax.ppermute(values, ALL, pairs)


def pick(values, index, axis):
    return lax.dynamic_index_in_dim(values, index, axis, keepdims=False)


def fence(values, after):
    def kernel(*refs):
        del refs

    return pl.pallas_call(
        kernel,
        out_shape=[jax.ShapeDtypeStruct(value.shape, value.dtype) for value in values],
        in_specs=[pl.BlockSpec(memory_space=pl.ANY)] * (len(values) + len(after)),
        out_specs=[pl.BlockSpec(memory_space=pl.ANY)] * len(values),
        input_output_aliases={index: index for index in range(len(values))},
        name="fence",
    )(*values, *after)


def assemble(held, rows):
    quarter = rows // 8
    columns = held[0].shape[-1]

    def kernel(*refs):
        sources, target, sems = refs[:8], refs[8], refs[9]
        rep, shard = lax.axis_index("rep"), lax.axis_index("shard")
        x, core, z, y = rep // 2, rep % 2, shard // 2, shard % 2
        copies = []
        for other_core in range(2):
            half = core if other_core == 0 else 1 - core
            for other_y in range(2):
                row = y if other_y == 0 else 1 - y
                for turn in range(4):
                    owner = ((z + 4 - turn) % 4) * 2 + row
                    base = owner * rows + half * (rows // 2)
                    main = sources[other_core * 4 + other_y].at[turn]
                    cross = sources[other_core * 4 + 2 + other_y].at[turn]
                    for piece, start, count in (
                        (main.at[pl.ds(0, quarter)], base + x * quarter, quarter),
                        (main.at[pl.ds(quarter, 2 * quarter)], base + 2 * quarter, 2 * quarter),
                        (cross, base + (1 - x) * quarter, quarter),
                    ):
                        place_at = pl.ds(pl.multiple_of(start, 16), count)
                        copies.append(
                            pltpu.make_async_copy(piece, target.at[place_at], sems.at[len(copies)])
                        )
        for copy in copies:
            copy.start()
        for copy in copies:
            copy.wait()

    return pl.pallas_call(
        kernel,
        out_shape=jax.ShapeDtypeStruct((8 * rows, columns), jnp.bfloat16),
        in_specs=[pl.BlockSpec(memory_space=pl.ANY)] * 8,
        out_specs=pl.BlockSpec(memory_space=pltpu.VMEM),
        scratch_shapes=[pltpu.SemaphoreType.DMA((48,))],
        compiler_params=pltpu.CompilerParams(vmem_limit_bytes=24 * 1024 * 1024),
        name="assemble",
    )(*held)


def tuned_gather(pieces):
    x, core, z, y = place()
    results, after = [], None
    for own in pieces:
        rows = own.shape[0]
        quarter = rows // 8
        half = lax.dynamic_slice_in_dim(own, core * (rows // 2), rows // 2, 0)
        mine = jnp.concatenate(
            [lax.dynamic_slice_in_dim(half, x * quarter, quarter, 0), half[2 * quarter :]], axis=0
        )
        if after is not None:
            mine = fence([mine], after)[0]
        after = [send(mine, dz=turn) for turn in range(1, 4)]
        along_z = jnp.stack([mine] + after)
        across_y = send(along_z, dy=1)
        held = [along_z, across_y]
        held += [send(group[:, :quarter], dx=1) for group in held]
        held += [send(group, dcore=1) for group in held]
        results.append(assemble(held, rows))
    return results


def add_low(left, right):
    return (left.astype(jnp.float32) + right.astype(jnp.float32)).astype(jnp.bfloat16)


def tuned_reduce(grad):
    rows, columns = grad.shape[0] // 8, grad.shape[1]
    quarter = rows // 8
    x, core, z, y = place()
    parts = grad.reshape(4, 2, 2, rows // 2, columns)
    far = pick(parts, 1 - core, 2)
    yield [far]
    half = add_low(pick(parts, core, 2), send(far, dcore=1))
    far = lax.dynamic_slice_in_dim(half, (1 - x) * quarter, quarter, 2)
    yield [far]
    near = add_low(lax.dynamic_slice_in_dim(half, x * quarter, quarter, 2), send(far, dx=1))
    both = half[:, :, 2 * quarter :]
    there = jnp.concatenate([pick(near, 1 - y, 1), pick(both, 1 - y, 1)], axis=1)
    here = jnp.concatenate([pick(near, y, 1), pick(both, y, 1)], axis=1)
    yield [there]
    column = add_low(here, send(there, dy=1))
    turns = [pick(column, (z + turn) % 4, 0) for turn in range(1, 4)]
    yield turns
    total = pick(column, z, 0).astype(jnp.float32)
    for turn in range(1, 4):
        total = total + send(turns[turn - 1], dz=turn).astype(jnp.float32)
    total = total.astype(jnp.bfloat16)
    yield [total]
    across = send(total, dx=1)
    own_x, other_x = total[:quarter], across[:quarter]
    owned = jnp.concatenate(
        [
            jnp.where(x == 0, own_x, other_x),
            jnp.where(x == 0, other_x, own_x),
            add_low(total[quarter:], across[quarter:]),
        ],
        axis=0,
    )
    yield [owned]
    beside = send(owned, dcore=1)
    return jnp.concatenate(
        [jnp.where(core == 0, owned, beside), jnp.where(core == 0, beside, owned)], axis=0
    )


def general_stages(grad):
    yield []
    return general_reduce(grad)


class Reductions:

    def __init__(self):
        self.tuned = tuned()
        self.running, self.results = {}, {}

    def add(self, name, grad):
        grad = grad.astype(jnp.bfloat16)
        self.running[name] = tuned_reduce(grad) if self.tuned else general_stages(grad)

    def step(self, values):
        after = []
        for name in list(self.running):
            try:
                after += next(self.running[name])
            except StopIteration as stop:
                self.results[name] = stop.value
                del self.running[name]
        if not after:
            return values
        return fence(values, after)

    def finish(self):
        while self.running:
            self.step_free()
        return self.results

    def step_free(self):
        for name in list(self.running):
            try:
                next(self.running[name])
            except StopIteration as stop:
                self.results[name] = stop.value
                del self.running[name]


def tuned():
    return lax.axis_size("rep") == 4 and lax.axis_size("shard") == 8


def gather_weights(mixer_in, mixer_out, swiglu_in, swiglu_out, gains, conv_kernel):
    rows = mixer_in.shape[0]
    owners = lax.axis_size("shard")
    width = conv_kernel.shape[1]
    count = gains.shape[0] + conv_kernel.size
    lanes = -(-count // rows)
    vector = jnp.concatenate([gains, conv_kernel.reshape(-1)])
    vector = jnp.pad(vector, (0, lanes * rows - count)).reshape(rows, lanes)
    low_in = mixer_in.astype(jnp.bfloat16)
    tail = STEP_LANES - MH - lanes
    conv_piece = jnp.concatenate(
        [low_in[:, QKV + GATE :], vector.astype(jnp.bfloat16), jnp.zeros((rows, tail), jnp.bfloat16)],
        axis=1,
    )
    pieces = [
        conv_piece,
        low_in[:, :QKV],
        low_in[:, QKV : QKV + GATE],
        mixer_out.astype(jnp.bfloat16),
        swiglu_in.astype(jnp.bfloat16),
        swiglu_out.astype(jnp.bfloat16),
    ]
    if tuned():
        pieces = tuned_gather(pieces)
    else:
        pieces = [general_gather(piece) for piece in pieces]
    every = pieces[0][:, CONV + MH : CONV + MH + lanes].reshape(owners, rows * lanes)
    gains_all = every[:, : gains.shape[0]].reshape(-1)
    taps = every[:, gains.shape[0] : count].reshape(owners, KC + 1, width)
    taps = jnp.swapaxes(taps, 0, 1).reshape(KC + 1, owners * width)
    return pieces + [gains_all.astype(jnp.float32), taps.astype(jnp.float32)]


def with_vectors(conv_g, gains_g, taps_g, head_grad):
    owners = lax.axis_size("shard")
    rows = conv_g.shape[0] // owners
    width = taps_g.shape[1] // owners
    vector = jnp.concatenate(
        [
            gains_g.reshape(owners, -1),
            jnp.swapaxes(taps_g.reshape(KC + 1, owners, width), 0, 1).reshape(owners, -1),
            jnp.broadcast_to(head_grad.reshape(1, -1), (owners, head_grad.size)),
        ],
        axis=1,
    )
    count = vector.shape[1]
    lanes = -(-count // rows)
    vector = jnp.pad(vector, ((0, 0), (0, lanes * rows - count))).reshape(owners * rows, lanes)
    used = CONV + MH
    vector = jnp.pad(vector, ((0, 0), (MH, STEP_LANES - MH - lanes)))
    return jnp.concatenate([conv_g[:, :CONV], conv_g[:, CONV:] + vector], axis=1)


def split_vectors(conv, own_gains, width, head_shape):
    rows = conv.shape[0]
    count = own_gains + (KC + 1) * width + head_shape[0] * head_shape[1]
    lanes = -(-count // rows)
    used = CONV + MH
    flat = conv[:, used : used + lanes].astype(jnp.float32).reshape(-1)
    taps_end = own_gains + (KC + 1) * width
    return (
        flat[:own_gains],
        flat[own_gains:taps_end].reshape(KC + 1, width),
        flat[taps_end:count].reshape(head_shape),
    )


def forward_backward(tokens, cotangent, seq_row, weights, head_params):
    low, low_back = make_rounders()
    w_conv, w_qkv, w_gate, w_out, w_up, w_down, gain_all, taps = weights
    segment, token_position, valid = layout(seq_row, tokens.shape[0])
    values = tokens.astype(jnp.float32)

    normed, pull_norm = jax.vjp(lambda v, g: low(normalize(v, g)), values, gain_all[:D])
    normed_low = rows_of(normed)
    scan_out, pull_scan = jax.vjp(
        lambda p, k, h: state_space(p, k, h, segment, low, low_back),
        dot(normed_low, w_conv),
        taps,
        head_params,
    )
    context, pull_context = jax.vjp(
        lambda p: attention(p, segment, token_position, low, low_back), dot(normed_low, w_qkv)
    )
    mamba_out, pull_gating = jax.vjp(
        lambda s, z, g: gating(s, z, g, low), scan_out, dot(normed_low, w_gate), gain_all[2 * D :]
    )
    joined = jnp.concatenate([rows_of(context), rows_of(mamba_out)], axis=1)
    hidden = values + dot(joined, w_out)
    normed_ff, pull_ff = jax.vjp(lambda v, g: low(normalize(v, g)), hidden, gain_all[D : 2 * D])
    normed_ff_low = rows_of(normed_ff)
    activated, pull_active = jax.vjp(lambda g: activation(g, low), dot(normed_ff_low, w_up))
    activated_low = rows_of(activated)
    output = (hidden + dot(activated_low, w_down)).astype(jnp.bfloat16)

    moving = Reductions()
    cot = jnp.where(valid[:, None], cotangent, jnp.zeros_like(cotangent))
    (up_cot,) = pull_active(dot_right(cot, w_down))
    up_cot = rows_of(up_cot)
    moving.add("down", dot_left(activated_low, cot))
    (up_cot,) = moving.step([up_cot])
    moving.add("up", dot_left(normed_ff_low, up_cot))
    (ff_cot,) = moving.step([dot_right(up_cot, w_up)])
    hidden_part, gain_ff = pull_ff(ff_cot)
    hidden_cot = cot.astype(jnp.float32) + hidden_part
    hidden_low = rows_of(hidden_cot)
    moving.add("out", dot_left(joined, hidden_low))
    (joined_cot,) = moving.step([dot_right(hidden_low, w_out)])
    scan_cot, gate_cot, gain_scan = pull_gating(joined_cot[:, QUERY_HEADS * HEAD_SIZE :])
    gate_cot = rows_of(gate_cot)
    moving.add("gate", dot_left(normed_low, gate_cot))
    (scan_cot,) = moving.step([scan_cot])
    conv_cot, taps_grad, head_grad = pull_scan(scan_cot)
    conv_cot = rows_of(conv_cot)
    (context_cot,) = moving.step([fence([joined_cot[:, : QUERY_HEADS * HEAD_SIZE]], [conv_cot])[0]])
    (qkv_cot,) = pull_context(context_cot)
    qkv_cot = rows_of(qkv_cot)
    normed_cot = (
        dot_right(qkv_cot, w_qkv) + dot_right(gate_cot, w_gate) + dot_right(conv_cot, w_conv)
    )
    tokens_part, gain_in = pull_norm(normed_cot)
    token_grad = hidden_cot + tokens_part
    gains_grad = jnp.concatenate([gain_in, gain_ff, gain_scan])
    moving.add(
        "conv", with_vectors(dot_left(normed_low, conv_cot), gains_grad, taps_grad, head_grad)
    )
    moving.add("qkv", dot_left(normed_low, qkv_cot))
    return output, token_grad, moving.finish()


def on_device(
    tokens,
    cotangent,
    seq_lengths,
    mixer_in,
    mixer_in_mean,
    mixer_in_square,
    mixer_out,
    mixer_out_mean,
    mixer_out_square,
    swiglu_in,
    swiglu_in_mean,
    swiglu_in_square,
    swiglu_out,
    swiglu_out_mean,
    swiglu_out_square,
    gains,
    gains_mean,
    gains_square,
    conv_kernel,
    conv_kernel_mean,
    conv_kernel_square,
    head_params,
    head_params_mean,
    head_params_square,
):
    weights = gather_weights(mixer_in, mixer_out, swiglu_in, swiglu_out, gains, conv_kernel)
    output, token_grad, sums = forward_backward(
        tokens, cotangent, seq_lengths[0], weights, head_params
    )
    own_gains, own_taps, head_grad = split_vectors(
        sums["conv"], gains.shape[0], conv_kernel.shape[1], head_params.shape
    )
    matrix = jnp.concatenate([sums["qkv"], sums["gate"], sums["conv"][:, : CONV + MH]], axis=1)
    owned = (
        matrix.astype(jnp.float32),
        sums["out"].astype(jnp.float32),
        sums["up"].astype(jnp.float32),
        sums["down"].astype(jnp.float32),
        own_gains,
        own_taps,
    )
    masters = (mixer_in, mixer_out, swiglu_in, swiglu_out, gains, conv_kernel)
    means = (
        mixer_in_mean,
        mixer_out_mean,
        swiglu_in_mean,
        swiglu_out_mean,
        gains_mean,
        conv_kernel_mean,
    )
    squares = (
        mixer_in_square,
        mixer_out_square,
        swiglu_in_square,
        swiglu_out_square,
        gains_square,
        conv_kernel_square,
    )
    rates = (MATRIX_RATE, MATRIX_RATE, MATRIX_RATE, MATRIX_RATE, VECTOR_RATE, VECTOR_RATE)
    updated = [
        adamw(masters[index], means[index], squares[index], owned[index], rates[index])
        for index in range(6)
    ]
    head_new = adamw(head_params, head_params_mean, head_params_square, head_grad, VECTOR_RATE)
    return (
        output,
        token_grad,
        updated[0][0],
        updated[0][1],
        updated[0][2],
        updated[1][0],
        updated[1][1],
        updated[1][2],
        updated[2][0],
        updated[2][1],
        updated[2][2],
        updated[3][0],
        updated[3][1],
        updated[3][2],
        updated[4][0],
        updated[4][1],
        updated[4][2],
        updated[5][0],
        updated[5][1],
        updated[5][2],
        head_new[0],
        head_new[1],
        head_new[2],
    )


def solution(mesh):
    return jax.shard_map(
        on_device,
        mesh=mesh,
        in_specs=(
            P(("rep", "shard"), None),
            P(("rep", "shard"), None),
            P(("rep", "shard"), None),
            P("shard", None),
            P("shard", None),
            P("shard", None),
            P("shard", None),
            P("shard", None),
            P("shard", None),
            P("shard", None),
            P("shard", None),
            P("shard", None),
            P("shard", None),
            P("shard", None),
            P("shard", None),
            P("shard"),
            P("shard"),
            P("shard"),
            P(None, "shard"),
            P(None, "shard"),
            P(None, "shard"),
            P(),
            P(),
            P(),
        ),
        out_specs=(
            P(("rep", "shard"), None),
            P(("rep", "shard"), None),
            P("shard", None),
            P("shard", None),
            P("shard", None),
            P("shard", None),
            P("shard", None),
            P("shard", None),
            P("shard", None),
            P("shard", None),
            P("shard", None),
            P("shard", None),
            P("shard", None),
            P("shard", None),
            P("shard"),
            P("shard"),
            P("shard"),
            P(None, "shard"),
            P(None, "shard"),
            P(None, "shard"),
            P(),
            P(),
            P(),
        ),
        check_vma=False,
    )
```

```python
import functools

import jax
import jax.numpy as jnp
from jax import lax
from jax.experimental import pallas as pl
from jax.experimental.pallas import tpu as pltpu
from jax.sharding import Mesh, PartitionSpec as P

D = 1024
FF = 2048
QUERY_HEADS = 8
KEY_VALUE_HEADS = 2
HEAD_SIZE = 64
MH = 24
MP = 64
NS = 128
KC = 4
STEP = 10


NORM_EPS = 1e-05
ROPE_BASE = 100000000000.0
BETA_MEAN = 0.9
BETA_SQUARE = 0.95
ADAM_EPS = 1e-08
DECAY = 0.1
MATRIX_RATE = 0.03
VECTOR_RATE = 0.5


def make_rounders():

    def round_value(values):
        return lax.optimization_barrier(values.astype(jnp.bfloat16)).astype(jnp.float32)

    def pass_value(values):
        return values

    value_rounder = jax.custom_vjp(round_value)
    grad_rounder = jax.custom_vjp(pass_value)

    def value_keep(values):
        return (round_value(values), None)

    def value_pass(kept, grad):
        return (grad,)

    def grad_keep(values):
        return (values, None)

    def grad_round(kept, grad):
        return (round_value(grad),)

    value_rounder.defvjp(value_keep, value_pass)
    grad_rounder.defvjp(grad_keep, grad_round)
    return (value_rounder, grad_rounder)


def normalize(values, gain):
    return values * lax.rsqrt(jnp.mean(values * values, axis=-1, keepdims=True) + NORM_EPS) * gain


def layout(seq_row, span_length):
    count = seq_row.shape[0]
    ends = jnp.cumsum(seq_row)
    starts = ends - seq_row
    slots = jnp.arange(span_length, dtype=jnp.int32)
    segment = jnp.sum((slots[:, None] >= ends[None, :]).astype(jnp.int32), axis=1)
    valid = slots < ends[count - 1]
    segment = jnp.where(valid, segment, count + slots)
    match = segment[:, None] == jnp.arange(count, dtype=jnp.int32)[None, :]
    first = jnp.sum(jnp.where(match, starts[None, :], 0), axis=1)
    token_position = jnp.where(valid, slots - first, 0)
    return (segment, token_position, valid)


def apply_rotary(values, token_position):
    half = HEAD_SIZE // 2
    freq = ROPE_BASE ** (-(jnp.arange(half, dtype=jnp.float32) * 2.0 / HEAD_SIZE))
    angle = token_position.astype(jnp.float32)[:, None] * freq[None, :]
    cosine = jnp.cos(angle)[:, None, :]
    sine = jnp.sin(angle)[:, None, :]
    first_half = values[..., :half]
    second_half = values[..., half:]
    return jnp.concatenate(
        [first_half * cosine - second_half * sine, second_half * cosine + first_half * sine],
        axis=-1,
    )


def rows_of(matrix):
    return matrix.astype(jnp.bfloat16)


def dot(left, right):
    return jnp.dot(left, right, preferred_element_type=jnp.float32)


def dot_left(left, right):
    return lax.dot_general(left, right, (((0,), (0,)), ((), ())), preferred_element_type=jnp.float32)


def dot_right(left, right):
    return lax.dot_general(left, right, (((1,), (1,)), ((), ())), preferred_element_type=jnp.float32)


def attention(projected, segment, token_position, low, low_back):
    span_length = projected.shape[0]
    key_offset = QUERY_HEADS * HEAD_SIZE
    value_offset = key_offset + KEY_VALUE_HEADS * HEAD_SIZE
    query_matrix = projected[:, :key_offset].reshape(span_length, QUERY_HEADS, HEAD_SIZE)
    key_matrix = projected[:, key_offset:value_offset].reshape(
        span_length, KEY_VALUE_HEADS, HEAD_SIZE
    )
    value_matrix = low(
        projected[:, value_offset:].reshape(span_length, KEY_VALUE_HEADS, HEAD_SIZE)
    )
    query_matrix = low(apply_rotary(query_matrix, token_position)).reshape(
        span_length, KEY_VALUE_HEADS, QUERY_HEADS // KEY_VALUE_HEADS, HEAD_SIZE
    )
    key_matrix = low(apply_rotary(key_matrix, token_position))
    slots = jnp.arange(span_length, dtype=jnp.int32)
    allowed = (segment[:, None] == segment[None, :]) & (slots[None, :] <= slots[:, None])
    scores = jnp.einsum("tagd,sad->agts", query_matrix, key_matrix, precision=None) * HEAD_SIZE ** (
        -0.5
    )
    scores = low_back(scores)
    scores = jnp.where(allowed[None, None], scores, -1000000000.0)
    probs = low(jax.nn.softmax(scores, axis=-1))
    context = low_back(jnp.einsum("agts,sad->tagd", probs, value_matrix, precision=None))
    return low(context.reshape(span_length, QUERY_HEADS * HEAD_SIZE))


def convolution(conv_in, kernel, segment, low):
    span_length = conv_in.shape[0]
    summed = jnp.zeros_like(conv_in) + kernel[KC][None, :]
    for lag in range(KC):
        shifted = jnp.concatenate(
            [jnp.zeros((lag, CONV), jnp.float32), conv_in[: span_length - lag]], axis=0
        )
        earlier = jnp.concatenate(
            [jnp.full((lag,), -1, jnp.int32), segment[: span_length - lag]], axis=0
        )
        keep = earlier == segment
        summed = summed + kernel[KC - 1 - lag][None, :] * jnp.where(keep[:, None], shifted, 0.0)
    return low(jax.nn.silu(summed))


def scan(conv_out, step_raw, head_params, segment, low, low_back):
    span_length = conv_out.shape[0]
    slots = jnp.arange(span_length, dtype=jnp.int32)
    allowed = (segment[:, None] == segment[None, :]) & (slots[None, :] <= slots[:, None])
    scan_x = conv_out[:, : MH * MP].reshape(span_length, MH, MP)
    scan_b = conv_out[:, MH * MP : MH * MP + NS]
    scan_c = conv_out[:, MH * MP + NS :]
    step_size = jax.nn.softplus(step_raw + head_params[0][None, :])
    cumulative = jnp.cumsum(-step_size * jnp.exp(head_params[1])[None, :], axis=0)
    intersection = low_back(jnp.dot(scan_c, scan_b.T, precision=None))
    cum_heads = cumulative.T
    spread = cum_heads[:, :, None] - cum_heads[:, None, :]
    decay_matrix = jnp.exp(jnp.where(allowed[None], spread, -10000.0))
    mixing = low(intersection[None] * decay_matrix * step_size.T[:, None, :])
    scan_out = low_back(jnp.einsum("hts,shp->thp", mixing, scan_x, precision=None))
    scan_out = scan_out + head_params[2][None, :, None] * scan_x
    return scan_out.reshape(span_length, MH * MP)


def gating(scan_out, gate_z, gain, low):
    return low(normalize(scan_out * jax.nn.silu(gate_z), gain))


def activation(gate_up, low):
    return low(jax.nn.silu(gate_up[:, :FF]) * gate_up[:, FF:])


def adamw(weight, mean, square, grad, rate):
    mean_new = BETA_MEAN * mean + (1.0 - BETA_MEAN) * grad
    square_new = BETA_SQUARE * square + (1.0 - BETA_SQUARE) * grad * grad
    corrected = (
        mean_new
        / (1.0 - BETA_MEAN**STEP)
        / (jnp.sqrt(square_new / (1.0 - BETA_SQUARE**STEP)) + ADAM_EPS)
    )
    return (weight - rate * (corrected + DECAY * weight), mean_new, square_new)


QKV = (QUERY_HEADS + 2 * KEY_VALUE_HEADS) * HEAD_SIZE
GATE = MH * MP
CONV = MH * MP + 2 * NS
STEP_LANES = 128


def general_gather(own, rep, shard):
    part = own
    if rep:
        copies = lax.axis_size(rep)
        rows = own.shape[0] // copies
        part = lax.dynamic_slice_in_dim(own, lax.axis_index(rep) * rows, rows, 0)
    return lax.all_gather(part, shard + rep, axis=0, tiled=True)


def general_reduce(grad, rep, shard):
    piece = lax.psum_scatter(grad, shard + rep, scatter_dimension=0, tiled=True)
    return lax.all_gather(piece, rep, axis=0, tiled=True)


def place():
    return tuple(lax.axis_index(name) for name in ("x", "core", "z", "y"))


def send(values, dx=0, dcore=0, dz=0, dy=0):
    pairs = []
    for x in range(2):
        for core in range(2):
            for z in range(4):
                for y in range(2):
                    start = (x * 2 + core) * 8 + z * 2 + y
                    end = ((x ^ dx) * 2 + (core ^ dcore)) * 8 + ((z + dz) % 4) * 2 + (y ^ dy)
                    pairs.append((start, end))
    return lax.ppermute(values, ("x", "core", "z", "y"), pairs)


def pick(values, index, axis):
    return lax.dynamic_index_in_dim(values, index, axis, keepdims=False)


def fence(values, after):
    def kernel(*refs):
        del refs

    return pl.pallas_call(
        kernel,
        out_shape=[jax.ShapeDtypeStruct(value.shape, value.dtype) for value in values],
        in_specs=[pl.BlockSpec(memory_space=pl.ANY)] * (len(values) + len(after)),
        out_specs=[pl.BlockSpec(memory_space=pl.ANY)] * len(values),
        input_output_aliases={index: index for index in range(len(values))},
        name="fence",
    )(*values, *after)


def assemble(held, rows):
    quarter = rows // 8
    columns = held[0].shape[-1]

    def kernel(*refs):
        sources, target, sems = refs[:8], refs[8], refs[9]
        x, core, z, y = place()
        copies = []
        for other_core in range(2):
            half = core if other_core == 0 else 1 - core
            for other_y in range(2):
                row = y if other_y == 0 else 1 - y
                for turn in range(4):
                    owner = ((z + 4 - turn) % 4) * 2 + row
                    base = owner * rows + half * (rows // 2)
                    main = sources[other_core * 4 + other_y].at[turn]
                    cross = sources[other_core * 4 + 2 + other_y].at[turn]
                    for piece, start, count in (
                        (main.at[pl.ds(0, quarter)], base + x * quarter, quarter),
                        (main.at[pl.ds(quarter, 2 * quarter)], base + 2 * quarter, 2 * quarter),
                        (cross, base + (1 - x) * quarter, quarter),
                    ):
                        place_at = pl.ds(pl.multiple_of(start, 16), count)
                        copies.append(
                            pltpu.make_async_copy(piece, target.at[place_at], sems.at[len(copies)])
                        )
        for copy in copies:
            copy.start()
        for copy in copies:
            copy.wait()

    return pl.pallas_call(
        kernel,
        out_shape=jax.ShapeDtypeStruct((8 * rows, columns), jnp.bfloat16),
        in_specs=[pl.BlockSpec(memory_space=pl.ANY)] * 8,
        out_specs=pl.BlockSpec(memory_space=pltpu.VMEM),
        scratch_shapes=[pltpu.SemaphoreType.DMA((48,))],
        compiler_params=pltpu.CompilerParams(vmem_limit_bytes=24 * 1024 * 1024),
        name="assemble",
    )(*held)


def tuned_gather(pieces):
    x, core, z, y = place()
    results, after = [], None
    for own in pieces:
        rows = own.shape[0]
        quarter = rows // 8
        half = lax.dynamic_slice_in_dim(own, core * (rows // 2), rows // 2, 0)
        mine = jnp.concatenate(
            [lax.dynamic_slice_in_dim(half, x * quarter, quarter, 0), half[2 * quarter :]], axis=0
        )
        if after is not None:
            mine = fence([mine], after)[0]
        after = [send(mine, dz=turn) for turn in range(1, 4)]
        along_z = jnp.stack([mine] + after)
        across_y = send(along_z, dy=1)
        held = [along_z, across_y]
        held += [send(group[:, :quarter], dx=1) for group in held]
        held += [send(group, dcore=1) for group in held]
        results.append(assemble(held, rows))
    return results


def add_low(left, right):
    return (left.astype(jnp.float32) + right.astype(jnp.float32)).astype(jnp.bfloat16)


def tuned_reduce(grad):
    rows, columns = grad.shape[0] // 8, grad.shape[1]
    quarter = rows // 8
    x, core, z, y = place()
    parts = grad.reshape(4, 2, 2, rows // 2, columns)
    far = pick(parts, 1 - core, 2)
    yield [far]
    half = add_low(pick(parts, core, 2), send(far, dcore=1))
    far = lax.dynamic_slice_in_dim(half, (1 - x) * quarter, quarter, 2)
    yield [far]
    near = add_low(lax.dynamic_slice_in_dim(half, x * quarter, quarter, 2), send(far, dx=1))
    both = half[:, :, 2 * quarter :]
    there = jnp.concatenate([pick(near, 1 - y, 1), pick(both, 1 - y, 1)], axis=1)
    here = jnp.concatenate([pick(near, y, 1), pick(both, y, 1)], axis=1)
    yield [there]
    column = add_low(here, send(there, dy=1))
    turns = [pick(column, (z + turn) % 4, 0) for turn in range(1, 4)]
    yield turns
    total = pick(column, z, 0).astype(jnp.float32)
    for turn in range(1, 4):
        total = total + send(turns[turn - 1], dz=turn).astype(jnp.float32)
    total = total.astype(jnp.bfloat16)
    yield [total]
    across = send(total, dx=1)
    own_x, other_x = total[:quarter], across[:quarter]
    owned = jnp.concatenate(
        [
            jnp.where(x == 0, own_x, other_x),
            jnp.where(x == 0, other_x, own_x),
            add_low(total[quarter:], across[quarter:]),
        ],
        axis=0,
    )
    yield [owned]
    beside = send(owned, dcore=1)
    return jnp.concatenate(
        [jnp.where(core == 0, owned, beside), jnp.where(core == 0, beside, owned)], axis=0
    )


def paired_reduce(grad):
    rows, columns = grad.shape[0] // 8, grad.shape[1]
    x, core, z, y = place()
    parts = grad.reshape(8, 2, rows // 2, columns)
    far = pick(parts, 1 - core, 1)
    yield [far]
    half = add_low(pick(parts, core, 1), send(far, dcore=1)).reshape(4 * rows, columns)
    yield [half]
    own = lax.psum_scatter(half, ("z", "y", "x"), scatter_dimension=0, tiled=True)
    yield None
    across = send(own, dx=1)
    owned = jnp.concatenate(
        [jnp.where(x == 0, own, across), jnp.where(x == 0, across, own)], axis=0
    )
    yield None
    beside = send(owned, dcore=1)
    return jnp.concatenate(
        [jnp.where(core == 0, owned, beside), jnp.where(core == 0, beside, owned)], axis=0
    )


def general_stages(grad, rep, shard):
    yield None
    return general_reduce(grad, rep, shard)


class Reductions:

    def __init__(self, axes):
        self.axes = axes
        self.running, self.results, self.waiting = {}, {}, {}

    def add(self, name, grad, paired=False):
        grad = grad.astype(jnp.bfloat16)
        if not tuned(self.axes):
            self.running[name] = general_stages(grad, *self.axes)
        elif paired:
            self.running[name] = paired_reduce(grad)
        else:
            self.running[name] = tuned_reduce(grad)

    def step(self, values):
        after = []
        for name in list(self.running):
            if self.waiting.get(name):
                continue
            ready = self.advance(name)
            if ready is None:
                self.waiting[name] = True
            else:
                after += ready
        return fence(values, after) if after else values

    def advance(self, name):
        try:
            return next(self.running[name])
        except StopIteration as stop:
            self.results[name] = stop.value
            del self.running[name]
            return []

    def finish(self):
        while self.running:
            for name in list(self.running):
                self.advance(name)
        return self.results


def tuned(axes):
    return axes == (("x", "core"), ("z", "y"))


def gather_weights(axes, mixer_in, mixer_out, swiglu_in, swiglu_out, gains, conv_kernel):
    rows = mixer_in.shape[0]
    rep, shard = axes
    owners = lax.axis_size(shard)
    width = conv_kernel.shape[1]
    count = gains.shape[0] + conv_kernel.size
    lanes = -(-count // rows)
    vector = jnp.concatenate([gains, conv_kernel.reshape(-1)])
    vector = jnp.pad(vector, (0, lanes * rows - count)).reshape(rows, lanes)
    low_in = mixer_in.astype(jnp.bfloat16)
    tail = STEP_LANES - MH - lanes
    conv_piece = jnp.concatenate(
        [low_in[:, QKV + GATE :], vector.astype(jnp.bfloat16), jnp.zeros((rows, tail), jnp.bfloat16)],
        axis=1,
    )
    pieces = [conv_piece, low_in[:, : QKV + GATE]]
    if tuned(axes):
        pieces = tuned_gather(pieces)
    else:
        pieces = [general_gather(piece, rep, shard) for piece in pieces]
    for master in (mixer_out, swiglu_in, swiglu_out):
        pieces.append(general_gather(master.astype(jnp.bfloat16), rep, shard))
    every = pieces[0][:, CONV + MH : CONV + MH + lanes].reshape(owners, rows * lanes)
    gains_all = every[:, : gains.shape[0]].reshape(-1)
    taps = every[:, gains.shape[0] : count].reshape(owners, KC + 1, width)
    taps = jnp.swapaxes(taps, 0, 1).reshape(KC + 1, owners * width)
    return pieces + [gains_all.astype(jnp.float32), taps.astype(jnp.float32)]


def with_vectors(conv_g, gains_g, taps_g, head_grad, owners):
    rows = conv_g.shape[0] // owners
    width = taps_g.shape[1] // owners
    vector = jnp.concatenate(
        [
            gains_g.reshape(owners, -1),
            jnp.swapaxes(taps_g.reshape(KC + 1, owners, width), 0, 1).reshape(owners, -1),
            jnp.broadcast_to(head_grad.reshape(1, -1), (owners, head_grad.size)),
        ],
        axis=1,
    )
    count = vector.shape[1]
    lanes = -(-count // rows)
    vector = jnp.pad(vector, ((0, 0), (0, lanes * rows - count))).reshape(owners * rows, lanes)
    vector = jnp.pad(vector, ((0, 0), (MH, STEP_LANES - MH - lanes)))
    return jnp.concatenate([conv_g[:, :CONV], conv_g[:, CONV:] + vector], axis=1)


def split_vectors(conv, own_gains, width, head_shape):
    rows = conv.shape[0]
    count = own_gains + (KC + 1) * width + head_shape[0] * head_shape[1]
    lanes = -(-count // rows)
    used = CONV + MH
    flat = conv[:, used : used + lanes].astype(jnp.float32).reshape(-1)
    taps_end = own_gains + (KC + 1) * width
    return (
        flat[:own_gains],
        flat[own_gains:taps_end].reshape(KC + 1, width),
        flat[taps_end:count].reshape(head_shape),
    )


def forward_backward(axes, tokens, cotangent, seq_row, weights, head_params):
    low, low_back = make_rounders()
    w_conv, w_side, w_out, w_up, w_down, gain_all, taps = weights
    segment, token_position, valid = layout(seq_row, tokens.shape[0])
    values = tokens.astype(jnp.float32)
    context_width = QUERY_HEADS * HEAD_SIZE

    normed, pull_norm = jax.vjp(lambda v, g: low(normalize(v, g)), values, gain_all[:D])
    normed_low = rows_of(normed)
    projected = dot(normed_low, w_conv)
    conv_out, pull_conv = jax.vjp(
        lambda p, k: convolution(p, k, segment, low), projected[:, :CONV], taps
    )
    scan_out, pull_scan = jax.vjp(
        lambda c, r, h: scan(c, r, h, segment, low, low_back),
        conv_out,
        projected[:, CONV : CONV + MH],
        head_params,
    )
    beside = dot(normed_low, w_side)
    context, pull_context = jax.vjp(
        lambda p: attention(p, segment, token_position, low, low_back), beside[:, :QKV]
    )
    mamba_out, pull_gating = jax.vjp(
        lambda s, z, g: gating(s, z, g, low), scan_out, beside[:, QKV:], gain_all[2 * D :]
    )
    joined = jnp.concatenate([rows_of(context), rows_of(mamba_out)], axis=1)
    hidden = values + dot(joined, w_out)
    normed_ff, pull_ff = jax.vjp(lambda v, g: low(normalize(v, g)), hidden, gain_all[D : 2 * D])
    normed_ff_low = rows_of(normed_ff)
    activated, pull_active = jax.vjp(lambda g: activation(g, low), dot(normed_ff_low, w_up))
    activated_low = rows_of(activated)
    output = (hidden + dot(activated_low, w_down)).astype(jnp.bfloat16)

    moving = Reductions(axes)
    cot = jnp.where(valid[:, None], cotangent, jnp.zeros_like(cotangent))
    (up_cot,) = pull_active(dot_right(cot, w_down))
    up_cot = rows_of(up_cot)
    moving.add("down", dot_left(activated_low, cot), paired=True)
    (up_cot,) = moving.step([up_cot])
    moving.add("up", dot_left(normed_ff_low, up_cot), paired=True)
    (ff_cot,) = moving.step([dot_right(up_cot, w_up)])
    hidden_part, gain_ff = pull_ff(ff_cot)
    hidden_cot = cot.astype(jnp.float32) + hidden_part
    hidden_low = rows_of(hidden_cot)
    moving.add("out", dot_left(joined, hidden_low), paired=True)
    (joined_cot,) = moving.step([dot_right(hidden_low, w_out)])
    scan_cot, gate_cot, gain_scan = pull_gating(joined_cot[:, context_width:])
    (qkv_cot,) = pull_context(joined_cot[:, :context_width])
    side_cot = jnp.concatenate([rows_of(qkv_cot), rows_of(gate_cot)], axis=1)
    moving.add("side", dot_left(normed_low, side_cot))
    (scan_cot,) = moving.step([scan_cot])
    conv_out_cot, step_cot, head_grad = pull_scan(scan_cot)
    (conv_out_cot,) = moving.step([conv_out_cot])
    conv_cot, taps_grad = pull_conv(conv_out_cot)
    conv_cot = rows_of(
        jnp.concatenate(
            [conv_cot, step_cot, jnp.zeros((tokens.shape[0], STEP_LANES - MH), jnp.float32)], axis=1
        )
    )
    (conv_cot,) = moving.step([conv_cot])
    normed_cot = dot_right(side_cot, w_side) + dot_right(conv_cot, w_conv)
    tokens_part, gain_in = pull_norm(normed_cot)
    token_grad = hidden_cot + tokens_part
    gains_grad = jnp.concatenate([gain_in, gain_ff, gain_scan])
    owners = lax.axis_size(axes[1])
    moving.add(
        "conv",
        with_vectors(dot_left(normed_low, conv_cot), gains_grad, taps_grad, head_grad, owners),
    )
    return output, token_grad, moving.finish()


def on_device(
    axes,
    tokens,
    cotangent,
    seq_lengths,
    mixer_in,
    mixer_in_mean,
    mixer_in_square,
    mixer_out,
    mixer_out_mean,
    mixer_out_square,
    swiglu_in,
    swiglu_in_mean,
    swiglu_in_square,
    swiglu_out,
    swiglu_out_mean,
    swiglu_out_square,
    gains,
    gains_mean,
    gains_square,
    conv_kernel,
    conv_kernel_mean,
    conv_kernel_square,
    head_params,
    head_params_mean,
    head_params_square,
):
    weights = gather_weights(axes, mixer_in, mixer_out, swiglu_in, swiglu_out, gains, conv_kernel)
    output, token_grad, sums = forward_backward(
        axes, tokens, cotangent, seq_lengths[0], weights, head_params
    )
    own_gains, own_taps, head_grad = split_vectors(
        sums["conv"], gains.shape[0], conv_kernel.shape[1], head_params.shape
    )
    matrix = jnp.concatenate([sums["side"], sums["conv"][:, : CONV + MH]], axis=1)
    owned = (
        matrix.astype(jnp.float32),
        sums["out"].astype(jnp.float32),
        sums["up"].astype(jnp.float32),
        sums["down"].astype(jnp.float32),
        own_gains,
        own_taps,
    )
    masters = (mixer_in, mixer_out, swiglu_in, swiglu_out, gains, conv_kernel)
    means = (
        mixer_in_mean,
        mixer_out_mean,
        swiglu_in_mean,
        swiglu_out_mean,
        gains_mean,
        conv_kernel_mean,
    )
    squares = (
        mixer_in_square,
        mixer_out_square,
        swiglu_in_square,
        swiglu_out_square,
        gains_square,
        conv_kernel_square,
    )
    rates = (MATRIX_RATE, MATRIX_RATE, MATRIX_RATE, MATRIX_RATE, VECTOR_RATE, VECTOR_RATE)
    updated = [
        adamw(masters[index], means[index], squares[index], owned[index], rates[index])
        for index in range(6)
    ]
    head_new = adamw(head_params, head_params_mean, head_params_square, head_grad, VECTOR_RATE)
    return (
        output,
        token_grad,
        updated[0][0],
        updated[0][1],
        updated[0][2],
        updated[1][0],
        updated[1][1],
        updated[1][2],
        updated[2][0],
        updated[2][1],
        updated[2][2],
        updated[3][0],
        updated[3][1],
        updated[3][2],
        updated[4][0],
        updated[4][1],
        updated[4][2],
        updated[5][0],
        updated[5][1],
        updated[5][2],
        head_new[0],
        head_new[1],
        head_new[2],
    )


def solution(mesh):
    rep, shard = ("rep",), ("shard",)
    if mesh.shape["rep"] == 4 and mesh.shape["shard"] == 8:
        rep, shard = ("x", "core"), ("z", "y")
        mesh = Mesh(mesh.devices.reshape(2, 2, 4, 2), rep + shard)
    rows, owned, across, copied = P(rep + shard, None), P(shard, None), P(None, shard), P()
    optimizer = (owned,) * 12 + (P(shard),) * 3 + (across,) * 3 + (copied,) * 3
    return jax.shard_map(
        functools.partial(on_device, (rep, shard)),
        mesh=mesh,
        in_specs=(rows, rows, rows) + optimizer,
        out_specs=(rows, rows) + optimizer,
        check_vma=False,
    )
```

```python
import functools

import jax
import jax.numpy as jnp
from jax import lax
from jax.experimental import pallas as pl
from jax.experimental.pallas import tpu as pltpu
from jax.sharding import Mesh, PartitionSpec as P

D = 1024
FF = 2048
QUERY_HEADS = 8
KEY_VALUE_HEADS = 2
HEAD_SIZE = 64
MH = 24
MP = 64
NS = 128
KC = 4
STEP = 10


NORM_EPS = 1e-05
ROPE_BASE = 100000000000.0
BETA_MEAN = 0.9
BETA_SQUARE = 0.95
ADAM_EPS = 1e-08
DECAY = 0.1
MATRIX_RATE = 0.03
VECTOR_RATE = 0.5


def make_rounders():

    def round_value(values):
        return lax.optimization_barrier(values.astype(jnp.bfloat16)).astype(jnp.float32)

    def pass_value(values):
        return values

    value_rounder = jax.custom_vjp(round_value)
    grad_rounder = jax.custom_vjp(pass_value)

    def value_keep(values):
        return (round_value(values), None)

    def value_pass(kept, grad):
        return (grad,)

    def grad_keep(values):
        return (values, None)

    def grad_round(kept, grad):
        return (round_value(grad),)

    value_rounder.defvjp(value_keep, value_pass)
    grad_rounder.defvjp(grad_keep, grad_round)
    return (value_rounder, grad_rounder)


def normalize(values, gain):
    return values * lax.rsqrt(jnp.mean(values * values, axis=-1, keepdims=True) + NORM_EPS) * gain


def layout(seq_row, span_length):
    count = seq_row.shape[0]
    ends = jnp.cumsum(seq_row)
    starts = ends - seq_row
    slots = jnp.arange(span_length, dtype=jnp.int32)
    segment = jnp.sum((slots[:, None] >= ends[None, :]).astype(jnp.int32), axis=1)
    valid = slots < ends[count - 1]
    segment = jnp.where(valid, segment, count + slots)
    match = segment[:, None] == jnp.arange(count, dtype=jnp.int32)[None, :]
    first = jnp.sum(jnp.where(match, starts[None, :], 0), axis=1)
    token_position = jnp.where(valid, slots - first, 0)
    return (segment, token_position, valid)


def apply_rotary(values, token_position):
    half = HEAD_SIZE // 2
    freq = ROPE_BASE ** (-(jnp.arange(half, dtype=jnp.float32) * 2.0 / HEAD_SIZE))
    angle = token_position.astype(jnp.float32)[:, None] * freq[None, :]
    cosine = jnp.cos(angle)[:, None, :]
    sine = jnp.sin(angle)[:, None, :]
    first_half = values[..., :half]
    second_half = values[..., half:]
    return jnp.concatenate(
        [first_half * cosine - second_half * sine, second_half * cosine + first_half * sine],
        axis=-1,
    )


def rows_of(matrix):
    return matrix.astype(jnp.bfloat16)


def dot(left, right):
    return jnp.dot(left, right, preferred_element_type=jnp.float32)


def dot_left(left, right):
    return lax.dot_general(left, right, (((0,), (0,)), ((), ())), preferred_element_type=jnp.float32)


def dot_right(left, right):
    return lax.dot_general(left, right, (((1,), (1,)), ((), ())), preferred_element_type=jnp.float32)


def attention(projected, segment, token_position, low, low_back):
    span_length = projected.shape[0]
    key_offset = QUERY_HEADS * HEAD_SIZE
    value_offset = key_offset + KEY_VALUE_HEADS * HEAD_SIZE
    query_matrix = projected[:, :key_offset].reshape(span_length, QUERY_HEADS, HEAD_SIZE)
    key_matrix = projected[:, key_offset:value_offset].reshape(
        span_length, KEY_VALUE_HEADS, HEAD_SIZE
    )
    value_matrix = low(
        projected[:, value_offset:].reshape(span_length, KEY_VALUE_HEADS, HEAD_SIZE)
    )
    query_matrix = low(apply_rotary(query_matrix, token_position)).reshape(
        span_length, KEY_VALUE_HEADS, QUERY_HEADS // KEY_VALUE_HEADS, HEAD_SIZE
    )
    key_matrix = low(apply_rotary(key_matrix, token_position))
    slots = jnp.arange(span_length, dtype=jnp.int32)
    allowed = (segment[:, None] == segment[None, :]) & (slots[None, :] <= slots[:, None])
    scores = jnp.einsum("tagd,sad->agts", query_matrix, key_matrix, precision=None) * HEAD_SIZE ** (
        -0.5
    )
    scores = low_back(scores)
    scores = jnp.where(allowed[None, None], scores, -1000000000.0)
    probs = low(jax.nn.softmax(scores, axis=-1))
    context = low_back(jnp.einsum("agts,sad->tagd", probs, value_matrix, precision=None))
    return low(context.reshape(span_length, QUERY_HEADS * HEAD_SIZE))


def convolution(conv_in, kernel, segment, low):
    span_length = conv_in.shape[0]
    summed = jnp.zeros_like(conv_in) + kernel[KC][None, :]
    for lag in range(KC):
        shifted = jnp.concatenate(
            [jnp.zeros((lag, CONV), jnp.float32), conv_in[: span_length - lag]], axis=0
        )
        earlier = jnp.concatenate(
            [jnp.full((lag,), -1, jnp.int32), segment[: span_length - lag]], axis=0
        )
        keep = earlier == segment
        summed = summed + kernel[KC - 1 - lag][None, :] * jnp.where(keep[:, None], shifted, 0.0)
    return low(jax.nn.silu(summed))


def scan(conv_out, step_raw, head_params, segment, low, low_back):
    span_length = conv_out.shape[0]
    slots = jnp.arange(span_length, dtype=jnp.int32)
    allowed = (segment[:, None] == segment[None, :]) & (slots[None, :] <= slots[:, None])
    scan_x = conv_out[:, : MH * MP].reshape(span_length, MH, MP)
    scan_b = conv_out[:, MH * MP : MH * MP + NS]
    scan_c = conv_out[:, MH * MP + NS :]
    step_size = jax.nn.softplus(step_raw + head_params[0][None, :])
    cumulative = jnp.cumsum(-step_size * jnp.exp(head_params[1])[None, :], axis=0)
    intersection = low_back(jnp.dot(scan_c, scan_b.T, precision=None))
    cum_heads = cumulative.T
    spread = cum_heads[:, :, None] - cum_heads[:, None, :]
    decay_matrix = jnp.exp(jnp.where(allowed[None], spread, -10000.0))
    mixing = low(intersection[None] * decay_matrix * step_size.T[:, None, :])
    scan_out = low_back(jnp.einsum("hts,shp->thp", mixing, scan_x, precision=None))
    scan_out = scan_out + head_params[2][None, :, None] * scan_x
    return scan_out.reshape(span_length, MH * MP)


def gating(scan_out, gate_z, gain, low):
    return low(normalize(scan_out * jax.nn.silu(gate_z), gain))


def activation(gate_up, low):
    return low(jax.nn.silu(gate_up[:, :FF]) * gate_up[:, FF:])


def adamw(weight, mean, square, grad, rate):
    mean_new = BETA_MEAN * mean + (1.0 - BETA_MEAN) * grad
    square_new = BETA_SQUARE * square + (1.0 - BETA_SQUARE) * grad * grad
    corrected = (
        mean_new
        / (1.0 - BETA_MEAN**STEP)
        / (jnp.sqrt(square_new / (1.0 - BETA_SQUARE**STEP)) + ADAM_EPS)
    )
    return (weight - rate * (corrected + DECAY * weight), mean_new, square_new)


QKV = (QUERY_HEADS + 2 * KEY_VALUE_HEADS) * HEAD_SIZE
GATE = MH * MP
CONV = MH * MP + 2 * NS
STEP_LANES = 128


def general_gather(own, rep, shard):
    part = own
    if rep:
        copies = lax.axis_size(rep)
        rows = own.shape[0] // copies
        part = lax.dynamic_slice_in_dim(own, lax.axis_index(rep) * rows, rows, 0)
    return lax.all_gather(part, shard + rep, axis=0, tiled=True)


def general_reduce(grad, rep, shard):
    piece = lax.psum_scatter(grad, shard + rep, scatter_dimension=0, tiled=True)
    return lax.all_gather(piece, rep, axis=0, tiled=True)


def place():
    return tuple(lax.axis_index(name) for name in ("x", "core", "z", "y"))


def send(values, dx=0, dcore=0, dz=0, dy=0):
    pairs = []
    for x in range(2):
        for core in range(2):
            for z in range(4):
                for y in range(2):
                    start = (x * 2 + core) * 8 + z * 2 + y
                    end = ((x ^ dx) * 2 + (core ^ dcore)) * 8 + ((z + dz) % 4) * 2 + (y ^ dy)
                    pairs.append((start, end))
    return lax.ppermute(values, ("x", "core", "z", "y"), pairs)


def pick(values, index, axis):
    return lax.dynamic_index_in_dim(values, index, axis, keepdims=False)


def fence(values, after):
    def kernel(*refs):
        del refs

    return pl.pallas_call(
        kernel,
        out_shape=[jax.ShapeDtypeStruct(value.shape, value.dtype) for value in values],
        in_specs=[pl.BlockSpec(memory_space=pl.ANY)] * (len(values) + len(after)),
        out_specs=[pl.BlockSpec(memory_space=pl.ANY)] * len(values),
        input_output_aliases={index: index for index in range(len(values))},
        name="fence",
    )(*values, *after)


def assemble(mine, beside, widths):
    half = mine.shape[0] // 8
    columns = [sum(widths[:index]) for index in range(len(widths))]

    def kernel(mine_ref, beside_ref, *refs):
        targets, sems = refs[:-1], refs[-1]
        core = lax.axis_index("core")
        copies = []
        for source, which in ((mine_ref, core), (beside_ref, 1 - core)):
            for owner in range(8):
                start = pl.multiple_of(owner * 2 * half + which * half, 16)
                for target, column, width in zip(targets, columns, widths):
                    copies.append(
                        pltpu.make_async_copy(
                            source.at[pl.ds(owner * half, half), pl.ds(column, width)],
                            target.at[pl.ds(start, half)],
                            sems.at[len(copies)],
                        )
                    )
        for copy in copies:
            copy.start()
        for copy in copies:
            copy.wait()

    return pl.pallas_call(
        kernel,
        out_shape=[jax.ShapeDtypeStruct((16 * half, width), jnp.bfloat16) for width in widths],
        in_specs=[pl.BlockSpec(memory_space=pl.ANY)] * 2,
        out_specs=[pl.BlockSpec(memory_space=pltpu.VMEM)] * len(widths),
        scratch_shapes=[pltpu.SemaphoreType.DMA((16 * len(widths),))],
        compiler_params=pltpu.CompilerParams(vmem_limit_bytes=24 * 1024 * 1024),
        name="assemble",
    )(mine, beside)


def paired_gather(own, widths):
    rows = own.shape[0]
    x, core, z, y = place()
    part = lax.dynamic_slice_in_dim(own, (core * 2 + x) * (rows // 4), rows // 4, 0)
    mine = lax.all_gather(part.astype(jnp.bfloat16), ("z", "y", "x"), axis=0, tiled=True)
    return assemble(mine, send(mine, dcore=1), widths)


def add_low(left, right):
    return (left.astype(jnp.float32) + right.astype(jnp.float32)).astype(jnp.bfloat16)


def tuned_reduce(grad):
    rows, columns = grad.shape[0] // 8, grad.shape[1]
    quarter = rows // 8
    x, core, z, y = place()
    parts = grad.reshape(4, 2, 2, rows // 2, columns)
    far = pick(parts, 1 - core, 2)
    yield [far]
    half = add_low(pick(parts, core, 2), send(far, dcore=1))
    far = lax.dynamic_slice_in_dim(half, (1 - x) * quarter, quarter, 2)
    yield [far]
    near = add_low(lax.dynamic_slice_in_dim(half, x * quarter, quarter, 2), send(far, dx=1))
    both = half[:, :, 2 * quarter :]
    there = jnp.concatenate([pick(near, 1 - y, 1), pick(both, 1 - y, 1)], axis=1)
    here = jnp.concatenate([pick(near, y, 1), pick(both, y, 1)], axis=1)
    yield [there]
    column = add_low(here, send(there, dy=1))
    turns = [pick(column, (z + turn) % 4, 0) for turn in range(1, 4)]
    yield turns
    total = pick(column, z, 0).astype(jnp.float32)
    for turn in range(1, 4):
        total = total + send(turns[turn - 1], dz=turn).astype(jnp.float32)
    total = total.astype(jnp.bfloat16)
    yield [total]
    across = send(total, dx=1)
    own_x, other_x = total[:quarter], across[:quarter]
    owned = jnp.concatenate(
        [
            jnp.where(x == 0, own_x, other_x),
            jnp.where(x == 0, other_x, own_x),
            add_low(total[quarter:], across[quarter:]),
        ],
        axis=0,
    )
    yield [owned]
    beside = send(owned, dcore=1)
    return jnp.concatenate(
        [jnp.where(core == 0, owned, beside), jnp.where(core == 0, beside, owned)], axis=0
    )


def paired_reduce(grad):
    rows, columns = grad.shape[0] // 8, grad.shape[1]
    x, core, z, y = place()
    parts = grad.reshape(8, 2, rows // 2, columns)
    far = pick(parts, 1 - core, 1)
    yield [far]
    half = add_low(pick(parts, core, 1), send(far, dcore=1))
    parts = half.reshape(8, 2, rows // 4, columns)
    far = pick(parts, 1 - x, 1)
    yield [far]
    near = add_low(pick(parts, x, 1), send(far, dx=1)).reshape(2 * rows, columns)
    yield [near]
    own = lax.psum_scatter(near, ("z", "y"), scatter_dimension=0, tiled=True)
    yield None
    across = send(own, dx=1)
    owned = jnp.concatenate(
        [jnp.where(x == 0, own, across), jnp.where(x == 0, across, own)], axis=0
    )
    yield None
    beside = send(owned, dcore=1)
    return jnp.concatenate(
        [jnp.where(core == 0, owned, beside), jnp.where(core == 0, beside, owned)], axis=0
    )


def general_stages(grad, rep, shard):
    yield None
    return general_reduce(grad, rep, shard)


class Reductions:

    def __init__(self, axes):
        self.axes = axes
        self.running, self.results, self.waiting = {}, {}, {}

    def add(self, name, grad, paired=False):
        grad = grad.astype(jnp.bfloat16)
        if not tuned(self.axes):
            self.running[name] = general_stages(grad, *self.axes)
        elif paired:
            self.running[name] = paired_reduce(grad)
        else:
            self.running[name] = tuned_reduce(grad)

    def step(self, values):
        after = []
        for name in list(self.running):
            if self.waiting.get(name):
                continue
            ready = self.advance(name)
            if ready is None:
                self.waiting[name] = True
            else:
                after += ready
        return fence(values, after) if after else values

    def advance(self, name):
        try:
            return next(self.running[name])
        except StopIteration as stop:
            self.results[name] = stop.value
            del self.running[name]
            return []

    def finish(self):
        while self.running:
            for name in list(self.running):
                self.advance(name)
        return self.results


def tuned(axes):
    return axes == (("x", "core"), ("z", "y"))


def gather_weights(axes, mixer_in, mixer_out, swiglu_in, swiglu_out, gains, conv_kernel):
    rows = mixer_in.shape[0]
    rep, shard = axes
    owners = lax.axis_size(shard)
    width = conv_kernel.shape[1]
    count = gains.shape[0] + conv_kernel.size
    lanes = -(-count // rows)
    vector = jnp.concatenate([gains, conv_kernel.reshape(-1)])
    vector = jnp.pad(vector, (0, lanes * rows - count)).reshape(rows, lanes)
    tail = STEP_LANES - MH - lanes
    piece_in = jnp.concatenate(
        [mixer_in[:, QKV + GATE :], vector, jnp.zeros((rows, tail)), mixer_in[:, : QKV + GATE]],
        axis=1,
    )
    pieces = []
    for master in (piece_in, mixer_out, swiglu_in, swiglu_out):
        widths = (master.shape[1],)
        if master is piece_in:
            widths = (CONV + STEP_LANES, QKV + GATE)
        if tuned(axes):
            pieces += paired_gather(master, widths)
        else:
            every = general_gather(master.astype(jnp.bfloat16), rep, shard)
            pieces += jnp.split(every, widths[:1], axis=1)[: len(widths)]
    every = pieces[0][:, CONV + MH : CONV + MH + lanes].reshape(owners, rows * lanes)
    gains_all = every[:, : gains.shape[0]].reshape(-1)
    taps = every[:, gains.shape[0] : count].reshape(owners, KC + 1, width)
    taps = jnp.swapaxes(taps, 0, 1).reshape(KC + 1, owners * width)
    return pieces + [gains_all.astype(jnp.float32), taps.astype(jnp.float32)]


def with_vectors(conv_g, gains_g, taps_g, head_grad, owners):
    rows = conv_g.shape[0] // owners
    width = taps_g.shape[1] // owners
    vector = jnp.concatenate(
        [
            gains_g.reshape(owners, -1),
            jnp.swapaxes(taps_g.reshape(KC + 1, owners, width), 0, 1).reshape(owners, -1),
            jnp.broadcast_to(head_grad.reshape(1, -1), (owners, head_grad.size)),
        ],
        axis=1,
    )
    count = vector.shape[1]
    lanes = -(-count // rows)
    vector = jnp.pad(vector, ((0, 0), (0, lanes * rows - count))).reshape(owners * rows, lanes)
    vector = jnp.pad(vector, ((0, 0), (MH, STEP_LANES - MH - lanes)))
    return jnp.concatenate([conv_g[:, :CONV], conv_g[:, CONV:] + vector], axis=1)


def split_vectors(conv, own_gains, width, head_shape):
    rows = conv.shape[0]
    count = own_gains + (KC + 1) * width + head_shape[0] * head_shape[1]
    lanes = -(-count // rows)
    used = CONV + MH
    flat = conv[:, used : used + lanes].astype(jnp.float32).reshape(-1)
    taps_end = own_gains + (KC + 1) * width
    return (
        flat[:own_gains],
        flat[own_gains:taps_end].reshape(KC + 1, width),
        flat[taps_end:count].reshape(head_shape),
    )


def forward_backward(axes, tokens, cotangent, seq_row, weights, head_params):
    low, low_back = make_rounders()
    w_conv, w_side, w_out, w_up, w_down, gain_all, taps = weights
    segment, token_position, valid = layout(seq_row, tokens.shape[0])
    values = tokens.astype(jnp.float32)
    context_width = QUERY_HEADS * HEAD_SIZE

    normed, pull_norm = jax.vjp(lambda v, g: low(normalize(v, g)), values, gain_all[:D])
    normed_low = rows_of(normed)
    projected = dot(normed_low, w_conv)
    conv_out, pull_conv = jax.vjp(
        lambda p, k: convolution(p, k, segment, low), projected[:, :CONV], taps
    )
    scan_out, pull_scan = jax.vjp(
        lambda c, r, h: scan(c, r, h, segment, low, low_back),
        conv_out,
        projected[:, CONV : CONV + MH],
        head_params,
    )
    beside = dot(normed_low, w_side)
    context, pull_context = jax.vjp(
        lambda p: attention(p, segment, token_position, low, low_back), beside[:, :QKV]
    )
    mamba_out, pull_gating = jax.vjp(
        lambda s, z, g: gating(s, z, g, low), scan_out, beside[:, QKV:], gain_all[2 * D :]
    )
    joined = jnp.concatenate([rows_of(context), rows_of(mamba_out)], axis=1)
    hidden = values + dot(joined, w_out)
    normed_ff, pull_ff = jax.vjp(lambda v, g: low(normalize(v, g)), hidden, gain_all[D : 2 * D])
    normed_ff_low = rows_of(normed_ff)
    activated, pull_active = jax.vjp(lambda g: activation(g, low), dot(normed_ff_low, w_up))
    activated_low = rows_of(activated)
    output = (hidden + dot(activated_low, w_down)).astype(jnp.bfloat16)

    moving = Reductions(axes)
    cot = jnp.where(valid[:, None], cotangent, jnp.zeros_like(cotangent))
    (up_cot,) = pull_active(dot_right(cot, w_down))
    up_cot = rows_of(up_cot)
    moving.add("down", dot_left(activated_low, cot), paired=True)
    (up_cot,) = moving.step([up_cot])
    moving.add("up", dot_left(normed_ff_low, up_cot), paired=True)
    (ff_cot,) = moving.step([dot_right(up_cot, w_up)])
    hidden_part, gain_ff = pull_ff(ff_cot)
    hidden_cot = cot.astype(jnp.float32) + hidden_part
    hidden_low = rows_of(hidden_cot)
    moving.add("out", dot_left(joined, hidden_low), paired=True)
    (joined_cot,) = moving.step([dot_right(hidden_low, w_out)])
    scan_cot, gate_cot, gain_scan = pull_gating(joined_cot[:, context_width:])
    (qkv_cot,) = pull_context(joined_cot[:, :context_width])
    side_cot = jnp.concatenate([rows_of(qkv_cot), rows_of(gate_cot)], axis=1)
    moving.add("side", dot_left(normed_low, side_cot), paired=True)
    (scan_cot,) = moving.step([scan_cot])
    conv_out_cot, step_cot, head_grad = pull_scan(scan_cot)
    (conv_out_cot,) = moving.step([conv_out_cot])
    conv_cot, taps_grad = pull_conv(conv_out_cot)
    conv_cot = rows_of(
        jnp.concatenate(
            [conv_cot, step_cot, jnp.zeros((tokens.shape[0], STEP_LANES - MH), jnp.float32)], axis=1
        )
    )
    (conv_cot,) = moving.step([conv_cot])
    normed_cot = dot_right(side_cot, w_side) + dot_right(conv_cot, w_conv)
    tokens_part, gain_in = pull_norm(normed_cot)
    token_grad = hidden_cot + tokens_part
    gains_grad = jnp.concatenate([gain_in, gain_ff, gain_scan])
    owners = lax.axis_size(axes[1])
    moving.add(
        "conv",
        with_vectors(dot_left(normed_low, conv_cot), gains_grad, taps_grad, head_grad, owners),
    )
    return output, token_grad, moving.finish()


def on_device(
    axes,
    tokens,
    cotangent,
    seq_lengths,
    mixer_in,
    mixer_in_mean,
    mixer_in_square,
    mixer_out,
    mixer_out_mean,
    mixer_out_square,
    swiglu_in,
    swiglu_in_mean,
    swiglu_in_square,
    swiglu_out,
    swiglu_out_mean,
    swiglu_out_square,
    gains,
    gains_mean,
    gains_square,
    conv_kernel,
    conv_kernel_mean,
    conv_kernel_square,
    head_params,
    head_params_mean,
    head_params_square,
):
    weights = gather_weights(axes, mixer_in, mixer_out, swiglu_in, swiglu_out, gains, conv_kernel)
    output, token_grad, sums = forward_backward(
        axes, tokens, cotangent, seq_lengths[0], weights, head_params
    )
    own_gains, own_taps, head_grad = split_vectors(
        sums["conv"], gains.shape[0], conv_kernel.shape[1], head_params.shape
    )
    matrix = jnp.concatenate([sums["side"], sums["conv"][:, : CONV + MH]], axis=1)
    owned = (
        matrix.astype(jnp.float32),
        sums["out"].astype(jnp.float32),
        sums["up"].astype(jnp.float32),
        sums["down"].astype(jnp.float32),
        own_gains,
        own_taps,
    )
    masters = (mixer_in, mixer_out, swiglu_in, swiglu_out, gains, conv_kernel)
    means = (
        mixer_in_mean,
        mixer_out_mean,
        swiglu_in_mean,
        swiglu_out_mean,
        gains_mean,
        conv_kernel_mean,
    )
    squares = (
        mixer_in_square,
        mixer_out_square,
        swiglu_in_square,
        swiglu_out_square,
        gains_square,
        conv_kernel_square,
    )
    rates = (MATRIX_RATE, MATRIX_RATE, MATRIX_RATE, MATRIX_RATE, VECTOR_RATE, VECTOR_RATE)
    updated = [
        adamw(masters[index], means[index], squares[index], owned[index], rates[index])
        for index in range(6)
    ]
    head_new = adamw(head_params, head_params_mean, head_params_square, head_grad, VECTOR_RATE)
    return (
        output,
        token_grad,
        updated[0][0],
        updated[0][1],
        updated[0][2],
        updated[1][0],
        updated[1][1],
        updated[1][2],
        updated[2][0],
        updated[2][1],
        updated[2][2],
        updated[3][0],
        updated[3][1],
        updated[3][2],
        updated[4][0],
        updated[4][1],
        updated[4][2],
        updated[5][0],
        updated[5][1],
        updated[5][2],
        head_new[0],
        head_new[1],
        head_new[2],
    )


def solution(mesh):
    rep, shard = ("rep",), ("shard",)
    if mesh.shape["rep"] == 4 and mesh.shape["shard"] == 8:
        rep, shard = ("x", "core"), ("z", "y")
        mesh = Mesh(mesh.devices.reshape(2, 2, 4, 2), rep + shard)
    rows, owned, across, copied = P(rep + shard, None), P(shard, None), P(None, shard), P()
    optimizer = (owned,) * 12 + (P(shard),) * 3 + (across,) * 3 + (copied,) * 3
    return jax.shard_map(
        functools.partial(on_device, (rep, shard)),
        mesh=mesh,
        in_specs=(rows, rows, rows) + optimizer,
        out_specs=(rows, rows) + optimizer,
        check_vma=False,
    )
```

```python
import functools
import math

import jax
import jax.numpy as jnp
from jax import lax
from jax.experimental import pallas as pl
from jax.experimental.pallas import tpu as pltpu
from jax.sharding import Mesh, PartitionSpec as P

D = 1024
FF = 2048
QUERY_HEADS = 8
KEY_VALUE_HEADS = 2
HEAD_SIZE = 64
MH = 24
MP = 64
NS = 128
KC = 4
STEP = 10


NORM_EPS = 1e-05
ROPE_BASE = 100000000000.0
BETA_MEAN = 0.9
BETA_SQUARE = 0.95
ADAM_EPS = 1e-08
DECAY = 0.1
MATRIX_RATE = 0.03
VECTOR_RATE = 0.5


def make_rounders():

    def round_value(values):
        return lax.optimization_barrier(values.astype(jnp.bfloat16)).astype(jnp.float32)

    def pass_value(values):
        return values

    value_rounder = jax.custom_vjp(round_value)
    grad_rounder = jax.custom_vjp(pass_value)

    def value_keep(values):
        return (round_value(values), None)

    def value_pass(kept, grad):
        return (grad,)

    def grad_keep(values):
        return (values, None)

    def grad_round(kept, grad):
        return (round_value(grad),)

    value_rounder.defvjp(value_keep, value_pass)
    grad_rounder.defvjp(grad_keep, grad_round)
    return (value_rounder, grad_rounder)


def normalize(values, gain):
    return values * lax.rsqrt(jnp.mean(values * values, axis=-1, keepdims=True) + NORM_EPS) * gain


def layout(seq_row, span_length):
    count = seq_row.shape[0]
    ends = jnp.cumsum(seq_row)
    starts = ends - seq_row
    slots = jnp.arange(span_length, dtype=jnp.int32)
    segment = jnp.sum((slots[:, None] >= ends[None, :]).astype(jnp.int32), axis=1)
    valid = slots < ends[count - 1]
    segment = jnp.where(valid, segment, count + slots)
    match = segment[:, None] == jnp.arange(count, dtype=jnp.int32)[None, :]
    first = jnp.sum(jnp.where(match, starts[None, :], 0), axis=1)
    token_position = jnp.where(valid, slots - first, 0)
    return (segment, token_position, valid)


def apply_rotary(values, token_position):
    half = HEAD_SIZE // 2
    freq = ROPE_BASE ** (-(jnp.arange(half, dtype=jnp.float32) * 2.0 / HEAD_SIZE))
    angle = token_position.astype(jnp.float32)[:, None] * freq[None, :]
    cosine = jnp.cos(angle)[:, None, :]
    sine = jnp.sin(angle)[:, None, :]
    first_half = values[..., :half]
    second_half = values[..., half:]
    return jnp.concatenate(
        [first_half * cosine - second_half * sine, second_half * cosine + first_half * sine],
        axis=-1,
    )


def rows_of(matrix):
    return matrix.astype(jnp.bfloat16)


def dot(left, right):
    return jnp.dot(left, right, preferred_element_type=jnp.float32)


def dot_left(left, right):
    return lax.dot_general(left, right, (((0,), (0,)), ((), ())), preferred_element_type=jnp.float32)


def dot_right(left, right):
    return lax.dot_general(left, right, (((1,), (1,)), ((), ())), preferred_element_type=jnp.float32)


def attention(projected, segment, token_position, low, low_back):
    span_length = projected.shape[0]
    key_offset = QUERY_HEADS * HEAD_SIZE
    value_offset = key_offset + KEY_VALUE_HEADS * HEAD_SIZE
    query_matrix = projected[:, :key_offset].reshape(span_length, QUERY_HEADS, HEAD_SIZE)
    key_matrix = projected[:, key_offset:value_offset].reshape(
        span_length, KEY_VALUE_HEADS, HEAD_SIZE
    )
    value_matrix = low(
        projected[:, value_offset:].reshape(span_length, KEY_VALUE_HEADS, HEAD_SIZE)
    )
    query_matrix = low(apply_rotary(query_matrix, token_position)).reshape(
        span_length, KEY_VALUE_HEADS, QUERY_HEADS // KEY_VALUE_HEADS, HEAD_SIZE
    )
    key_matrix = low(apply_rotary(key_matrix, token_position))
    slots = jnp.arange(span_length, dtype=jnp.int32)
    allowed = (segment[:, None] == segment[None, :]) & (slots[None, :] <= slots[:, None])
    scores = jnp.einsum("tagd,sad->agts", query_matrix, key_matrix, precision=None) * HEAD_SIZE ** (
        -0.5
    )
    scores = low_back(scores)
    scores = jnp.where(allowed[None, None], scores, -1000000000.0)
    probs = low(jax.nn.softmax(scores, axis=-1))
    context = low_back(jnp.einsum("agts,sad->tagd", probs, value_matrix, precision=None))
    return low(context.reshape(span_length, QUERY_HEADS * HEAD_SIZE))


def convolution(conv_in, kernel, segment, low):
    span_length = conv_in.shape[0]
    summed = jnp.zeros_like(conv_in) + kernel[KC][None, :]
    for lag in range(KC):
        shifted = jnp.concatenate(
            [jnp.zeros((lag, CONV), jnp.float32), conv_in[: span_length - lag]], axis=0
        )
        earlier = jnp.concatenate(
            [jnp.full((lag,), -1, jnp.int32), segment[: span_length - lag]], axis=0
        )
        keep = earlier == segment
        summed = summed + kernel[KC - 1 - lag][None, :] * jnp.where(keep[:, None], shifted, 0.0)
    return low(jax.nn.silu(summed))


def scan(conv_out, step_raw, head_params, segment, low, low_back):
    span_length = conv_out.shape[0]
    slots = jnp.arange(span_length, dtype=jnp.int32)
    allowed = (segment[:, None] == segment[None, :]) & (slots[None, :] <= slots[:, None])
    scan_x = conv_out[:, : MH * MP].reshape(span_length, MH, MP)
    scan_b = conv_out[:, MH * MP : MH * MP + NS]
    scan_c = conv_out[:, MH * MP + NS :]
    step_size = jax.nn.softplus(step_raw + head_params[0][None, :])
    cumulative = jnp.cumsum(-step_size * jnp.exp(head_params[1])[None, :], axis=0)
    intersection = low_back(jnp.dot(scan_c, scan_b.T, precision=None))
    cum_heads = cumulative.T
    spread = cum_heads[:, :, None] - cum_heads[:, None, :]
    decay_matrix = jnp.exp(jnp.where(allowed[None], spread, -10000.0))
    mixing = low(intersection[None] * decay_matrix * step_size.T[:, None, :])
    scan_out = low_back(jnp.einsum("hts,shp->thp", mixing, scan_x, precision=None))
    scan_out = scan_out + head_params[2][None, :, None] * scan_x
    return scan_out.reshape(span_length, MH * MP)


def gating(scan_out, gate_z, gain, low):
    return low(normalize(scan_out * jax.nn.silu(gate_z), gain))


def activation(gate_up, low):
    return low(jax.nn.silu(gate_up[:, :FF]) * gate_up[:, FF:])


def adamw(weight, mean, square, grad, rate):
    mean_new = BETA_MEAN * mean + (1.0 - BETA_MEAN) * grad
    square_new = BETA_SQUARE * square + (1.0 - BETA_SQUARE) * grad * grad
    corrected = (
        mean_new
        / (1.0 - BETA_MEAN**STEP)
        / (jnp.sqrt(square_new / (1.0 - BETA_SQUARE**STEP)) + ADAM_EPS)
    )
    return (weight - rate * (corrected + DECAY * weight), mean_new, square_new)


QKV = (QUERY_HEADS + 2 * KEY_VALUE_HEADS) * HEAD_SIZE
GATE = MH * MP
CONV = MH * MP + 2 * NS
STEP_LANES = 128
MERGED = (("down", "up"), ("out", "side"))


def general_gather(own, rep, shard):
    part = own
    if rep:
        copies = lax.axis_size(rep)
        rows = own.shape[0] // copies
        part = lax.dynamic_slice_in_dim(own, lax.axis_index(rep) * rows, rows, 0)
    return lax.all_gather(part, shard + rep, axis=0, tiled=True)


def general_reduce(grad, rep, shard):
    piece = lax.psum_scatter(grad, shard + rep, scatter_dimension=0, tiled=True)
    return lax.all_gather(piece, rep, axis=0, tiled=True)


def place():
    return tuple(lax.axis_index(name) for name in ("x", "core", "z", "y"))


def send(values, dx=0, dcore=0, dz=0, dy=0):
    pairs = []
    for x in range(2):
        for core in range(2):
            for z in range(4):
                for y in range(2):
                    start = (x * 2 + core) * 8 + z * 2 + y
                    end = ((x ^ dx) * 2 + (core ^ dcore)) * 8 + ((z + dz) % 4) * 2 + (y ^ dy)
                    pairs.append((start, end))
    return lax.ppermute(values, ("x", "core", "z", "y"), pairs)


def pick(values, index, axis):
    return lax.dynamic_index_in_dim(values, index, axis, keepdims=False)


def fence(values, after):
    def kernel(*refs):
        del refs

    return pl.pallas_call(
        kernel,
        out_shape=[jax.ShapeDtypeStruct(value.shape, value.dtype) for value in values],
        in_specs=[pl.BlockSpec(memory_space=pl.ANY)] * (len(values) + len(after)),
        out_specs=[pl.BlockSpec(memory_space=pl.ANY)] * len(values),
        input_output_aliases={index: index for index in range(len(values))},
        name="fence",
    )(*values, *after)


def assemble(held, rows):
    quarter = rows // 8
    columns = held[0].shape[-1]

    def kernel(*refs):
        sources, target, sems = refs[:8], refs[8], refs[9]
        x, core, z, y = place()
        copies = []
        for other_core in range(2):
            half = core if other_core == 0 else 1 - core
            for other_y in range(2):
                row = y if other_y == 0 else 1 - y
                for turn in range(4):
                    owner = ((z + 4 - turn) % 4) * 2 + row
                    base = owner * rows + half * (rows // 2)
                    main = sources[other_core * 4 + other_y].at[turn]
                    cross = sources[other_core * 4 + 2 + other_y].at[turn]
                    for piece, start, count in (
                        (main.at[pl.ds(0, quarter)], base + x * quarter, quarter),
                        (main.at[pl.ds(quarter, 2 * quarter)], base + 2 * quarter, 2 * quarter),
                        (cross, base + (1 - x) * quarter, quarter),
                    ):
                        place_at = pl.ds(pl.multiple_of(start, 16), count)
                        copies.append(
                            pltpu.make_async_copy(piece, target.at[place_at], sems.at[len(copies)])
                        )
        for copy in copies:
            copy.start()
        for copy in copies:
            copy.wait()

    return pl.pallas_call(
        kernel,
        out_shape=jax.ShapeDtypeStruct((8 * rows, columns), jnp.bfloat16),
        in_specs=[pl.BlockSpec(memory_space=pl.ANY)] * 8,
        out_specs=pl.BlockSpec(memory_space=pltpu.VMEM),
        scratch_shapes=[pltpu.SemaphoreType.DMA((48,))],
        compiler_params=pltpu.CompilerParams(vmem_limit_bytes=24 * 1024 * 1024),
        name="assemble",
    )(*held)


def tuned_gather(pieces):
    x, core, z, y = place()
    results, after, held = [], None, None
    for own in pieces:
        rows = own.shape[0]
        quarter = rows // 8
        half = lax.dynamic_slice_in_dim(own, core * (rows // 2), rows // 2, 0)
        mine = jnp.concatenate(
            [lax.dynamic_slice_in_dim(half, x * quarter, quarter, 0), half[2 * quarter :]], axis=0
        )
        if after is not None:
            mine = fence([mine], after)[0]
        after = [send(mine, dz=turn) for turn in range(1, 4)]
        along_z = jnp.stack([mine] + after)
        across_y = send(along_z, dy=1)
        held = [along_z, across_y]
        held += [send(group[:, :quarter], dx=1) for group in held]
        held += [send(group, dcore=1) for group in held]
        results.append(assemble(held, rows))
    return results, held


def slabs(matrix, width=D):
    blocks = [matrix[..., start : start + width] for start in range(0, matrix.shape[-1], width)]
    return jnp.concatenate(blocks, axis=-2)


def merged_gather(masters):
    x, core, z, y = place()
    parts = []
    for master in masters:
        rows = master.shape[0] // 4
        part = lax.dynamic_slice_in_dim(master, (core * 2 + x) * rows, rows, 0)
        parts.append(slabs(part.astype(jnp.bfloat16)))
    own = jnp.concatenate(parts, axis=0)
    return lax.all_gather(own, ("z", "y", "x"), axis=0, tiled=True)


def merged_place(mine, shapes):
    beside = send(mine, dcore=1)
    total = mine.shape[0] // 16

    def kernel(mine_ref, beside_ref, *refs):
        targets, sems = refs[:-1], refs[-1]
        core = lax.axis_index("core")
        copies = []
        for source, which in ((mine_ref, core), (beside_ref, 1 - core)):
            start = 0
            for target, (rows, columns) in zip(targets, shapes):
                for column in range(0, columns, D):
                    copies.append(
                        pltpu.make_async_copy(
                            source.at[:, :, pl.ds(start, rows)],
                            target.at[:, which, :, :, pl.ds(column, D)],
                            sems.at[len(copies)],
                        )
                    )
                    start += rows
        for copy in copies:
            copy.start()
        for copy in copies:
            copy.wait()

    count = 2 * sum(columns // D for _, columns in shapes)
    placed = pl.pallas_call(
        kernel,
        out_shape=[
            jax.ShapeDtypeStruct((8, 2, 2, rows, columns), jnp.bfloat16) for rows, columns in shapes
        ],
        in_specs=[pl.BlockSpec(memory_space=pl.ANY)] * 2,
        out_specs=[pl.BlockSpec(memory_space=pltpu.VMEM)] * len(shapes),
        scratch_shapes=[pltpu.SemaphoreType.DMA((count,))],
        compiler_params=pltpu.CompilerParams(vmem_limit_bytes=40 * 1024 * 1024),
        name="merged_place",
    )(mine.reshape(8, 2, total, D), beside.reshape(8, 2, total, D))
    return [array.reshape(-1, array.shape[-1]) for array in placed]


def add_low(left, right):
    return (left.astype(jnp.float32) + right.astype(jnp.float32)).astype(jnp.bfloat16)


def tuned_reduce(grad):
    rows, columns = grad.shape[0] // 8, grad.shape[1]
    quarter = rows // 8
    x, core, z, y = place()
    parts = grad.reshape(4, 2, 2, rows // 2, columns)
    far = pick(parts, 1 - core, 2)
    yield [far]
    half = add_low(pick(parts, core, 2), send(far, dcore=1))
    far = lax.dynamic_slice_in_dim(half, (1 - x) * quarter, quarter, 2)
    yield [far]
    near = add_low(lax.dynamic_slice_in_dim(half, x * quarter, quarter, 2), send(far, dx=1))
    both = half[:, :, 2 * quarter :]
    there = jnp.concatenate([pick(near, 1 - y, 1), pick(both, 1 - y, 1)], axis=1)
    here = jnp.concatenate([pick(near, y, 1), pick(both, y, 1)], axis=1)
    yield [there]
    column = add_low(here, send(there, dy=1))
    turns = [pick(column, (z + turn) % 4, 0) for turn in range(1, 4)]
    yield turns
    total = pick(column, z, 0).astype(jnp.float32)
    for turn in range(1, 4):
        total = total + send(turns[turn - 1], dz=turn).astype(jnp.float32)
    total = total.astype(jnp.bfloat16)
    yield [total]
    across = send(total, dx=1)
    own_x, other_x = total[:quarter], across[:quarter]
    owned = jnp.concatenate(
        [
            jnp.where(x == 0, own_x, other_x),
            jnp.where(x == 0, other_x, own_x),
            add_low(total[quarter:], across[quarter:]),
        ],
        axis=0,
    )
    yield [owned]
    beside = send(owned, dcore=1)
    return jnp.concatenate(
        [jnp.where(core == 0, owned, beside), jnp.where(core == 0, beside, owned)], axis=0
    )


def swap_parts(own, late):
    x, core, z, y = place()
    (own,) = fence([own], late)
    across = send(own, dx=1)
    owned = jnp.concatenate(
        [jnp.where(x == 0, own, across), jnp.where(x == 0, across, own)], axis=0
    )
    beside = send(owned, dcore=1)
    return jnp.concatenate(
        [jnp.where(core == 0, owned, beside), jnp.where(core == 0, beside, owned)], axis=0
    )


def quarter_sum(grad):
    rows, columns = grad.shape[0] // 8, grad.shape[1]
    x, core, z, y = place()
    parts = grad.reshape(8, 2, rows // 2, columns)
    far = pick(parts, 1 - core, 1)
    yield [far]
    half = add_low(pick(parts, core, 1), send(far, dcore=1))
    parts = half.reshape(8, 2, rows // 4, columns)
    far = pick(parts, 1 - x, 1)
    yield [far]
    return add_low(pick(parts, x, 1), send(far, dx=1))


def merged_reduce(nears, late):
    width = math.gcd(*(near.shape[-1] for near in nears))
    every = jnp.concatenate([slabs(near, width) for near in nears], axis=1)
    yield [every]
    own = lax.psum_scatter(every.reshape(-1, width), ("z", "y"), scatter_dimension=0, tiled=True)
    yield []
    yield [own]
    yield None
    (own,) = fence([own], late)
    results, start = [], 0
    for near in nears:
        rows, columns = near.shape[1:]
        blocks = []
        for _ in range(0, columns, width):
            blocks.append(own[start : start + rows])
            start += rows
        results.append(swap_parts(jnp.concatenate(blocks, axis=1), late))
    return results


def general_stages(grad, rep, shard):
    yield None
    return general_reduce(grad, rep, shard)


class Reductions:

    def __init__(self, axes):
        self.axes = axes
        self.running, self.results, self.waiting, self.late = {}, {}, {}, []

    def add(self, name, grad, how="chain"):
        grad = grad.astype(jnp.bfloat16)
        if not tuned(self.axes):
            self.running[name] = general_stages(grad, *self.axes)
        elif how == "chain":
            self.running[name] = tuned_reduce(grad)
        else:
            self.running[name] = quarter_sum(grad)

    def step(self, values):
        after = []
        for name in list(self.running):
            if not self.waiting.get(name):
                ready = self.advance(name)
                if ready is None:
                    self.waiting[name] = True
                else:
                    after += ready
        return fence(values, after) if after else values

    def advance(self, name):
        try:
            return next(self.running[name])
        except StopIteration as stop:
            self.results[name] = stop.value
            del self.running[name]
        for group in MERGED:
            if tuned(self.axes) and name in group and all(n in self.results for n in group):
                nears = [self.results.pop(n) for n in group]
                self.running[group] = merged_reduce(nears, self.late)
                return self.advance(group)
        return []

    def finish(self, late):
        self.late += late
        while self.running:
            for name in list(self.running):
                self.advance(name)
        for group in MERGED:
            if group in self.results:
                self.results.update(zip(group, self.results[group]))
        return self.results


def tuned(axes):
    return axes == (("x", "core"), ("z", "y"))


def gather_weights(axes, mixer_in, mixer_out, swiglu_in, swiglu_out, gains, conv_kernel):
    rows = mixer_in.shape[0]
    rep, shard = axes
    owners = lax.axis_size(shard)
    width = conv_kernel.shape[1]
    count = gains.shape[0] + conv_kernel.size
    lanes = -(-count // rows)
    vector = jnp.concatenate([gains, conv_kernel.reshape(-1)])
    vector = jnp.pad(vector, (0, lanes * rows - count)).reshape(rows, lanes)
    low_in = mixer_in.astype(jnp.bfloat16)
    tail = STEP_LANES - MH - lanes
    conv_piece = jnp.concatenate(
        [low_in[:, QKV + GATE :], vector.astype(jnp.bfloat16), jnp.zeros((rows, tail), jnp.bfloat16)],
        axis=1,
    )
    pieces = [conv_piece, low_in[:, : QKV + GATE]]
    if tuned(axes):
        pieces, held = tuned_gather(pieces)
    else:
        pieces = [general_gather(piece, rep, shard) for piece in pieces]
    masters = (mixer_out, swiglu_in, swiglu_out)
    if tuned(axes):
        others = [merged_gather(masters), [(m.shape[0] // 4, m.shape[1]) for m in masters], held]
    else:
        others = [general_gather(master.astype(jnp.bfloat16), rep, shard) for master in masters]
    every = pieces[0][:, CONV + MH : CONV + MH + lanes].reshape(owners, rows * lanes)
    gains_all = every[:, : gains.shape[0]].reshape(-1)
    taps = every[:, gains.shape[0] : count].reshape(owners, KC + 1, width)
    taps = jnp.swapaxes(taps, 0, 1).reshape(KC + 1, owners * width)
    return pieces + [gains_all.astype(jnp.float32), taps.astype(jnp.float32), others]


def with_vectors(conv_g, gains_g, taps_g, head_grad, owners):
    rows = conv_g.shape[0] // owners
    width = taps_g.shape[1] // owners
    vector = jnp.concatenate(
        [
            gains_g.reshape(owners, -1),
            jnp.swapaxes(taps_g.reshape(KC + 1, owners, width), 0, 1).reshape(owners, -1),
            jnp.broadcast_to(head_grad.reshape(1, -1), (owners, head_grad.size)),
        ],
        axis=1,
    )
    count = vector.shape[1]
    lanes = -(-count // rows)
    vector = jnp.pad(vector, ((0, 0), (0, lanes * rows - count))).reshape(owners * rows, lanes)
    vector = jnp.pad(vector, ((0, 0), (MH, STEP_LANES - MH - lanes)))
    return jnp.concatenate([conv_g[:, :CONV], conv_g[:, CONV:] + vector], axis=1)


def split_vectors(conv, own_gains, width, head_shape):
    rows = conv.shape[0]
    count = own_gains + (KC + 1) * width + head_shape[0] * head_shape[1]
    lanes = -(-count // rows)
    used = CONV + MH
    flat = conv[:, used : used + lanes].astype(jnp.float32).reshape(-1)
    taps_end = own_gains + (KC + 1) * width
    return (
        flat[:own_gains],
        flat[own_gains:taps_end].reshape(KC + 1, width),
        flat[taps_end:count].reshape(head_shape),
    )


def forward_backward(axes, tokens, cotangent, seq_row, weights, head_params):
    low, low_back = make_rounders()
    w_conv, w_side, gain_all, taps, others = weights
    segment, token_position, valid = layout(seq_row, tokens.shape[0])
    values = tokens.astype(jnp.float32)
    context_width = QUERY_HEADS * HEAD_SIZE

    normed, pull_norm = jax.vjp(lambda v, g: low(normalize(v, g)), values, gain_all[:D])
    normed_low = rows_of(normed)
    projected = dot(normed_low, w_conv)
    if tuned(axes):
        (projected,) = fence([projected], others[2][:1])
    conv_out, pull_conv = jax.vjp(
        lambda p, k: convolution(p, k, segment, low), projected[:, :CONV], taps
    )
    if tuned(axes):
        (conv_out,) = fence([conv_out], others[2][1:3])
    scan_out, pull_scan = jax.vjp(
        lambda c, r, h: scan(c, r, h, segment, low, low_back),
        conv_out,
        projected[:, CONV : CONV + MH],
        head_params,
    )
    if tuned(axes):
        (scan_out,) = fence([scan_out], others[2][4:])
    beside = dot(normed_low, w_side)
    context, pull_context = jax.vjp(
        lambda p: attention(p, segment, token_position, low, low_back), beside[:, :QKV]
    )
    mamba_out, pull_gating = jax.vjp(
        lambda s, z, g: gating(s, z, g, low), scan_out, beside[:, QKV:], gain_all[2 * D :]
    )
    if tuned(axes):
        (gathered,) = fence([others[0]], [scan_out])
        others = merged_place(gathered, others[1])
    w_out, w_up, w_down = others
    joined = jnp.concatenate([rows_of(context), rows_of(mamba_out)], axis=1)
    hidden = values + dot(joined, w_out)
    normed_ff, pull_ff = jax.vjp(lambda v, g: low(normalize(v, g)), hidden, gain_all[D : 2 * D])
    normed_ff_low = rows_of(normed_ff)
    activated, pull_active = jax.vjp(lambda g: activation(g, low), dot(normed_ff_low, w_up))
    activated_low = rows_of(activated)
    output = (hidden + dot(activated_low, w_down)).astype(jnp.bfloat16)

    moving = Reductions(axes)
    cot = jnp.where(valid[:, None], cotangent, jnp.zeros_like(cotangent))
    (up_cot,) = pull_active(dot_right(cot, w_down))
    up_cot = rows_of(up_cot)
    moving.add("down", dot_left(activated_low, cot), "part")
    (up_cot,) = moving.step([up_cot])
    moving.add("up", dot_left(normed_ff_low, up_cot), "part")
    (ff_cot,) = moving.step([dot_right(up_cot, w_up)])
    hidden_part, gain_ff = pull_ff(ff_cot)
    hidden_cot = cot.astype(jnp.float32) + hidden_part
    hidden_low = rows_of(hidden_cot)
    moving.add("out", dot_left(joined, hidden_low), "part")
    (joined_cot,) = moving.step([dot_right(hidden_low, w_out)])
    scan_cot, gate_cot, gain_scan = pull_gating(joined_cot[:, context_width:])
    (qkv_cot,) = pull_context(joined_cot[:, :context_width])
    side_cot = jnp.concatenate([rows_of(qkv_cot), rows_of(gate_cot)], axis=1)
    moving.add("side", dot_left(normed_low, side_cot), "part")
    (scan_cot,) = moving.step([scan_cot])
    conv_out_cot, step_cot, head_grad = pull_scan(scan_cot)
    (conv_out_cot,) = moving.step([conv_out_cot])
    conv_cot, taps_grad = pull_conv(conv_out_cot)
    conv_cot = rows_of(
        jnp.concatenate(
            [conv_cot, step_cot, jnp.zeros((tokens.shape[0], STEP_LANES - MH), jnp.float32)], axis=1
        )
    )
    (conv_cot,) = moving.step([conv_cot])
    normed_cot = dot_right(side_cot, w_side) + dot_right(conv_cot, w_conv)
    tokens_part, gain_in = pull_norm(normed_cot)
    token_grad = hidden_cot + tokens_part
    gains_grad = jnp.concatenate([gain_in, gain_ff, gain_scan])
    owners = lax.axis_size(axes[1])
    conv_grad = rows_of(
        with_vectors(dot_left(normed_low, conv_cot), gains_grad, taps_grad, head_grad, owners)
    )
    moving.add("conv", conv_grad)
    return output, token_grad, moving.finish([conv_grad])


def on_device(
    axes,
    tokens,
    cotangent,
    seq_lengths,
    mixer_in,
    mixer_in_mean,
    mixer_in_square,
    mixer_out,
    mixer_out_mean,
    mixer_out_square,
    swiglu_in,
    swiglu_in_mean,
    swiglu_in_square,
    swiglu_out,
    swiglu_out_mean,
    swiglu_out_square,
    gains,
    gains_mean,
    gains_square,
    conv_kernel,
    conv_kernel_mean,
    conv_kernel_square,
    head_params,
    head_params_mean,
    head_params_square,
):
    weights = gather_weights(axes, mixer_in, mixer_out, swiglu_in, swiglu_out, gains, conv_kernel)
    output, token_grad, sums = forward_backward(
        axes, tokens, cotangent, seq_lengths[0], weights, head_params
    )
    own_gains, own_taps, head_grad = split_vectors(
        sums["conv"], gains.shape[0], conv_kernel.shape[1], head_params.shape
    )
    matrix = jnp.concatenate([sums["side"], sums["conv"][:, : CONV + MH]], axis=1)
    owned = (
        matrix.astype(jnp.float32),
        sums["out"].astype(jnp.float32),
        sums["up"].astype(jnp.float32),
        sums["down"].astype(jnp.float32),
        own_gains,
        own_taps,
    )
    masters = (mixer_in, mixer_out, swiglu_in, swiglu_out, gains, conv_kernel)
    means = (
        mixer_in_mean,
        mixer_out_mean,
        swiglu_in_mean,
        swiglu_out_mean,
        gains_mean,
        conv_kernel_mean,
    )
    squares = (
        mixer_in_square,
        mixer_out_square,
        swiglu_in_square,
        swiglu_out_square,
        gains_square,
        conv_kernel_square,
    )
    rates = (MATRIX_RATE, MATRIX_RATE, MATRIX_RATE, MATRIX_RATE, VECTOR_RATE, VECTOR_RATE)
    updated = [
        adamw(masters[index], means[index], squares[index], owned[index], rates[index])
        for index in range(6)
    ]
    head_new = adamw(head_params, head_params_mean, head_params_square, head_grad, VECTOR_RATE)
    return (
        output,
        token_grad,
        updated[0][0],
        updated[0][1],
        updated[0][2],
        updated[1][0],
        updated[1][1],
        updated[1][2],
        updated[2][0],
        updated[2][1],
        updated[2][2],
        updated[3][0],
        updated[3][1],
        updated[3][2],
        updated[4][0],
        updated[4][1],
        updated[4][2],
        updated[5][0],
        updated[5][1],
        updated[5][2],
        head_new[0],
        head_new[1],
        head_new[2],
    )


def solution(mesh):
    rep, shard = ("rep",), ("shard",)
    if mesh.shape["rep"] == 4 and mesh.shape["shard"] == 8:
        rep, shard = ("x", "core"), ("z", "y")
        mesh = Mesh(mesh.devices.reshape(2, 2, 4, 2), rep + shard)
    rows, owned, across, copied = P(rep + shard, None), P(shard, None), P(None, shard), P()
    optimizer = (owned,) * 12 + (P(shard),) * 3 + (across,) * 3 + (copied,) * 3
    return jax.shard_map(
        functools.partial(on_device, (rep, shard)),
        mesh=mesh,
        in_specs=(rows, rows, rows) + optimizer,
        out_specs=(rows, rows) + optimizer,
        check_vma=False,
    )
```

```python
import functools

import jax
import jax.numpy as jnp
from jax import lax
from jax.experimental import pallas as pl
from jax.experimental.pallas import tpu as pltpu
from jax.sharding import Mesh, PartitionSpec as P

D = 1024
FF = 2048
QUERY_HEADS = 8
KEY_VALUE_HEADS = 2
HEAD_SIZE = 64
MH = 24
MP = 64
NS = 128
KC = 4
STEP = 10


NORM_EPS = 1e-05
ROPE_BASE = 100000000000.0
BETA_MEAN = 0.9
BETA_SQUARE = 0.95
ADAM_EPS = 1e-08
DECAY = 0.1
MATRIX_RATE = 0.03
VECTOR_RATE = 0.5


def make_rounders():

    def round_value(values):
        return lax.optimization_barrier(values.astype(jnp.bfloat16)).astype(jnp.float32)

    def pass_value(values):
        return values

    value_rounder = jax.custom_vjp(round_value)
    grad_rounder = jax.custom_vjp(pass_value)

    def value_keep(values):
        return (round_value(values), None)

    def value_pass(kept, grad):
        return (grad,)

    def grad_keep(values):
        return (values, None)

    def grad_round(kept, grad):
        return (round_value(grad),)

    value_rounder.defvjp(value_keep, value_pass)
    grad_rounder.defvjp(grad_keep, grad_round)
    return (value_rounder, grad_rounder)


def normalize(values, gain):
    return values * lax.rsqrt(jnp.mean(values * values, axis=-1, keepdims=True) + NORM_EPS) * gain


def layout(seq_row, span_length):
    count = seq_row.shape[0]
    ends = jnp.cumsum(seq_row)
    starts = ends - seq_row
    slots = jnp.arange(span_length, dtype=jnp.int32)
    segment = jnp.sum((slots[:, None] >= ends[None, :]).astype(jnp.int32), axis=1)
    valid = slots < ends[count - 1]
    segment = jnp.where(valid, segment, count + slots)
    match = segment[:, None] == jnp.arange(count, dtype=jnp.int32)[None, :]
    first = jnp.sum(jnp.where(match, starts[None, :], 0), axis=1)
    token_position = jnp.where(valid, slots - first, 0)
    return (segment, token_position, valid)


def apply_rotary(values, token_position):
    half = HEAD_SIZE // 2
    freq = ROPE_BASE ** (-(jnp.arange(half, dtype=jnp.float32) * 2.0 / HEAD_SIZE))
    angle = token_position.astype(jnp.float32)[:, None] * freq[None, :]
    cosine = jnp.cos(angle)[:, None, :]
    sine = jnp.sin(angle)[:, None, :]
    first_half = values[..., :half]
    second_half = values[..., half:]
    return jnp.concatenate(
        [first_half * cosine - second_half * sine, second_half * cosine + first_half * sine],
        axis=-1,
    )


def rows_of(matrix):
    return matrix.astype(jnp.bfloat16)


def dot(left, right):
    return jnp.dot(left, right, preferred_element_type=jnp.float32)


def dot_left(left, right):
    return lax.dot_general(left, right, (((0,), (0,)), ((), ())), preferred_element_type=jnp.float32)


def dot_right(left, right):
    return lax.dot_general(left, right, (((1,), (1,)), ((), ())), preferred_element_type=jnp.float32)


def attention(projected, segment, token_position, low, low_back):
    span_length = projected.shape[0]
    key_offset = QUERY_HEADS * HEAD_SIZE
    value_offset = key_offset + KEY_VALUE_HEADS * HEAD_SIZE
    query_matrix = projected[:, :key_offset].reshape(span_length, QUERY_HEADS, HEAD_SIZE)
    key_matrix = projected[:, key_offset:value_offset].reshape(
        span_length, KEY_VALUE_HEADS, HEAD_SIZE
    )
    value_matrix = low(
        projected[:, value_offset:].reshape(span_length, KEY_VALUE_HEADS, HEAD_SIZE)
    )
    query_matrix = low(apply_rotary(query_matrix, token_position)).reshape(
        span_length, KEY_VALUE_HEADS, QUERY_HEADS // KEY_VALUE_HEADS, HEAD_SIZE
    )
    key_matrix = low(apply_rotary(key_matrix, token_position))
    slots = jnp.arange(span_length, dtype=jnp.int32)
    allowed = (segment[:, None] == segment[None, :]) & (slots[None, :] <= slots[:, None])
    scores = jnp.einsum("tagd,sad->agts", query_matrix, key_matrix, precision=None) * HEAD_SIZE ** (
        -0.5
    )
    scores = low_back(scores)
    scores = jnp.where(allowed[None, None], scores, -1000000000.0)
    probs = low(jax.nn.softmax(scores, axis=-1))
    context = low_back(jnp.einsum("agts,sad->tagd", probs, value_matrix, precision=None))
    return low(context.reshape(span_length, QUERY_HEADS * HEAD_SIZE))


def convolution(conv_in, kernel, segment, low):
    span_length = conv_in.shape[0]
    summed = jnp.zeros_like(conv_in) + kernel[KC][None, :]
    for lag in range(KC):
        shifted = jnp.concatenate(
            [jnp.zeros((lag, CONV), jnp.float32), conv_in[: span_length - lag]], axis=0
        )
        earlier = jnp.concatenate(
            [jnp.full((lag,), -1, jnp.int32), segment[: span_length - lag]], axis=0
        )
        keep = earlier == segment
        summed = summed + kernel[KC - 1 - lag][None, :] * jnp.where(keep[:, None], shifted, 0.0)
    return low(jax.nn.silu(summed))


TILE = 128


def mixing_tables(b_ref, c_ref, row_segment, column_segment, table, bias, transposed):
    left, right = (b_ref, c_ref) if transposed else (c_ref, b_ref)
    table[...] = dot_right(left[...], right[...])
    shape = table.shape
    first = lax.broadcasted_iota(jnp.int32, shape, 0)
    second = lax.broadcasted_iota(jnp.int32, shape, 1)
    order = (first <= second) if transposed else (second <= first)
    allowed = order & (column_segment[...] == row_segment[...])
    bias[...] = jnp.where(allowed, 0.0, -1e30)


def scan_forward_kernel(
    x_ref, b_ref, c_ref, cum_col, cum_row, step_row, skip, row_segment, column_segment,
    out_ref, table, bias,
):
    @pl.when(pl.program_id(0) == 0)
    def _():
        mixing_tables(b_ref, c_ref, row_segment, column_segment, table, bias, False)

    for start in range(0, x_ref.shape[0], TILE):
        rows, width = pl.ds(start, TILE), start + TILE
        halves = []
        for head in range(2):
            spread = cum_col[0, rows, head : head + 1] - cum_row[0, head : head + 1, :width]
            decay = jnp.exp(spread + bias[rows, :width])
            mixing = table[rows, :width] * decay * step_row[0, head : head + 1, :width]
            halves.append(dot(mixing.astype(jnp.bfloat16), x_ref[:width, :]))
        first = lax.broadcasted_iota(jnp.int32, (TILE, 2 * MP), 1) < MP
        out_ref[rows, :] = jnp.where(first, halves[0], halves[1]) + skip[...] * x_ref[
            rows, :
        ].astype(jnp.float32)


def scan_backward_kernel(
    cot_ref, out_ref, x_ref, b_ref, c_ref, cum_col, cum_row, step_col, skip,
    row_segment, column_segment, dx_ref, dcum_ref, dstep_ref, dskip_ref, dtable_ref,
    table, bias, dtable,
):
    @pl.when(pl.program_id(0) == 0)
    def _():
        mixing_tables(b_ref, c_ref, row_segment, column_segment, table, bias, True)
        dtable[...] = jnp.zeros_like(dtable)

    span = x_ref.shape[0]
    cot = cot_ref[...]
    cot_low = cot.astype(jnp.bfloat16)
    dskip_ref[...] = jnp.sum(cot * x_ref[...].astype(jnp.float32), axis=0, keepdims=True)
    for start in range(0, span, TILE):
        rows, later = pl.ds(start, TILE), pl.ds(start, span - start)
        first = lax.broadcasted_iota(jnp.int32, (TILE, 2 * MP), 1) < MP
        x_tile = x_ref[rows, :]
        halves = []
        for head in range(2):
            spread = cum_row[0, head : head + 1, start:] - cum_col[0, rows, head : head + 1]
            scaled = jnp.exp(spread + bias[rows, later]) * step_col[0, rows, head : head + 1]
            mixing = table[rows, later] * scaled
            mine = first if head == 0 else jnp.logical_not(first)
            x_head = jnp.where(mine, x_tile, jnp.zeros_like(x_tile))
            dtable[rows, later] += dot_right(x_head, cot_low[start:, :]) * scaled
            halves.append(dot(mixing.astype(jnp.bfloat16), cot_low[start:, :]))
        part = jnp.where(first, halves[0], halves[1])
        x_wide = x_tile.astype(jnp.float32)
        dx_ref[rows, :] = part + skip[...] * cot[start : start + TILE, :]
        into = x_wide * part
        product = out_ref[rows, :] - skip[...] * x_wide
        across = cot_low[start : start + TILE, :].astype(jnp.float32) * product - into
        for head in range(2):
            mine = first if head == 0 else jnp.logical_not(first)
            dcum_ref[0, rows, head : head + 1] = jnp.sum(
                jnp.where(mine, across, 0.0), axis=1, keepdims=True
            )
            dstep_ref[0, rows, head : head + 1] = jnp.sum(
                jnp.where(mine, into, 0.0), axis=1, keepdims=True
            )

    @pl.when(pl.program_id(0) == pl.num_programs(0) - 1)
    def _():
        dtable_ref[...] = dtable[...].astype(jnp.bfloat16)


def decay_steps(step_raw, head_params):
    step_size = jax.nn.softplus(step_raw + head_params[0][None, :])
    return step_size, jnp.cumsum(-step_size * jnp.exp(head_params[1])[None, :], axis=0)


def pair_columns(values):
    return jnp.swapaxes(values.reshape(values.shape[0], MH // 2, 2), 0, 1)


def scan_operands(conv_low, step_size, cumulative, head_params, segment):
    span = conv_low.shape[0]
    pair = pl.BlockSpec((span, 2 * MP), lambda i: (0, i))
    column = pl.BlockSpec((1, span, 2), lambda i: (i, 0, 0))
    row = pl.BlockSpec((1, 2, span), lambda i: (i, 0, 0))
    lanes = pl.BlockSpec((1, 2 * MP), lambda i: (0, i))
    b_spec = pl.BlockSpec((span, NS), lambda i: (0, MH // 2))
    c_spec = pl.BlockSpec((span, NS), lambda i: (0, MH // 2 + 1))
    row_segment = pl.BlockSpec((1, span), lambda i: (0, 0))
    column_segment = pl.BlockSpec((span, 1), lambda i: (0, 0))
    arrays = {
        "x": (conv_low, pair),
        "b": (conv_low, b_spec),
        "c": (conv_low, c_spec),
        "cum_col": (pair_columns(cumulative), column),
        "cum_row": (cumulative.T.reshape(MH // 2, 2, span), row),
        "step_col": (pair_columns(step_size), column),
        "step_row": (step_size.T.reshape(MH // 2, 2, span), row),
        "skip": (jnp.repeat(head_params[2], MP)[None, :], lanes),
        "row_segment": (segment[None, :], row_segment),
        "column_segment": (segment[:, None], column_segment),
    }
    return arrays, pair, column, lanes


def scan_forward(conv_low, step_size, cumulative, head_params, segment):
    span = conv_low.shape[0]
    arrays, pair, _, _ = scan_operands(conv_low, step_size, cumulative, head_params, segment)
    names = "x b c cum_col cum_row step_row skip row_segment column_segment".split()
    return pl.pallas_call(
        scan_forward_kernel,
        grid=(MH // 2,),
        out_shape=jax.ShapeDtypeStruct((span, MH * MP), jnp.float32),
        in_specs=[arrays[name][1] for name in names],
        out_specs=pair,
        scratch_shapes=[pltpu.VMEM((span, span), jnp.float32)] * 2,
        compiler_params=pltpu.CompilerParams(vmem_limit_bytes=32 * 1024 * 1024),
        name="scan_forward",
    )(*(arrays[name][0] for name in names))


def scan_backward(cot, out, conv_low, step_size, cumulative, head_params, segment):
    span = conv_low.shape[0]
    arrays, pair, column, lanes = scan_operands(
        conv_low, step_size, cumulative, head_params, segment
    )
    names = "x b c cum_col cum_row step_col skip row_segment column_segment".split()
    dx, dcum, dstep, dskip, dtable = pl.pallas_call(
        scan_backward_kernel,
        grid=(MH // 2,),
        out_shape=[
            jax.ShapeDtypeStruct((span, MH * MP), jnp.float32),
            jax.ShapeDtypeStruct((MH // 2, span, 2), jnp.float32),
            jax.ShapeDtypeStruct((MH // 2, span, 2), jnp.float32),
            jax.ShapeDtypeStruct((1, MH * MP), jnp.float32),
            jax.ShapeDtypeStruct((span, span), jnp.bfloat16),
        ],
        in_specs=[pair, pair] + [arrays[name][1] for name in names],
        out_specs=[pair, column, column, lanes, pl.BlockSpec((span, span), lambda i: (0, 0))],
        scratch_shapes=[pltpu.VMEM((span, span), jnp.float32)] * 3,
        compiler_params=pltpu.CompilerParams(vmem_limit_bytes=32 * 1024 * 1024),
        name="scan_backward",
    )(cot, out, *(arrays[name][0] for name in names))
    scan_b = conv_low[:, MH * MP : MH * MP + NS]
    scan_c = conv_low[:, MH * MP + NS :]
    conv_cot = jnp.concatenate([dx, dot(dtable, scan_c), dot_left(dtable, scan_b)], axis=1)
    dcum = jnp.swapaxes(dcum, 0, 1).reshape(span, MH)
    dstep = jnp.swapaxes(dstep, 0, 1).reshape(span, MH)
    dstep = jnp.where(step_size > 1e-30, dstep / jnp.maximum(step_size, 1e-30), 0.0)
    return conv_cot, dstep, dcum, jnp.sum(dskip.reshape(MH, MP), axis=1)


def gating(scan_out, gate_z, gain, low):
    return low(normalize(scan_out * jax.nn.silu(gate_z), gain))


def activation(gate_up, low):
    return low(jax.nn.silu(gate_up[:, :FF]) * gate_up[:, FF:])


def adamw(weight, mean, square, grad, rate):
    mean_new = BETA_MEAN * mean + (1.0 - BETA_MEAN) * grad
    square_new = BETA_SQUARE * square + (1.0 - BETA_SQUARE) * grad * grad
    corrected = (
        mean_new
        / (1.0 - BETA_MEAN**STEP)
        / (jnp.sqrt(square_new / (1.0 - BETA_SQUARE**STEP)) + ADAM_EPS)
    )
    return (weight - rate * (corrected + DECAY * weight), mean_new, square_new)


QKV = (QUERY_HEADS + 2 * KEY_VALUE_HEADS) * HEAD_SIZE
GATE = MH * MP
CONV = MH * MP + 2 * NS
STEP_LANES = 128


def general_gather(own, rep, shard):
    part = own
    if rep:
        copies = lax.axis_size(rep)
        rows = own.shape[0] // copies
        part = lax.dynamic_slice_in_dim(own, lax.axis_index(rep) * rows, rows, 0)
    return lax.all_gather(part, shard + rep, axis=0, tiled=True)


def general_reduce(grad, rep, shard):
    piece = lax.psum_scatter(grad, shard + rep, scatter_dimension=0, tiled=True)
    return lax.all_gather(piece, rep, axis=0, tiled=True)


def place():
    return tuple(lax.axis_index(name) for name in ("x", "core", "z", "y"))


def send(values, dx=0, dcore=0, dz=0, dy=0):
    pairs = []
    for x in range(2):
        for core in range(2):
            for z in range(4):
                for y in range(2):
                    start = (x * 2 + core) * 8 + z * 2 + y
                    end = ((x ^ dx) * 2 + (core ^ dcore)) * 8 + ((z + dz) % 4) * 2 + (y ^ dy)
                    pairs.append((start, end))
    return lax.ppermute(values, ("x", "core", "z", "y"), pairs)


def pick(values, index, axis):
    return lax.dynamic_index_in_dim(values, index, axis, keepdims=False)


def fence(values, after):
    def kernel(*refs):
        del refs

    return pl.pallas_call(
        kernel,
        out_shape=[jax.ShapeDtypeStruct(value.shape, value.dtype) for value in values],
        in_specs=[pl.BlockSpec(memory_space=pl.ANY)] * (len(values) + len(after)),
        out_specs=[pl.BlockSpec(memory_space=pl.ANY)] * len(values),
        input_output_aliases={index: index for index in range(len(values))},
        name="fence",
    )(*values, *after)


def assemble(held, rows):
    quarter = rows // 8
    columns = held[0].shape[-1]

    def kernel(*refs):
        sources, target, sems = refs[:8], refs[8], refs[9]
        x, core, z, y = place()
        copies = []
        for other_core in range(2):
            half = core if other_core == 0 else 1 - core
            for other_y in range(2):
                row = y if other_y == 0 else 1 - y
                for turn in range(4):
                    owner = ((z + 4 - turn) % 4) * 2 + row
                    base = owner * rows + half * (rows // 2)
                    main = sources[other_core * 4 + other_y].at[turn]
                    cross = sources[other_core * 4 + 2 + other_y].at[turn]
                    for piece, start, count in (
                        (main.at[pl.ds(0, quarter)], base + x * quarter, quarter),
                        (main.at[pl.ds(quarter, 2 * quarter)], base + 2 * quarter, 2 * quarter),
                        (cross, base + (1 - x) * quarter, quarter),
                    ):
                        place_at = pl.ds(pl.multiple_of(start, 16), count)
                        copies.append(
                            pltpu.make_async_copy(piece, target.at[place_at], sems.at[len(copies)])
                        )
        for copy in copies:
            copy.start()
        for copy in copies:
            copy.wait()

    return pl.pallas_call(
        kernel,
        out_shape=jax.ShapeDtypeStruct((8 * rows, columns), jnp.bfloat16),
        in_specs=[pl.BlockSpec(memory_space=pl.ANY)] * 8,
        out_specs=pl.BlockSpec(memory_space=pltpu.VMEM),
        scratch_shapes=[pltpu.SemaphoreType.DMA((48,))],
        compiler_params=pltpu.CompilerParams(vmem_limit_bytes=24 * 1024 * 1024),
        name="assemble",
    )(*held)


def tuned_gather(pieces):
    x, core, z, y = place()
    results, after = [], None
    for own in pieces:
        rows = own.shape[0]
        quarter = rows // 8
        half = lax.dynamic_slice_in_dim(own, core * (rows // 2), rows // 2, 0)
        mine = jnp.concatenate(
            [lax.dynamic_slice_in_dim(half, x * quarter, quarter, 0), half[2 * quarter :]], axis=0
        )
        if after is not None:
            mine = fence([mine], after)[0]
        after = [send(mine, dz=turn) for turn in range(1, 4)]
        along_z = jnp.stack([mine] + after)
        across_y = send(along_z, dy=1)
        held = [along_z, across_y]
        held += [send(group[:, :quarter], dx=1) for group in held]
        held += [send(group, dcore=1) for group in held]
        results.append(assemble(held, rows))
    return results


def add_low(left, right):
    return (left.astype(jnp.float32) + right.astype(jnp.float32)).astype(jnp.bfloat16)


def tuned_reduce(grad):
    rows, columns = grad.shape[0] // 8, grad.shape[1]
    quarter = rows // 8
    x, core, z, y = place()
    parts = grad.reshape(4, 2, 2, rows // 2, columns)
    far = pick(parts, 1 - core, 2)
    yield [far]
    half = add_low(pick(parts, core, 2), send(far, dcore=1))
    far = lax.dynamic_slice_in_dim(half, (1 - x) * quarter, quarter, 2)
    yield [far]
    near = add_low(lax.dynamic_slice_in_dim(half, x * quarter, quarter, 2), send(far, dx=1))
    both = half[:, :, 2 * quarter :]
    there = jnp.concatenate([pick(near, 1 - y, 1), pick(both, 1 - y, 1)], axis=1)
    here = jnp.concatenate([pick(near, y, 1), pick(both, y, 1)], axis=1)
    yield [there]
    column = add_low(here, send(there, dy=1))
    turns = [pick(column, (z + turn) % 4, 0) for turn in range(1, 4)]
    yield turns
    total = pick(column, z, 0).astype(jnp.float32)
    for turn in range(1, 4):
        total = total + send(turns[turn - 1], dz=turn).astype(jnp.float32)
    total = total.astype(jnp.bfloat16)
    yield [total]
    across = send(total, dx=1)
    own_x, other_x = total[:quarter], across[:quarter]
    owned = jnp.concatenate(
        [
            jnp.where(x == 0, own_x, other_x),
            jnp.where(x == 0, other_x, own_x),
            add_low(total[quarter:], across[quarter:]),
        ],
        axis=0,
    )
    yield [owned]
    beside = send(owned, dcore=1)
    return jnp.concatenate(
        [jnp.where(core == 0, owned, beside), jnp.where(core == 0, beside, owned)], axis=0
    )


def paired_reduce(grad):
    rows, columns = grad.shape[0] // 8, grad.shape[1]
    x, core, z, y = place()
    parts = grad.reshape(8, 2, rows // 2, columns)
    far = pick(parts, 1 - core, 1)
    yield [far]
    half = add_low(pick(parts, core, 1), send(far, dcore=1)).reshape(4 * rows, columns)
    yield [half]
    own = lax.psum_scatter(half, ("z", "y", "x"), scatter_dimension=0, tiled=True)
    yield None
    across = send(own, dx=1)
    owned = jnp.concatenate(
        [jnp.where(x == 0, own, across), jnp.where(x == 0, across, own)], axis=0
    )
    yield None
    beside = send(owned, dcore=1)
    return jnp.concatenate(
        [jnp.where(core == 0, owned, beside), jnp.where(core == 0, beside, owned)], axis=0
    )


def general_stages(grad, rep, shard):
    yield None
    return general_reduce(grad, rep, shard)


class Reductions:

    def __init__(self, axes):
        self.axes = axes
        self.running, self.results, self.waiting = {}, {}, {}

    def add(self, name, grad, paired=False):
        grad = grad.astype(jnp.bfloat16)
        if not tuned(self.axes):
            self.running[name] = general_stages(grad, *self.axes)
        elif paired:
            self.running[name] = paired_reduce(grad)
        else:
            self.running[name] = tuned_reduce(grad)

    def step(self, values):
        after = []
        for name in list(self.running):
            if self.waiting.get(name):
                continue
            ready = self.advance(name)
            if ready is None:
                self.waiting[name] = True
            else:
                after += ready
        return fence(values, after) if after else values

    def advance(self, name):
        try:
            return next(self.running[name])
        except StopIteration as stop:
            self.results[name] = stop.value
            del self.running[name]
            return []

    def finish(self):
        while self.running:
            for name in list(self.running):
                self.advance(name)
        return self.results


def tuned(axes):
    return axes == (("x", "core"), ("z", "y"))


def gather_weights(axes, mixer_in, mixer_out, swiglu_in, swiglu_out, gains, conv_kernel):
    rows = mixer_in.shape[0]
    rep, shard = axes
    owners = lax.axis_size(shard)
    width = conv_kernel.shape[1]
    count = gains.shape[0] + conv_kernel.size
    lanes = -(-count // rows)
    vector = jnp.concatenate([gains, conv_kernel.reshape(-1)])
    vector = jnp.pad(vector, (0, lanes * rows - count)).reshape(rows, lanes)
    low_in = mixer_in.astype(jnp.bfloat16)
    tail = STEP_LANES - MH - lanes
    conv_piece = jnp.concatenate(
        [low_in[:, QKV + GATE :], vector.astype(jnp.bfloat16), jnp.zeros((rows, tail), jnp.bfloat16)],
        axis=1,
    )
    pieces = [conv_piece, low_in[:, : QKV + GATE]]
    if tuned(axes):
        pieces = tuned_gather(pieces)
    else:
        pieces = [general_gather(piece, rep, shard) for piece in pieces]
    for master in (mixer_out, swiglu_in, swiglu_out):
        pieces.append(general_gather(master.astype(jnp.bfloat16), rep, shard))
    every = pieces[0][:, CONV + MH : CONV + MH + lanes].reshape(owners, rows * lanes)
    gains_all = every[:, : gains.shape[0]].reshape(-1)
    taps = every[:, gains.shape[0] : count].reshape(owners, KC + 1, width)
    taps = jnp.swapaxes(taps, 0, 1).reshape(KC + 1, owners * width)
    return pieces + [gains_all.astype(jnp.float32), taps.astype(jnp.float32)]


def with_vectors(conv_g, gains_g, taps_g, head_grad, owners):
    rows = conv_g.shape[0] // owners
    width = taps_g.shape[1] // owners
    vector = jnp.concatenate(
        [
            gains_g.reshape(owners, -1),
            jnp.swapaxes(taps_g.reshape(KC + 1, owners, width), 0, 1).reshape(owners, -1),
            jnp.broadcast_to(head_grad.reshape(1, -1), (owners, head_grad.size)),
        ],
        axis=1,
    )
    count = vector.shape[1]
    lanes = -(-count // rows)
    vector = jnp.pad(vector, ((0, 0), (0, lanes * rows - count))).reshape(owners * rows, lanes)
    vector = jnp.pad(vector, ((0, 0), (MH, STEP_LANES - MH - lanes)))
    return jnp.concatenate([conv_g[:, :CONV], conv_g[:, CONV:] + vector], axis=1)


def split_vectors(conv, own_gains, width, head_shape):
    rows = conv.shape[0]
    count = own_gains + (KC + 1) * width + head_shape[0] * head_shape[1]
    lanes = -(-count // rows)
    used = CONV + MH
    flat = conv[:, used : used + lanes].astype(jnp.float32).reshape(-1)
    taps_end = own_gains + (KC + 1) * width
    return (
        flat[:own_gains],
        flat[own_gains:taps_end].reshape(KC + 1, width),
        flat[taps_end:count].reshape(head_shape),
    )


def forward_backward(axes, tokens, cotangent, seq_row, weights, head_params):
    low, low_back = make_rounders()
    w_conv, w_side, w_out, w_up, w_down, gain_all, taps = weights
    segment, token_position, valid = layout(seq_row, tokens.shape[0])
    values = tokens.astype(jnp.float32)
    context_width = QUERY_HEADS * HEAD_SIZE

    normed, pull_norm = jax.vjp(lambda v, g: low(normalize(v, g)), values, gain_all[:D])
    normed_low = rows_of(normed)
    projected = dot(normed_low, w_conv)
    conv_out, pull_conv = jax.vjp(
        lambda p, k: convolution(p, k, segment, low), projected[:, :CONV], taps
    )
    conv_low = rows_of(conv_out)
    (step_size, cumulative), pull_steps = jax.vjp(
        decay_steps, projected[:, CONV : CONV + MH], head_params
    )
    scan_out = scan_forward(conv_low, step_size, cumulative, head_params, segment)
    beside = dot(normed_low, w_side)
    context, pull_context = jax.vjp(
        lambda p: attention(p, segment, token_position, low, low_back), beside[:, :QKV]
    )
    mamba_out, pull_gating = jax.vjp(
        lambda s, z, g: gating(s, z, g, low), scan_out, beside[:, QKV:], gain_all[2 * D :]
    )
    joined = jnp.concatenate([rows_of(context), rows_of(mamba_out)], axis=1)
    hidden = values + dot(joined, w_out)
    normed_ff, pull_ff = jax.vjp(lambda v, g: low(normalize(v, g)), hidden, gain_all[D : 2 * D])
    normed_ff_low = rows_of(normed_ff)
    activated, pull_active = jax.vjp(lambda g: activation(g, low), dot(normed_ff_low, w_up))
    activated_low = rows_of(activated)
    output = (hidden + dot(activated_low, w_down)).astype(jnp.bfloat16)

    moving = Reductions(axes)
    cot = jnp.where(valid[:, None], cotangent, jnp.zeros_like(cotangent))
    (up_cot,) = pull_active(dot_right(cot, w_down))
    up_cot = rows_of(up_cot)
    moving.add("down", dot_left(activated_low, cot), paired=True)
    (up_cot,) = moving.step([up_cot])
    moving.add("up", dot_left(normed_ff_low, up_cot), paired=True)
    (ff_cot,) = moving.step([dot_right(up_cot, w_up)])
    hidden_part, gain_ff = pull_ff(ff_cot)
    hidden_cot = cot.astype(jnp.float32) + hidden_part
    hidden_low = rows_of(hidden_cot)
    moving.add("out", dot_left(joined, hidden_low))
    (joined_cot,) = moving.step([dot_right(hidden_low, w_out)])
    scan_cot, gate_cot, gain_scan = pull_gating(joined_cot[:, context_width:])
    (qkv_cot,) = pull_context(joined_cot[:, :context_width])
    side_cot = jnp.concatenate([rows_of(qkv_cot), rows_of(gate_cot)], axis=1)
    moving.add("side", dot_left(normed_low, side_cot), paired=True)
    (scan_cot,) = moving.step([scan_cot])
    conv_out_cot, dstep, dcum, dskip = scan_backward(
        scan_cot, scan_out, conv_low, step_size, cumulative, head_params, segment
    )
    step_cot, head_grad = pull_steps((dstep, dcum))
    head_grad = head_grad.at[2].add(dskip)
    (conv_out_cot,) = moving.step([conv_out_cot])
    conv_cot, taps_grad = pull_conv(conv_out_cot)
    conv_cot = rows_of(
        jnp.concatenate(
            [conv_cot, step_cot, jnp.zeros((tokens.shape[0], STEP_LANES - MH), jnp.float32)], axis=1
        )
    )
    (conv_cot,) = moving.step([conv_cot])
    normed_cot = dot_right(side_cot, w_side) + dot_right(conv_cot, w_conv)
    tokens_part, gain_in = pull_norm(normed_cot)
    token_grad = hidden_cot + tokens_part
    gains_grad = jnp.concatenate([gain_in, gain_ff, gain_scan])
    owners = lax.axis_size(axes[1])
    moving.add(
        "conv",
        with_vectors(dot_left(normed_low, conv_cot), gains_grad, taps_grad, head_grad, owners),
    )
    return output, token_grad, moving.finish()


def on_device(
    axes,
    tokens,
    cotangent,
    seq_lengths,
    mixer_in,
    mixer_in_mean,
    mixer_in_square,
    mixer_out,
    mixer_out_mean,
    mixer_out_square,
    swiglu_in,
    swiglu_in_mean,
    swiglu_in_square,
    swiglu_out,
    swiglu_out_mean,
    swiglu_out_square,
    gains,
    gains_mean,
    gains_square,
    conv_kernel,
    conv_kernel_mean,
    conv_kernel_square,
    head_params,
    head_params_mean,
    head_params_square,
):
    weights = gather_weights(axes, mixer_in, mixer_out, swiglu_in, swiglu_out, gains, conv_kernel)
    output, token_grad, sums = forward_backward(
        axes, tokens, cotangent, seq_lengths[0], weights, head_params
    )
    own_gains, own_taps, head_grad = split_vectors(
        sums["conv"], gains.shape[0], conv_kernel.shape[1], head_params.shape
    )
    matrix = jnp.concatenate([sums["side"], sums["conv"][:, : CONV + MH]], axis=1)
    owned = (
        matrix.astype(jnp.float32),
        sums["out"].astype(jnp.float32),
        sums["up"].astype(jnp.float32),
        sums["down"].astype(jnp.float32),
        own_gains,
        own_taps,
    )
    masters = (mixer_in, mixer_out, swiglu_in, swiglu_out, gains, conv_kernel)
    means = (
        mixer_in_mean,
        mixer_out_mean,
        swiglu_in_mean,
        swiglu_out_mean,
        gains_mean,
        conv_kernel_mean,
    )
    squares = (
        mixer_in_square,
        mixer_out_square,
        swiglu_in_square,
        swiglu_out_square,
        gains_square,
        conv_kernel_square,
    )
    rates = (MATRIX_RATE, MATRIX_RATE, MATRIX_RATE, MATRIX_RATE, VECTOR_RATE, VECTOR_RATE)
    updated = [
        adamw(masters[index], means[index], squares[index], owned[index], rates[index])
        for index in range(6)
    ]
    head_new = adamw(head_params, head_params_mean, head_params_square, head_grad, VECTOR_RATE)
    return (
        output,
        token_grad,
        updated[0][0],
        updated[0][1],
        updated[0][2],
        updated[1][0],
        updated[1][1],
        updated[1][2],
        updated[2][0],
        updated[2][1],
        updated[2][2],
        updated[3][0],
        updated[3][1],
        updated[3][2],
        updated[4][0],
        updated[4][1],
        updated[4][2],
        updated[5][0],
        updated[5][1],
        updated[5][2],
        head_new[0],
        head_new[1],
        head_new[2],
    )


def solution(mesh):
    rep, shard = ("rep",), ("shard",)
    if mesh.shape["rep"] == 4 and mesh.shape["shard"] == 8:
        rep, shard = ("x", "core"), ("z", "y")
        mesh = Mesh(mesh.devices.reshape(2, 2, 4, 2), rep + shard)
    rows, owned, across, copied = P(rep + shard, None), P(shard, None), P(None, shard), P()
    optimizer = (owned,) * 12 + (P(shard),) * 3 + (across,) * 3 + (copied,) * 3
    return jax.shard_map(
        functools.partial(on_device, (rep, shard)),
        mesh=mesh,
        in_specs=(rows, rows, rows) + optimizer,
        out_specs=(rows, rows) + optimizer,
        check_vma=False,
    )
```

```python
import functools

import jax
import jax.numpy as jnp
from jax import lax
from jax.experimental import pallas as pl
from jax.experimental.pallas import tpu as pltpu
from jax.sharding import Mesh, PartitionSpec as P

D = 1024
FF = 2048
QUERY_HEADS = 8
KEY_VALUE_HEADS = 2
HEAD_SIZE = 64
MH = 24
MP = 64
NS = 128
KC = 4
STEP = 10


NORM_EPS = 1e-05
ROPE_BASE = 100000000000.0
BETA_MEAN = 0.9
BETA_SQUARE = 0.95
ADAM_EPS = 1e-08
DECAY = 0.1
MATRIX_RATE = 0.03
VECTOR_RATE = 0.5


def make_rounders():

    def round_value(values):
        return lax.optimization_barrier(values.astype(jnp.bfloat16)).astype(jnp.float32)

    def pass_value(values):
        return values

    value_rounder = jax.custom_vjp(round_value)
    grad_rounder = jax.custom_vjp(pass_value)

    def value_keep(values):
        return (round_value(values), None)

    def value_pass(kept, grad):
        return (grad,)

    def grad_keep(values):
        return (values, None)

    def grad_round(kept, grad):
        return (round_value(grad),)

    value_rounder.defvjp(value_keep, value_pass)
    grad_rounder.defvjp(grad_keep, grad_round)
    return (value_rounder, grad_rounder)


def normalize(values, gain):
    return values * lax.rsqrt(jnp.mean(values * values, axis=-1, keepdims=True) + NORM_EPS) * gain


def layout(seq_row, span_length):
    count = seq_row.shape[0]
    ends = jnp.cumsum(seq_row)
    starts = ends - seq_row
    slots = jnp.arange(span_length, dtype=jnp.int32)
    segment = jnp.sum((slots[:, None] >= ends[None, :]).astype(jnp.int32), axis=1)
    valid = slots < ends[count - 1]
    segment = jnp.where(valid, segment, count + slots)
    match = segment[:, None] == jnp.arange(count, dtype=jnp.int32)[None, :]
    first = jnp.sum(jnp.where(match, starts[None, :], 0), axis=1)
    token_position = jnp.where(valid, slots - first, 0)
    return (segment, token_position, valid)


def apply_rotary(values, token_position):
    half = HEAD_SIZE // 2
    freq = ROPE_BASE ** (-(jnp.arange(half, dtype=jnp.float32) * 2.0 / HEAD_SIZE))
    angle = token_position.astype(jnp.float32)[:, None] * freq[None, :]
    cosine = jnp.cos(angle)[:, None, :]
    sine = jnp.sin(angle)[:, None, :]
    first_half = values[..., :half]
    second_half = values[..., half:]
    return jnp.concatenate(
        [first_half * cosine - second_half * sine, second_half * cosine + first_half * sine],
        axis=-1,
    )


def rows_of(matrix):
    return matrix.astype(jnp.bfloat16)


def dot(left, right):
    return jnp.dot(left, right, preferred_element_type=jnp.float32)


def dot_left(left, right):
    return lax.dot_general(left, right, (((0,), (0,)), ((), ())), preferred_element_type=jnp.float32)


def dot_right(left, right):
    return lax.dot_general(left, right, (((1,), (1,)), ((), ())), preferred_element_type=jnp.float32)


def attention(projected, segment, token_position, low, low_back):
    span_length = projected.shape[0]
    key_offset = QUERY_HEADS * HEAD_SIZE
    value_offset = key_offset + KEY_VALUE_HEADS * HEAD_SIZE
    query_matrix = projected[:, :key_offset].reshape(span_length, QUERY_HEADS, HEAD_SIZE)
    key_matrix = projected[:, key_offset:value_offset].reshape(
        span_length, KEY_VALUE_HEADS, HEAD_SIZE
    )
    value_matrix = low(
        projected[:, value_offset:].reshape(span_length, KEY_VALUE_HEADS, HEAD_SIZE)
    )
    query_matrix = low(apply_rotary(query_matrix, token_position)).reshape(
        span_length, KEY_VALUE_HEADS, QUERY_HEADS // KEY_VALUE_HEADS, HEAD_SIZE
    )
    key_matrix = low(apply_rotary(key_matrix, token_position))
    slots = jnp.arange(span_length, dtype=jnp.int32)
    allowed = (segment[:, None] == segment[None, :]) & (slots[None, :] <= slots[:, None])
    scores = jnp.einsum("tagd,sad->agts", query_matrix, key_matrix, precision=None) * HEAD_SIZE ** (
        -0.5
    )
    scores = low_back(scores)
    scores = jnp.where(allowed[None, None], scores, -1000000000.0)
    probs = low(jax.nn.softmax(scores, axis=-1))
    context = low_back(jnp.einsum("agts,sad->tagd", probs, value_matrix, precision=None))
    return low(context.reshape(span_length, QUERY_HEADS * HEAD_SIZE))


def convolution(conv_in, kernel, segment, low):
    span_length = conv_in.shape[0]
    summed = jnp.zeros_like(conv_in) + kernel[KC][None, :]
    for lag in range(KC):
        shifted = jnp.concatenate(
            [jnp.zeros((lag, CONV), jnp.float32), conv_in[: span_length - lag]], axis=0
        )
        earlier = jnp.concatenate(
            [jnp.full((lag,), -1, jnp.int32), segment[: span_length - lag]], axis=0
        )
        keep = earlier == segment
        summed = summed + kernel[KC - 1 - lag][None, :] * jnp.where(keep[:, None], shifted, 0.0)
    return low(jax.nn.silu(summed))


TILE = 128


def mixing_tables(b_ref, c_ref, row_segment, column_segment, table, bias, transposed):
    left, right = (b_ref, c_ref) if transposed else (c_ref, b_ref)
    table[...] = dot_right(left[...], right[...])
    shape = table.shape
    first = lax.broadcasted_iota(jnp.int32, shape, 0)
    second = lax.broadcasted_iota(jnp.int32, shape, 1)
    order = (first <= second) if transposed else (second <= first)
    allowed = order & (column_segment[...] == row_segment[...])
    bias[...] = jnp.where(allowed, 0.0, -1e30)


def scan_forward_kernel(
    x_ref, b_ref, c_ref, cum_col, cum_row, step_row, skip, row_segment, column_segment,
    out_ref, table, bias,
):
    @pl.when(pl.program_id(0) == 0)
    def _():
        mixing_tables(b_ref, c_ref, row_segment, column_segment, table, bias, False)

    for start in range(0, x_ref.shape[0], TILE):
        rows, width = pl.ds(start, TILE), start + TILE
        halves = []
        for head in range(2):
            spread = cum_col[0, rows, head : head + 1] - cum_row[0, head : head + 1, :width]
            decay = jnp.exp(spread + bias[rows, :width])
            mixing = table[rows, :width] * decay * step_row[0, head : head + 1, :width]
            halves.append(dot(mixing.astype(jnp.bfloat16), x_ref[:width, :]))
        first = lax.broadcasted_iota(jnp.int32, (TILE, 2 * MP), 1) < MP
        out_ref[rows, :] = jnp.where(first, halves[0], halves[1]) + skip[...] * x_ref[
            rows, :
        ].astype(jnp.float32)


def scan_backward_kernel(
    cot_ref, out_ref, x_ref, b_ref, c_ref, cum_col, cum_row, step_col, skip,
    row_segment, column_segment, dx_ref, dcum_ref, dstep_ref, dskip_ref, dtable_ref,
    table, bias, dtable,
):
    @pl.when(pl.program_id(0) == 0)
    def _():
        mixing_tables(b_ref, c_ref, row_segment, column_segment, table, bias, True)
        dtable[...] = jnp.zeros_like(dtable)

    span = x_ref.shape[0]
    cot = cot_ref[...]
    cot_low = cot.astype(jnp.bfloat16)
    dskip_ref[...] = jnp.sum(cot * x_ref[...].astype(jnp.float32), axis=0, keepdims=True)
    for start in range(0, span, TILE):
        rows, later = pl.ds(start, TILE), pl.ds(start, span - start)
        first = lax.broadcasted_iota(jnp.int32, (TILE, 2 * MP), 1) < MP
        x_tile = x_ref[rows, :]
        halves = []
        for head in range(2):
            spread = cum_row[0, head : head + 1, start:] - cum_col[0, rows, head : head + 1]
            scaled = jnp.exp(spread + bias[rows, later]) * step_col[0, rows, head : head + 1]
            mixing = table[rows, later] * scaled
            mine = first if head == 0 else jnp.logical_not(first)
            x_head = jnp.where(mine, x_tile, jnp.zeros_like(x_tile))
            dtable[rows, later] += dot_right(x_head, cot_low[start:, :]) * scaled
            halves.append(dot(mixing.astype(jnp.bfloat16), cot_low[start:, :]))
        part = jnp.where(first, halves[0], halves[1])
        x_wide = x_tile.astype(jnp.float32)
        dx_ref[rows, :] = part + skip[...] * cot[start : start + TILE, :]
        into = x_wide * part
        product = out_ref[rows, :] - skip[...] * x_wide
        across = cot_low[start : start + TILE, :].astype(jnp.float32) * product - into
        for head in range(2):
            mine = first if head == 0 else jnp.logical_not(first)
            dcum_ref[0, rows, head : head + 1] = jnp.sum(
                jnp.where(mine, across, 0.0), axis=1, keepdims=True
            )
            dstep_ref[0, rows, head : head + 1] = jnp.sum(
                jnp.where(mine, into, 0.0), axis=1, keepdims=True
            )

    @pl.when(pl.program_id(0) == pl.num_programs(0) - 1)
    def _():
        dtable_ref[...] = dtable[...].astype(jnp.bfloat16)


def decay_steps(step_raw, head_params):
    step_size = jax.nn.softplus(step_raw + head_params[0][None, :])
    return step_size, jnp.cumsum(-step_size * jnp.exp(head_params[1])[None, :], axis=0)


def pair_columns(values):
    return jnp.swapaxes(values.reshape(values.shape[0], MH // 2, 2), 0, 1)


def scan_operands(conv_low, step_size, cumulative, head_params, segment):
    span = conv_low.shape[0]
    pair = pl.BlockSpec((span, 2 * MP), lambda i: (0, i))
    column = pl.BlockSpec((1, span, 2), lambda i: (i, 0, 0))
    row = pl.BlockSpec((1, 2, span), lambda i: (i, 0, 0))
    lanes = pl.BlockSpec((1, 2 * MP), lambda i: (0, i))
    b_spec = pl.BlockSpec((span, NS), lambda i: (0, MH // 2))
    c_spec = pl.BlockSpec((span, NS), lambda i: (0, MH // 2 + 1))
    row_segment = pl.BlockSpec((1, span), lambda i: (0, 0))
    column_segment = pl.BlockSpec((span, 1), lambda i: (0, 0))
    arrays = {
        "x": (conv_low, pair),
        "b": (conv_low, b_spec),
        "c": (conv_low, c_spec),
        "cum_col": (pair_columns(cumulative), column),
        "cum_row": (cumulative.T.reshape(MH // 2, 2, span), row),
        "step_col": (pair_columns(step_size), column),
        "step_row": (step_size.T.reshape(MH // 2, 2, span), row),
        "skip": (jnp.repeat(head_params[2], MP)[None, :], lanes),
        "row_segment": (segment[None, :], row_segment),
        "column_segment": (segment[:, None], column_segment),
    }
    return arrays, pair, column, lanes


def scan_forward(conv_low, step_size, cumulative, head_params, segment):
    span = conv_low.shape[0]
    arrays, pair, _, _ = scan_operands(conv_low, step_size, cumulative, head_params, segment)
    names = "x b c cum_col cum_row step_row skip row_segment column_segment".split()
    return pl.pallas_call(
        scan_forward_kernel,
        grid=(MH // 2,),
        out_shape=jax.ShapeDtypeStruct((span, MH * MP), jnp.float32),
        in_specs=[arrays[name][1] for name in names],
        out_specs=pair,
        scratch_shapes=[pltpu.VMEM((span, span), jnp.float32)] * 2,
        compiler_params=pltpu.CompilerParams(vmem_limit_bytes=32 * 1024 * 1024),
        name="scan_forward",
    )(*(arrays[name][0] for name in names))


def scan_backward(cot, out, conv_low, step_size, cumulative, head_params, segment):
    span = conv_low.shape[0]
    arrays, pair, column, lanes = scan_operands(
        conv_low, step_size, cumulative, head_params, segment
    )
    names = "x b c cum_col cum_row step_col skip row_segment column_segment".split()
    dx, dcum, dstep, dskip, dtable = pl.pallas_call(
        scan_backward_kernel,
        grid=(MH // 2,),
        out_shape=[
            jax.ShapeDtypeStruct((span, MH * MP), jnp.float32),
            jax.ShapeDtypeStruct((MH // 2, span, 2), jnp.float32),
            jax.ShapeDtypeStruct((MH // 2, span, 2), jnp.float32),
            jax.ShapeDtypeStruct((1, MH * MP), jnp.float32),
            jax.ShapeDtypeStruct((span, span), jnp.bfloat16),
        ],
        in_specs=[pair, pair] + [arrays[name][1] for name in names],
        out_specs=[pair, column, column, lanes, pl.BlockSpec((span, span), lambda i: (0, 0))],
        scratch_shapes=[pltpu.VMEM((span, span), jnp.float32)] * 3,
        compiler_params=pltpu.CompilerParams(vmem_limit_bytes=32 * 1024 * 1024),
        name="scan_backward",
    )(cot, out, *(arrays[name][0] for name in names))
    scan_b = conv_low[:, MH * MP : MH * MP + NS]
    scan_c = conv_low[:, MH * MP + NS :]
    conv_cot = jnp.concatenate([dx, dot(dtable, scan_c), dot_left(dtable, scan_b)], axis=1)
    dcum = jnp.swapaxes(dcum, 0, 1).reshape(span, MH)
    dstep = jnp.swapaxes(dstep, 0, 1).reshape(span, MH)
    dstep = jnp.where(step_size > 1e-30, dstep / jnp.maximum(step_size, 1e-30), 0.0)
    return conv_cot, dstep, dcum, jnp.sum(dskip.reshape(MH, MP), axis=1)


def gating(scan_out, gate_z, gain, low):
    return low(normalize(scan_out * jax.nn.silu(gate_z), gain))


def activation(gate_up, low):
    return low(jax.nn.silu(gate_up[:, :FF]) * gate_up[:, FF:])


def adamw(weight, mean, square, grad, rate):
    mean_new = BETA_MEAN * mean + (1.0 - BETA_MEAN) * grad
    square_new = BETA_SQUARE * square + (1.0 - BETA_SQUARE) * grad * grad
    corrected = (
        mean_new
        / (1.0 - BETA_MEAN**STEP)
        / (jnp.sqrt(square_new / (1.0 - BETA_SQUARE**STEP)) + ADAM_EPS)
    )
    return (weight - rate * (corrected + DECAY * weight), mean_new, square_new)


QKV = (QUERY_HEADS + 2 * KEY_VALUE_HEADS) * HEAD_SIZE
GATE = MH * MP
CONV = MH * MP + 2 * NS
STEP_LANES = 128


def general_gather(own, rep, shard):
    part = own
    if rep:
        copies = lax.axis_size(rep)
        rows = own.shape[0] // copies
        part = lax.dynamic_slice_in_dim(own, lax.axis_index(rep) * rows, rows, 0)
    return lax.all_gather(part, shard + rep, axis=0, tiled=True)


def gather_two(first, second, rep, shard):
    rows = first.shape[0] // lax.axis_size(rep)
    start = lax.axis_index(rep) * rows
    parts = [lax.dynamic_slice_in_dim(master, start, rows, 0) for master in (first, second)]
    own = jnp.stack(parts).astype(jnp.bfloat16)
    every = lax.all_gather(own, shard + rep, axis=0, tiled=False)
    return [every[:, index].reshape(-1, first.shape[1]) for index in range(2)]


def general_reduce(grad, rep, shard):
    piece = lax.psum_scatter(grad, shard + rep, scatter_dimension=0, tiled=True)
    return lax.all_gather(piece, rep, axis=0, tiled=True)


def place():
    return tuple(lax.axis_index(name) for name in ("x", "core", "z", "y"))


def send(values, dx=0, dcore=0, dz=0, dy=0):
    pairs = []
    for x in range(2):
        for core in range(2):
            for z in range(4):
                for y in range(2):
                    start = (x * 2 + core) * 8 + z * 2 + y
                    end = ((x ^ dx) * 2 + (core ^ dcore)) * 8 + ((z + dz) % 4) * 2 + (y ^ dy)
                    pairs.append((start, end))
    return lax.ppermute(values, ("x", "core", "z", "y"), pairs)


def pick(values, index, axis):
    return lax.dynamic_index_in_dim(values, index, axis, keepdims=False)


def fence(values, after):
    def kernel(*refs):
        del refs

    return pl.pallas_call(
        kernel,
        out_shape=[jax.ShapeDtypeStruct(value.shape, value.dtype) for value in values],
        in_specs=[pl.BlockSpec(memory_space=pl.ANY)] * (len(values) + len(after)),
        out_specs=[pl.BlockSpec(memory_space=pl.ANY)] * len(values),
        input_output_aliases={index: index for index in range(len(values))},
        name="fence",
    )(*values, *after)


def assemble(held, rows):
    quarter = rows // 8
    columns = held[0].shape[-1]

    def kernel(*refs):
        sources, target, sems = refs[:8], refs[8], refs[9]
        x, core, z, y = place()
        copies = []
        for other_core in range(2):
            half = core if other_core == 0 else 1 - core
            for other_y in range(2):
                row = y if other_y == 0 else 1 - y
                for turn in range(4):
                    owner = ((z + 4 - turn) % 4) * 2 + row
                    base = owner * rows + half * (rows // 2)
                    main = sources[other_core * 4 + other_y].at[turn]
                    cross = sources[other_core * 4 + 2 + other_y].at[turn]
                    for piece, start, count in (
                        (main.at[pl.ds(0, quarter)], base + x * quarter, quarter),
                        (main.at[pl.ds(quarter, 2 * quarter)], base + 2 * quarter, 2 * quarter),
                        (cross, base + (1 - x) * quarter, quarter),
                    ):
                        place_at = pl.ds(pl.multiple_of(start, 16), count)
                        copies.append(
                            pltpu.make_async_copy(piece, target.at[place_at], sems.at[len(copies)])
                        )
        for copy in copies:
            copy.start()
        for copy in copies:
            copy.wait()

    return pl.pallas_call(
        kernel,
        out_shape=jax.ShapeDtypeStruct((8 * rows, columns), jnp.bfloat16),
        in_specs=[pl.BlockSpec(memory_space=pl.ANY)] * 8,
        out_specs=pl.BlockSpec(memory_space=pltpu.VMEM),
        scratch_shapes=[pltpu.SemaphoreType.DMA((48,))],
        compiler_params=pltpu.CompilerParams(vmem_limit_bytes=24 * 1024 * 1024),
        name="assemble",
    )(*held)


def tuned_gather(pieces):
    x, core, z, y = place()
    results, after = [], None
    for own in pieces:
        rows = own.shape[0]
        quarter = rows // 8
        half = lax.dynamic_slice_in_dim(own, core * (rows // 2), rows // 2, 0)
        mine = jnp.concatenate(
            [lax.dynamic_slice_in_dim(half, x * quarter, quarter, 0), half[2 * quarter :]], axis=0
        )
        if after is not None:
            mine = fence([mine], after)[0]
        after = [send(mine, dz=turn) for turn in range(1, 4)]
        along_z = jnp.stack([mine] + after)
        across_y = send(along_z, dy=1)
        held = [along_z, across_y]
        held += [send(group[:, :quarter], dx=1) for group in held]
        held += [send(group, dcore=1) for group in held]
        results.append(assemble(held, rows))
    return results


def add_low(left, right):
    return (left.astype(jnp.float32) + right.astype(jnp.float32)).astype(jnp.bfloat16)


def tuned_reduce(grad):
    rows, columns = grad.shape[0] // 8, grad.shape[1]
    quarter = rows // 8
    x, core, z, y = place()
    parts = grad.reshape(4, 2, 2, rows // 2, columns)
    far = pick(parts, 1 - core, 2)
    yield [far]
    half = add_low(pick(parts, core, 2), send(far, dcore=1))
    far = lax.dynamic_slice_in_dim(half, (1 - x) * quarter, quarter, 2)
    yield [far]
    near = add_low(lax.dynamic_slice_in_dim(half, x * quarter, quarter, 2), send(far, dx=1))
    both = half[:, :, 2 * quarter :]
    there = jnp.concatenate([pick(near, 1 - y, 1), pick(both, 1 - y, 1)], axis=1)
    here = jnp.concatenate([pick(near, y, 1), pick(both, y, 1)], axis=1)
    yield [there]
    column = add_low(here, send(there, dy=1))
    turns = [pick(column, (z + turn) % 4, 0) for turn in range(1, 4)]
    yield turns
    total = pick(column, z, 0).astype(jnp.float32)
    for turn in range(1, 4):
        total = total + send(turns[turn - 1], dz=turn).astype(jnp.float32)
    total = total.astype(jnp.bfloat16)
    yield [total]
    across = send(total, dx=1)
    own_x, other_x = total[:quarter], across[:quarter]
    owned = jnp.concatenate(
        [
            jnp.where(x == 0, own_x, other_x),
            jnp.where(x == 0, other_x, own_x),
            add_low(total[quarter:], across[quarter:]),
        ],
        axis=0,
    )
    yield [owned]
    beside = send(owned, dcore=1)
    return jnp.concatenate(
        [jnp.where(core == 0, owned, beside), jnp.where(core == 0, beside, owned)], axis=0
    )


def paired_reduce(grad):
    rows, columns = grad.shape[0] // 8, grad.shape[1]
    x, core, z, y = place()
    parts = grad.reshape(8, 2, rows // 2, columns)
    far = pick(parts, 1 - core, 1)
    yield [far]
    half = add_low(pick(parts, core, 1), send(far, dcore=1)).reshape(4 * rows, columns)
    yield [half]
    own = lax.psum_scatter(half, ("z", "y", "x"), scatter_dimension=0, tiled=True)
    yield None
    across = send(own, dx=1)
    owned = jnp.concatenate(
        [jnp.where(x == 0, own, across), jnp.where(x == 0, across, own)], axis=0
    )
    yield None
    beside = send(owned, dcore=1)
    return jnp.concatenate(
        [jnp.where(core == 0, owned, beside), jnp.where(core == 0, beside, owned)], axis=0
    )


def general_stages(grad, rep, shard):
    yield None
    return general_reduce(grad, rep, shard)


class Reductions:

    def __init__(self, axes):
        self.axes = axes
        self.running, self.results, self.waiting = {}, {}, {}

    def add(self, name, grad, paired=False):
        grad = grad.astype(jnp.bfloat16)
        if not tuned(self.axes):
            self.running[name] = general_stages(grad, *self.axes)
        elif paired:
            self.running[name] = paired_reduce(grad)
        else:
            self.running[name] = tuned_reduce(grad)

    def step(self, values):
        after = []
        for name in list(self.running):
            if self.waiting.get(name):
                continue
            ready = self.advance(name)
            if ready is None:
                self.waiting[name] = True
            else:
                after += ready
        return fence(values, after) if after else values

    def advance(self, name):
        try:
            return next(self.running[name])
        except StopIteration as stop:
            self.results[name] = stop.value
            del self.running[name]
            return []

    def finish(self):
        while self.running:
            for name in list(self.running):
                self.advance(name)
        return self.results


def tuned(axes):
    return axes == (("x", "core"), ("z", "y"))


def gather_weights(axes, mixer_in, mixer_out, swiglu_in, swiglu_out, gains, conv_kernel):
    rows = mixer_in.shape[0]
    rep, shard = axes
    owners = lax.axis_size(shard)
    width = conv_kernel.shape[1]
    count = gains.shape[0] + conv_kernel.size
    lanes = -(-count // rows)
    vector = jnp.concatenate([gains, conv_kernel.reshape(-1)])
    vector = jnp.pad(vector, (0, lanes * rows - count)).reshape(rows, lanes)
    low_in = mixer_in.astype(jnp.bfloat16)
    tail = STEP_LANES - MH - lanes
    conv_piece = jnp.concatenate(
        [low_in[:, QKV + GATE :], vector.astype(jnp.bfloat16), jnp.zeros((rows, tail), jnp.bfloat16)],
        axis=1,
    )
    pieces = [conv_piece, low_in[:, : QKV + GATE]]
    if tuned(axes):
        pieces = tuned_gather(pieces)
    else:
        pieces = [general_gather(piece, rep, shard) for piece in pieces]
    if tuned(axes):
        w_out, w_down = gather_two(mixer_out, swiglu_out, rep, shard)
        pieces += [w_out, general_gather(swiglu_in.astype(jnp.bfloat16), rep, shard), w_down]
    else:
        for master in (mixer_out, swiglu_in, swiglu_out):
            pieces.append(general_gather(master.astype(jnp.bfloat16), rep, shard))
    every = pieces[0][:, CONV + MH : CONV + MH + lanes].reshape(owners, rows * lanes)
    gains_all = every[:, : gains.shape[0]].reshape(-1)
    taps = every[:, gains.shape[0] : count].reshape(owners, KC + 1, width)
    taps = jnp.swapaxes(taps, 0, 1).reshape(KC + 1, owners * width)
    return pieces + [gains_all.astype(jnp.float32), taps.astype(jnp.float32)]


def with_vectors(conv_g, gains_g, taps_g, head_grad, owners):
    rows = conv_g.shape[0] // owners
    width = taps_g.shape[1] // owners
    vector = jnp.concatenate(
        [
            gains_g.reshape(owners, -1),
            jnp.swapaxes(taps_g.reshape(KC + 1, owners, width), 0, 1).reshape(owners, -1),
            jnp.broadcast_to(head_grad.reshape(1, -1), (owners, head_grad.size)),
        ],
        axis=1,
    )
    count = vector.shape[1]
    lanes = -(-count // rows)
    vector = jnp.pad(vector, ((0, 0), (0, lanes * rows - count))).reshape(owners * rows, lanes)
    vector = jnp.pad(vector, ((0, 0), (MH, STEP_LANES - MH - lanes)))
    return jnp.concatenate([conv_g[:, :CONV], conv_g[:, CONV:] + vector], axis=1)


def split_vectors(conv, own_gains, width, head_shape):
    rows = conv.shape[0]
    count = own_gains + (KC + 1) * width + head_shape[0] * head_shape[1]
    lanes = -(-count // rows)
    used = CONV + MH
    flat = conv[:, used : used + lanes].astype(jnp.float32).reshape(-1)
    taps_end = own_gains + (KC + 1) * width
    return (
        flat[:own_gains],
        flat[own_gains:taps_end].reshape(KC + 1, width),
        flat[taps_end:count].reshape(head_shape),
    )


def forward_backward(axes, tokens, cotangent, seq_row, weights, head_params):
    low, low_back = make_rounders()
    w_conv, w_side, w_out, w_up, w_down, gain_all, taps = weights
    segment, token_position, valid = layout(seq_row, tokens.shape[0])
    values = tokens.astype(jnp.float32)
    context_width = QUERY_HEADS * HEAD_SIZE

    normed, pull_norm = jax.vjp(lambda v, g: low(normalize(v, g)), values, gain_all[:D])
    normed_low = rows_of(normed)
    projected = dot(normed_low, w_conv)
    conv_out, pull_conv = jax.vjp(
        lambda p, k: convolution(p, k, segment, low), projected[:, :CONV], taps
    )
    conv_low = rows_of(conv_out)
    (step_size, cumulative), pull_steps = jax.vjp(
        decay_steps, projected[:, CONV : CONV + MH], head_params
    )
    scan_out = scan_forward(conv_low, step_size, cumulative, head_params, segment)
    beside = dot(normed_low, w_side)
    context, pull_context = jax.vjp(
        lambda p: attention(p, segment, token_position, low, low_back), beside[:, :QKV]
    )
    mamba_out, pull_gating = jax.vjp(
        lambda s, z, g: gating(s, z, g, low), scan_out, beside[:, QKV:], gain_all[2 * D :]
    )
    joined = jnp.concatenate([rows_of(context), rows_of(mamba_out)], axis=1)
    hidden = values + dot(joined, w_out)
    normed_ff, pull_ff = jax.vjp(lambda v, g: low(normalize(v, g)), hidden, gain_all[D : 2 * D])
    normed_ff_low = rows_of(normed_ff)
    activated, pull_active = jax.vjp(lambda g: activation(g, low), dot(normed_ff_low, w_up))
    activated_low = rows_of(activated)
    output = (hidden + dot(activated_low, w_down)).astype(jnp.bfloat16)

    moving = Reductions(axes)
    cot = jnp.where(valid[:, None], cotangent, jnp.zeros_like(cotangent))
    (up_cot,) = pull_active(dot_right(cot, w_down))
    up_cot = rows_of(up_cot)
    moving.add("down", dot_left(activated_low, cot), paired=True)
    (up_cot,) = moving.step([up_cot])
    moving.add("up", dot_left(normed_ff_low, up_cot), paired=True)
    (ff_cot,) = moving.step([dot_right(up_cot, w_up)])
    hidden_part, gain_ff = pull_ff(ff_cot)
    hidden_cot = cot.astype(jnp.float32) + hidden_part
    hidden_low = rows_of(hidden_cot)
    moving.add("out", dot_left(joined, hidden_low), paired=True)
    (joined_cot,) = moving.step([dot_right(hidden_low, w_out)])
    scan_cot, gate_cot, gain_scan = pull_gating(joined_cot[:, context_width:])
    (qkv_cot,) = pull_context(joined_cot[:, :context_width])
    side_cot = jnp.concatenate([rows_of(qkv_cot), rows_of(gate_cot)], axis=1)
    moving.add("side", dot_left(normed_low, side_cot))
    (scan_cot,) = moving.step([scan_cot])
    conv_out_cot, dstep, dcum, dskip = scan_backward(
        scan_cot, scan_out, conv_low, step_size, cumulative, head_params, segment
    )
    step_cot, head_grad = pull_steps((dstep, dcum))
    head_grad = head_grad.at[2].add(dskip)
    (conv_out_cot,) = moving.step([conv_out_cot])
    conv_cot, taps_grad = pull_conv(conv_out_cot)
    conv_cot = rows_of(
        jnp.concatenate(
            [conv_cot, step_cot, jnp.zeros((tokens.shape[0], STEP_LANES - MH), jnp.float32)], axis=1
        )
    )
    (conv_cot,) = moving.step([conv_cot])
    normed_cot = dot_right(side_cot, w_side) + dot_right(conv_cot, w_conv)
    tokens_part, gain_in = pull_norm(normed_cot)
    token_grad = hidden_cot + tokens_part
    gains_grad = jnp.concatenate([gain_in, gain_ff, gain_scan])
    owners = lax.axis_size(axes[1])
    moving.add(
        "conv",
        with_vectors(dot_left(normed_low, conv_cot), gains_grad, taps_grad, head_grad, owners),
    )
    return output, token_grad, moving.finish()


def on_device(
    axes,
    tokens,
    cotangent,
    seq_lengths,
    mixer_in,
    mixer_in_mean,
    mixer_in_square,
    mixer_out,
    mixer_out_mean,
    mixer_out_square,
    swiglu_in,
    swiglu_in_mean,
    swiglu_in_square,
    swiglu_out,
    swiglu_out_mean,
    swiglu_out_square,
    gains,
    gains_mean,
    gains_square,
    conv_kernel,
    conv_kernel_mean,
    conv_kernel_square,
    head_params,
    head_params_mean,
    head_params_square,
):
    weights = gather_weights(axes, mixer_in, mixer_out, swiglu_in, swiglu_out, gains, conv_kernel)
    output, token_grad, sums = forward_backward(
        axes, tokens, cotangent, seq_lengths[0], weights, head_params
    )
    own_gains, own_taps, head_grad = split_vectors(
        sums["conv"], gains.shape[0], conv_kernel.shape[1], head_params.shape
    )
    matrix = jnp.concatenate([sums["side"].T, sums["conv"][:, : CONV + MH].T], axis=0)
    owned = (
        matrix.astype(jnp.float32),
        sums["out"].astype(jnp.float32),
        sums["up"].astype(jnp.float32),
        sums["down"].astype(jnp.float32),
        own_gains,
        own_taps,
    )
    masters = (mixer_in, mixer_out, swiglu_in, swiglu_out, gains, conv_kernel)
    means = (
        mixer_in_mean,
        mixer_out_mean,
        swiglu_in_mean,
        swiglu_out_mean,
        gains_mean,
        conv_kernel_mean,
    )
    squares = (
        mixer_in_square,
        mixer_out_square,
        swiglu_in_square,
        swiglu_out_square,
        gains_square,
        conv_kernel_square,
    )
    rates = (MATRIX_RATE, MATRIX_RATE, MATRIX_RATE, MATRIX_RATE, VECTOR_RATE, VECTOR_RATE)
    turned = adamw(mixer_in.T, mixer_in_mean.T, mixer_in_square.T, owned[0], rates[0])
    updated = [tuple(array.T for array in turned)] + [
        adamw(masters[index], means[index], squares[index], owned[index], rates[index])
        for index in range(1, 6)
    ]
    head_new = adamw(head_params, head_params_mean, head_params_square, head_grad, VECTOR_RATE)
    return (
        output,
        token_grad,
        updated[0][0],
        updated[0][1],
        updated[0][2],
        updated[1][0],
        updated[1][1],
        updated[1][2],
        updated[2][0],
        updated[2][1],
        updated[2][2],
        updated[3][0],
        updated[3][1],
        updated[3][2],
        updated[4][0],
        updated[4][1],
        updated[4][2],
        updated[5][0],
        updated[5][1],
        updated[5][2],
        head_new[0],
        head_new[1],
        head_new[2],
    )


def solution(mesh):
    rep, shard = ("rep",), ("shard",)
    if mesh.shape["rep"] == 4 and mesh.shape["shard"] == 8:
        rep, shard = ("x", "core"), ("z", "y")
        mesh = Mesh(mesh.devices.reshape(2, 2, 4, 2), rep + shard)
    rows, owned, across, copied = P(rep + shard, None), P(shard, None), P(None, shard), P()
    optimizer = (owned,) * 12 + (P(shard),) * 3 + (across,) * 3 + (copied,) * 3
    return jax.shard_map(
        functools.partial(on_device, (rep, shard)),
        mesh=mesh,
        in_specs=(rows, rows, rows) + optimizer,
        out_specs=(rows, rows) + optimizer,
        check_vma=False,
    )
```

```python
import functools

import jax
import jax.numpy as jnp
from jax import lax
from jax.experimental import pallas as pl
from jax.experimental.pallas import tpu as pltpu
from jax.sharding import Mesh, PartitionSpec as P

D = 1024
FF = 2048
QUERY_HEADS = 8
KEY_VALUE_HEADS = 2
HEAD_SIZE = 64
MH = 24
MP = 64
NS = 128
KC = 4
STEP = 10


NORM_EPS = 1e-05
ROPE_BASE = 100000000000.0
BETA_MEAN = 0.9
BETA_SQUARE = 0.95
ADAM_EPS = 1e-08
DECAY = 0.1
MATRIX_RATE = 0.03
VECTOR_RATE = 0.5


def make_rounders():

    def round_value(values):
        return lax.optimization_barrier(values.astype(jnp.bfloat16)).astype(jnp.float32)

    def pass_value(values):
        return values

    value_rounder = jax.custom_vjp(round_value)
    grad_rounder = jax.custom_vjp(pass_value)

    def value_keep(values):
        return (round_value(values), None)

    def value_pass(kept, grad):
        return (grad,)

    def grad_keep(values):
        return (values, None)

    def grad_round(kept, grad):
        return (round_value(grad),)

    value_rounder.defvjp(value_keep, value_pass)
    grad_rounder.defvjp(grad_keep, grad_round)
    return (value_rounder, grad_rounder)


def normalize(values, gain):
    return values * lax.rsqrt(jnp.mean(values * values, axis=-1, keepdims=True) + NORM_EPS) * gain


def layout(seq_row, span_length):
    count = seq_row.shape[0]
    ends = jnp.cumsum(seq_row)
    starts = ends - seq_row
    slots = jnp.arange(span_length, dtype=jnp.int32)
    segment = jnp.sum((slots[:, None] >= ends[None, :]).astype(jnp.int32), axis=1)
    valid = slots < ends[count - 1]
    segment = jnp.where(valid, segment, count + slots)
    match = segment[:, None] == jnp.arange(count, dtype=jnp.int32)[None, :]
    first = jnp.sum(jnp.where(match, starts[None, :], 0), axis=1)
    token_position = jnp.where(valid, slots - first, 0)
    return (segment, token_position, valid)


def apply_rotary(values, token_position):
    half = HEAD_SIZE // 2
    freq = ROPE_BASE ** (-(jnp.arange(half, dtype=jnp.float32) * 2.0 / HEAD_SIZE))
    angle = token_position.astype(jnp.float32)[:, None] * freq[None, :]
    cosine = jnp.cos(angle)[:, None, :]
    sine = jnp.sin(angle)[:, None, :]
    first_half = values[..., :half]
    second_half = values[..., half:]
    return jnp.concatenate(
        [first_half * cosine - second_half * sine, second_half * cosine + first_half * sine],
        axis=-1,
    )


def rows_of(matrix):
    return matrix.astype(jnp.bfloat16)


def dot(left, right):
    return jnp.dot(left, right, preferred_element_type=jnp.float32)


def dot_left(left, right):
    return lax.dot_general(left, right, (((0,), (0,)), ((), ())), preferred_element_type=jnp.float32)


def dot_right(left, right):
    return lax.dot_general(left, right, (((1,), (1,)), ((), ())), preferred_element_type=jnp.float32)


def attention(projected, segment, token_position, low, low_back):
    span_length = projected.shape[0]
    key_offset = QUERY_HEADS * HEAD_SIZE
    value_offset = key_offset + KEY_VALUE_HEADS * HEAD_SIZE
    query_matrix = projected[:, :key_offset].reshape(span_length, QUERY_HEADS, HEAD_SIZE)
    key_matrix = projected[:, key_offset:value_offset].reshape(
        span_length, KEY_VALUE_HEADS, HEAD_SIZE
    )
    value_matrix = low(
        projected[:, value_offset:].reshape(span_length, KEY_VALUE_HEADS, HEAD_SIZE)
    )
    query_matrix = low(apply_rotary(query_matrix, token_position)).reshape(
        span_length, KEY_VALUE_HEADS, QUERY_HEADS // KEY_VALUE_HEADS, HEAD_SIZE
    )
    key_matrix = low(apply_rotary(key_matrix, token_position))
    slots = jnp.arange(span_length, dtype=jnp.int32)
    allowed = (segment[:, None] == segment[None, :]) & (slots[None, :] <= slots[:, None])
    scores = jnp.einsum("tagd,sad->agts", query_matrix, key_matrix, precision=None) * HEAD_SIZE ** (
        -0.5
    )
    scores = low_back(scores)
    scores = jnp.where(allowed[None, None], scores, -1000000000.0)
    probs = low(jax.nn.softmax(scores, axis=-1))
    context = low_back(jnp.einsum("agts,sad->tagd", probs, value_matrix, precision=None))
    return low(context.reshape(span_length, QUERY_HEADS * HEAD_SIZE))


def convolution(conv_in, kernel, segment, low):
    span_length = conv_in.shape[0]
    summed = jnp.zeros_like(conv_in) + kernel[KC][None, :]
    for lag in range(KC):
        shifted = jnp.concatenate(
            [jnp.zeros((lag, CONV), jnp.float32), conv_in[: span_length - lag]], axis=0
        )
        earlier = jnp.concatenate(
            [jnp.full((lag,), -1, jnp.int32), segment[: span_length - lag]], axis=0
        )
        keep = earlier == segment
        summed = summed + kernel[KC - 1 - lag][None, :] * jnp.where(keep[:, None], shifted, 0.0)
    return low(jax.nn.silu(summed))


TILE = 128


def mixing_tables(b_ref, c_ref, row_segment, column_segment, table, bias, transposed):
    left, right = (b_ref, c_ref) if transposed else (c_ref, b_ref)
    table[...] = dot_right(left[...], right[...])
    shape = table.shape
    first = lax.broadcasted_iota(jnp.int32, shape, 0)
    second = lax.broadcasted_iota(jnp.int32, shape, 1)
    order = (first <= second) if transposed else (second <= first)
    allowed = order & (column_segment[...] == row_segment[...])
    bias[...] = jnp.where(allowed, 0.0, -1e30)


def scan_forward_kernel(
    x_ref, b_ref, c_ref, cum_col, cum_row, step_row, skip, row_segment, column_segment,
    out_ref, table, bias,
):
    @pl.when(pl.program_id(0) == 0)
    def _():
        mixing_tables(b_ref, c_ref, row_segment, column_segment, table, bias, False)

    for start in range(0, x_ref.shape[0], TILE):
        rows, width = pl.ds(start, TILE), start + TILE
        halves = []
        for head in range(2):
            spread = cum_col[0, rows, head : head + 1] - cum_row[0, head : head + 1, :width]
            decay = jnp.exp(spread + bias[rows, :width])
            mixing = table[rows, :width] * decay * step_row[0, head : head + 1, :width]
            halves.append(dot(mixing.astype(jnp.bfloat16), x_ref[:width, :]))
        first = lax.broadcasted_iota(jnp.int32, (TILE, 2 * MP), 1) < MP
        out_ref[rows, :] = jnp.where(first, halves[0], halves[1]) + skip[...] * x_ref[
            rows, :
        ].astype(jnp.float32)


def scan_backward_kernel(
    cot_ref, out_ref, x_ref, b_ref, c_ref, cum_col, cum_row, step_col, skip,
    row_segment, column_segment, dx_ref, dcum_ref, dstep_ref, dskip_ref, dtable_ref,
    table, bias, dtable,
):
    @pl.when(pl.program_id(0) == 0)
    def _():
        mixing_tables(b_ref, c_ref, row_segment, column_segment, table, bias, True)
        dtable[...] = jnp.zeros_like(dtable)

    span = x_ref.shape[0]
    cot = cot_ref[...]
    cot_low = cot.astype(jnp.bfloat16)
    dskip_ref[...] = jnp.sum(cot * x_ref[...].astype(jnp.float32), axis=0, keepdims=True)
    for start in range(0, span, TILE):
        rows, later = pl.ds(start, TILE), pl.ds(start, span - start)
        first = lax.broadcasted_iota(jnp.int32, (TILE, 2 * MP), 1) < MP
        x_tile = x_ref[rows, :]
        halves = []
        for head in range(2):
            spread = cum_row[0, head : head + 1, start:] - cum_col[0, rows, head : head + 1]
            scaled = jnp.exp(spread + bias[rows, later]) * step_col[0, rows, head : head + 1]
            mixing = table[rows, later] * scaled
            mine = first if head == 0 else jnp.logical_not(first)
            x_head = jnp.where(mine, x_tile, jnp.zeros_like(x_tile))
            dtable[rows, later] += dot_right(x_head, cot_low[start:, :]) * scaled
            halves.append(dot(mixing.astype(jnp.bfloat16), cot_low[start:, :]))
        part = jnp.where(first, halves[0], halves[1])
        x_wide = x_tile.astype(jnp.float32)
        dx_ref[rows, :] = part + skip[...] * cot[start : start + TILE, :]
        into = x_wide * part
        product = out_ref[rows, :] - skip[...] * x_wide
        across = cot_low[start : start + TILE, :].astype(jnp.float32) * product - into
        for head in range(2):
            mine = first if head == 0 else jnp.logical_not(first)
            dcum_ref[0, rows, head : head + 1] = jnp.sum(
                jnp.where(mine, across, 0.0), axis=1, keepdims=True
            )
            dstep_ref[0, rows, head : head + 1] = jnp.sum(
                jnp.where(mine, into, 0.0), axis=1, keepdims=True
            )

    @pl.when(pl.program_id(0) == pl.num_programs(0) - 1)
    def _():
        dtable_ref[...] = dtable[...].astype(jnp.bfloat16)


def decay_steps(step_raw, head_params):
    step_size = jax.nn.softplus(step_raw + head_params[0][None, :])
    return step_size, jnp.cumsum(-step_size * jnp.exp(head_params[1])[None, :], axis=0)


def pair_columns(values):
    return jnp.swapaxes(values.reshape(values.shape[0], MH // 2, 2), 0, 1)


def scan_operands(conv_low, step_size, cumulative, head_params, segment):
    span = conv_low.shape[0]
    pair = pl.BlockSpec((span, 2 * MP), lambda i: (0, i))
    column = pl.BlockSpec((1, span, 2), lambda i: (i, 0, 0))
    row = pl.BlockSpec((1, 2, span), lambda i: (i, 0, 0))
    lanes = pl.BlockSpec((1, 2 * MP), lambda i: (0, i))
    b_spec = pl.BlockSpec((span, NS), lambda i: (0, MH // 2))
    c_spec = pl.BlockSpec((span, NS), lambda i: (0, MH // 2 + 1))
    row_segment = pl.BlockSpec((1, span), lambda i: (0, 0))
    column_segment = pl.BlockSpec((span, 1), lambda i: (0, 0))
    arrays = {
        "x": (conv_low, pair),
        "b": (conv_low, b_spec),
        "c": (conv_low, c_spec),
        "cum_col": (pair_columns(cumulative), column),
        "cum_row": (cumulative.T.reshape(MH // 2, 2, span), row),
        "step_col": (pair_columns(step_size), column),
        "step_row": (step_size.T.reshape(MH // 2, 2, span), row),
        "skip": (jnp.repeat(head_params[2], MP)[None, :], lanes),
        "row_segment": (segment[None, :], row_segment),
        "column_segment": (segment[:, None], column_segment),
    }
    return arrays, pair, column, lanes


def scan_forward(conv_low, step_size, cumulative, head_params, segment):
    span = conv_low.shape[0]
    arrays, pair, _, _ = scan_operands(conv_low, step_size, cumulative, head_params, segment)
    names = "x b c cum_col cum_row step_row skip row_segment column_segment".split()
    return pl.pallas_call(
        scan_forward_kernel,
        grid=(MH // 2,),
        out_shape=jax.ShapeDtypeStruct((span, MH * MP), jnp.float32),
        in_specs=[arrays[name][1] for name in names],
        out_specs=pair,
        scratch_shapes=[pltpu.VMEM((span, span), jnp.float32)] * 2,
        compiler_params=pltpu.CompilerParams(vmem_limit_bytes=32 * 1024 * 1024),
        name="scan_forward",
    )(*(arrays[name][0] for name in names))


def scan_backward(cot, out, conv_low, step_size, cumulative, head_params, segment):
    span = conv_low.shape[0]
    arrays, pair, column, lanes = scan_operands(
        conv_low, step_size, cumulative, head_params, segment
    )
    names = "x b c cum_col cum_row step_col skip row_segment column_segment".split()
    dx, dcum, dstep, dskip, dtable = pl.pallas_call(
        scan_backward_kernel,
        grid=(MH // 2,),
        out_shape=[
            jax.ShapeDtypeStruct((span, MH * MP), jnp.float32),
            jax.ShapeDtypeStruct((MH // 2, span, 2), jnp.float32),
            jax.ShapeDtypeStruct((MH // 2, span, 2), jnp.float32),
            jax.ShapeDtypeStruct((1, MH * MP), jnp.float32),
            jax.ShapeDtypeStruct((span, span), jnp.bfloat16),
        ],
        in_specs=[pair, pair] + [arrays[name][1] for name in names],
        out_specs=[pair, column, column, lanes, pl.BlockSpec((span, span), lambda i: (0, 0))],
        scratch_shapes=[pltpu.VMEM((span, span), jnp.float32)] * 3,
        compiler_params=pltpu.CompilerParams(vmem_limit_bytes=32 * 1024 * 1024),
        name="scan_backward",
    )(cot, out, *(arrays[name][0] for name in names))
    scan_b = conv_low[:, MH * MP : MH * MP + NS]
    scan_c = conv_low[:, MH * MP + NS :]
    conv_cot = jnp.concatenate([dx, dot(dtable, scan_c), dot_left(dtable, scan_b)], axis=1)
    dcum = jnp.swapaxes(dcum, 0, 1).reshape(span, MH)
    dstep = jnp.swapaxes(dstep, 0, 1).reshape(span, MH)
    dstep = jnp.where(step_size > 1e-30, dstep / jnp.maximum(step_size, 1e-30), 0.0)
    return conv_cot, dstep, dcum, jnp.sum(dskip.reshape(MH, MP), axis=1)


def gating(scan_out, gate_z, gain, low):
    return low(normalize(scan_out * jax.nn.silu(gate_z), gain))


def activation(gate_up, low):
    return low(jax.nn.silu(gate_up[:, :FF]) * gate_up[:, FF:])


def adamw(weight, mean, square, grad, rate):
    mean_new = BETA_MEAN * mean + (1.0 - BETA_MEAN) * grad
    square_new = BETA_SQUARE * square + (1.0 - BETA_SQUARE) * grad * grad
    corrected = (
        mean_new
        / (1.0 - BETA_MEAN**STEP)
        / (jnp.sqrt(square_new / (1.0 - BETA_SQUARE**STEP)) + ADAM_EPS)
    )
    return (weight - rate * (corrected + DECAY * weight), mean_new, square_new)


QKV = (QUERY_HEADS + 2 * KEY_VALUE_HEADS) * HEAD_SIZE
GATE = MH * MP
CONV = MH * MP + 2 * NS
STEP_LANES = 128


def general_gather(own, rep, shard):
    part = own
    if rep:
        copies = lax.axis_size(rep)
        rows = own.shape[0] // copies
        part = lax.dynamic_slice_in_dim(own, lax.axis_index(rep) * rows, rows, 0)
    return lax.all_gather(part, shard + rep, axis=0, tiled=True)


def gather_two(first, second, rep, shard):
    rows = first.shape[0] // lax.axis_size(rep)
    start = lax.axis_index(rep) * rows
    parts = [lax.dynamic_slice_in_dim(master, start, rows, 0) for master in (first, second)]
    own = jnp.stack(parts).astype(jnp.bfloat16)
    every = lax.all_gather(own, shard + rep, axis=0, tiled=False)
    return [every[:, index].reshape(-1, first.shape[1]) for index in range(2)]


def general_reduce(grad, rep, shard):
    piece = lax.psum_scatter(grad, shard + rep, scatter_dimension=0, tiled=True)
    return lax.all_gather(piece, rep, axis=0, tiled=True)


def place():
    return tuple(lax.axis_index(name) for name in ("x", "core", "z", "y"))


def send(values, dx=0, dcore=0, dz=0, dy=0):
    pairs = []
    for x in range(2):
        for core in range(2):
            for z in range(4):
                for y in range(2):
                    start = (x * 2 + core) * 8 + z * 2 + y
                    end = ((x ^ dx) * 2 + (core ^ dcore)) * 8 + ((z + dz) % 4) * 2 + (y ^ dy)
                    pairs.append((start, end))
    return lax.ppermute(values, ("x", "core", "z", "y"), pairs)


def pick(values, index, axis):
    return lax.dynamic_index_in_dim(values, index, axis, keepdims=False)


def fence(values, after):
    def kernel(*refs):
        del refs

    return pl.pallas_call(
        kernel,
        out_shape=[jax.ShapeDtypeStruct(value.shape, value.dtype) for value in values],
        in_specs=[pl.BlockSpec(memory_space=pl.ANY)] * (len(values) + len(after)),
        out_specs=[pl.BlockSpec(memory_space=pl.ANY)] * len(values),
        input_output_aliases={index: index for index in range(len(values))},
        name="fence",
    )(*values, *after)


def assemble(held, rows):
    quarter = rows // 8
    columns = held[0].shape[-1]

    def kernel(*refs):
        sources, target, sems = refs[:8], refs[8], refs[9]
        x, core, z, y = place()
        copies = []
        for other_core in range(2):
            half = core if other_core == 0 else 1 - core
            for other_y in range(2):
                row = y if other_y == 0 else 1 - y
                for turn in range(4):
                    owner = ((z + 4 - turn) % 4) * 2 + row
                    base = owner * rows + half * (rows // 2)
                    main = sources[other_core * 4 + other_y].at[turn]
                    cross = sources[other_core * 4 + 2 + other_y].at[turn]
                    for piece, start, count in (
                        (main.at[pl.ds(0, quarter)], base + x * quarter, quarter),
                        (main.at[pl.ds(quarter, 2 * quarter)], base + 2 * quarter, 2 * quarter),
                        (cross, base + (1 - x) * quarter, quarter),
                    ):
                        place_at = pl.ds(pl.multiple_of(start, 16), count)
                        copies.append(
                            pltpu.make_async_copy(piece, target.at[place_at], sems.at[len(copies)])
                        )
        for copy in copies:
            copy.start()
        for copy in copies:
            copy.wait()

    return pl.pallas_call(
        kernel,
        out_shape=jax.ShapeDtypeStruct((8 * rows, columns), jnp.bfloat16),
        in_specs=[pl.BlockSpec(memory_space=pl.ANY)] * 8,
        out_specs=pl.BlockSpec(memory_space=pltpu.VMEM),
        scratch_shapes=[pltpu.SemaphoreType.DMA((48,))],
        compiler_params=pltpu.CompilerParams(vmem_limit_bytes=24 * 1024 * 1024),
        name="assemble",
    )(*held)


def tuned_gather(pieces):
    x, core, z, y = place()
    results, after = [], None
    for own in pieces:
        rows = own.shape[0]
        quarter = rows // 8
        half = lax.dynamic_slice_in_dim(own, core * (rows // 2), rows // 2, 0)
        mine = jnp.concatenate(
            [lax.dynamic_slice_in_dim(half, x * quarter, quarter, 0), half[2 * quarter :]], axis=0
        )
        if after is not None:
            mine = fence([mine], after)[0]
        after = [send(mine, dz=turn) for turn in range(1, 4)]
        along_z = jnp.stack([mine] + after)
        across_y = send(along_z, dy=1)
        held = [along_z, across_y]
        held += [send(group[:, :quarter], dx=1) for group in held]
        held += [send(group, dcore=1) for group in held]
        results.append(assemble(held, rows))
    return results


def add_low(left, right):
    return (left.astype(jnp.float32) + right.astype(jnp.float32)).astype(jnp.bfloat16)


def tuned_reduce(grad):
    rows, columns = grad.shape[0] // 8, grad.shape[1]
    quarter = rows // 8
    x, core, z, y = place()
    parts = grad.reshape(4, 2, 2, rows // 2, columns)
    far = pick(parts, 1 - core, 2)
    yield [far]
    half = add_low(pick(parts, core, 2), send(far, dcore=1))
    far = lax.dynamic_slice_in_dim(half, (1 - x) * quarter, quarter, 2)
    yield [far]
    near = add_low(lax.dynamic_slice_in_dim(half, x * quarter, quarter, 2), send(far, dx=1))
    both = half[:, :, 2 * quarter :]
    there = jnp.concatenate([pick(near, 1 - y, 1), pick(both, 1 - y, 1)], axis=1)
    here = jnp.concatenate([pick(near, y, 1), pick(both, y, 1)], axis=1)
    yield [there]
    column = add_low(here, send(there, dy=1))
    turns = [pick(column, (z + turn) % 4, 0) for turn in range(1, 4)]
    turns = (yield turns) or turns
    total = pick(column, z, 0).astype(jnp.float32)
    for turn in range(1, 4):
        total = total + send(turns[turn - 1], dz=turn).astype(jnp.float32)
    total = total.astype(jnp.bfloat16)
    (total,) = (yield [total]) or (total,)
    across = send(total, dx=1)
    own_x, other_x = total[:quarter], across[:quarter]
    owned = jnp.concatenate(
        [
            jnp.where(x == 0, own_x, other_x),
            jnp.where(x == 0, other_x, own_x),
            add_low(total[quarter:], across[quarter:]),
        ],
        axis=0,
    )
    (owned,) = (yield [owned]) or (owned,)
    beside = send(owned, dcore=1)
    return jnp.concatenate(
        [jnp.where(core == 0, owned, beside), jnp.where(core == 0, beside, owned)], axis=0
    )


def paired_reduce(grad):
    rows, columns = grad.shape[0] // 8, grad.shape[1]
    x, core, z, y = place()
    parts = grad.reshape(8, 2, rows // 2, columns)
    far = pick(parts, 1 - core, 1)
    yield [far]
    half = add_low(pick(parts, core, 1), send(far, dcore=1)).reshape(4 * rows, columns)
    yield [half]
    own = lax.psum_scatter(half, ("z", "y", "x"), scatter_dimension=0, tiled=True)
    yield None
    across = send(own, dx=1)
    owned = jnp.concatenate(
        [jnp.where(x == 0, own, across), jnp.where(x == 0, across, own)], axis=0
    )
    yield None
    beside = send(owned, dcore=1)
    return jnp.concatenate(
        [jnp.where(core == 0, owned, beside), jnp.where(core == 0, beside, owned)], axis=0
    )


def general_stages(grad, rep, shard):
    yield None
    return general_reduce(grad, rep, shard)


class Reductions:

    def __init__(self, axes):
        self.axes = axes
        self.running, self.results, self.waiting = {}, {}, {}

    def add(self, name, grad, paired=False):
        grad = grad.astype(jnp.bfloat16)
        if not tuned(self.axes):
            self.running[name] = general_stages(grad, *self.axes)
        elif paired:
            self.running[name] = paired_reduce(grad)
        else:
            self.running[name] = tuned_reduce(grad)

    def step(self, values):
        after = []
        for name in list(self.running):
            if self.waiting.get(name):
                continue
            ready = self.advance(name)
            if ready is None:
                self.waiting[name] = True
            else:
                after += ready
        return fence(values, after) if after else values

    def advance(self, name):
        try:
            return next(self.running[name])
        except StopIteration as stop:
            self.results[name] = stop.value
            del self.running[name]
            return []

    def interleave(self, first, second):
        next(self.running[first])
        reply = None
        try:
            while True:
                ahead = next(self.running[first])
                reply = fence(self.running[second].send(reply), ahead)
        except StopIteration as stop:
            self.results[second] = stop.value
            del self.running[second]

    def finish(self):
        while self.running:
            for name in list(self.running):
                self.advance(name)
        return self.results


def tuned(axes):
    return axes == (("x", "core"), ("z", "y"))


def gather_weights(axes, mixer_in, mixer_out, swiglu_in, swiglu_out, gains, conv_kernel):
    rows = mixer_in.shape[0]
    rep, shard = axes
    owners = lax.axis_size(shard)
    width = conv_kernel.shape[1]
    count = gains.shape[0] + conv_kernel.size
    lanes = -(-count // rows)
    vector = jnp.concatenate([gains, conv_kernel.reshape(-1)])
    vector = jnp.pad(vector, (0, lanes * rows - count)).reshape(rows, lanes)
    low_in = mixer_in.astype(jnp.bfloat16)
    tail = STEP_LANES - MH - lanes
    conv_piece = jnp.concatenate(
        [low_in[:, QKV + GATE :], vector.astype(jnp.bfloat16), jnp.zeros((rows, tail), jnp.bfloat16)],
        axis=1,
    )
    pieces = [conv_piece, low_in[:, : QKV + GATE]]
    if tuned(axes):
        pieces = tuned_gather(pieces)
    else:
        pieces = [general_gather(piece, rep, shard) for piece in pieces]
    if tuned(axes):
        w_out, w_down = gather_two(mixer_out, swiglu_out, rep, shard)
        pieces += [w_out, general_gather(swiglu_in.astype(jnp.bfloat16), rep, shard), w_down]
    else:
        for master in (mixer_out, swiglu_in, swiglu_out):
            pieces.append(general_gather(master.astype(jnp.bfloat16), rep, shard))
    every = pieces[0][:, CONV + MH : CONV + MH + lanes].reshape(owners, rows * lanes)
    gains_all = every[:, : gains.shape[0]].reshape(-1)
    taps = every[:, gains.shape[0] : count].reshape(owners, KC + 1, width)
    taps = jnp.swapaxes(taps, 0, 1).reshape(KC + 1, owners * width)
    return pieces + [gains_all.astype(jnp.float32), taps.astype(jnp.float32)]


def with_vectors(conv_g, gains_g, taps_g, head_grad, owners):
    rows = conv_g.shape[0] // owners
    width = taps_g.shape[1] // owners
    vector = jnp.concatenate(
        [
            gains_g.reshape(owners, -1),
            jnp.swapaxes(taps_g.reshape(KC + 1, owners, width), 0, 1).reshape(owners, -1),
            jnp.broadcast_to(head_grad.reshape(1, -1), (owners, head_grad.size)),
        ],
        axis=1,
    )
    count = vector.shape[1]
    lanes = -(-count // rows)
    vector = jnp.pad(vector, ((0, 0), (0, lanes * rows - count))).reshape(owners * rows, lanes)
    vector = jnp.pad(vector, ((0, 0), (MH, STEP_LANES - MH - lanes)))
    return jnp.concatenate([conv_g[:, :CONV], conv_g[:, CONV:] + vector], axis=1)


def split_vectors(conv, own_gains, width, head_shape):
    rows = conv.shape[0]
    count = own_gains + (KC + 1) * width + head_shape[0] * head_shape[1]
    lanes = -(-count // rows)
    used = CONV + MH
    flat = conv[:, used : used + lanes].astype(jnp.float32).reshape(-1)
    taps_end = own_gains + (KC + 1) * width
    return (
        flat[:own_gains],
        flat[own_gains:taps_end].reshape(KC + 1, width),
        flat[taps_end:count].reshape(head_shape),
    )


def forward_backward(axes, tokens, cotangent, seq_row, weights, head_params):
    low, low_back = make_rounders()
    w_conv, w_side, w_out, w_up, w_down, gain_all, taps = weights
    segment, token_position, valid = layout(seq_row, tokens.shape[0])
    values = tokens.astype(jnp.float32)
    context_width = QUERY_HEADS * HEAD_SIZE

    normed, pull_norm = jax.vjp(lambda v, g: low(normalize(v, g)), values, gain_all[:D])
    normed_low = rows_of(normed)
    projected = dot(normed_low, w_conv)
    conv_out, pull_conv = jax.vjp(
        lambda p, k: convolution(p, k, segment, low), projected[:, :CONV], taps
    )
    conv_low = rows_of(conv_out)
    (step_size, cumulative), pull_steps = jax.vjp(
        decay_steps, projected[:, CONV : CONV + MH], head_params
    )
    scan_out = scan_forward(conv_low, step_size, cumulative, head_params, segment)
    beside = dot(normed_low, w_side)
    context, pull_context = jax.vjp(
        lambda p: attention(p, segment, token_position, low, low_back), beside[:, :QKV]
    )
    mamba_out, pull_gating = jax.vjp(
        lambda s, z, g: gating(s, z, g, low), scan_out, beside[:, QKV:], gain_all[2 * D :]
    )
    joined = jnp.concatenate([rows_of(context), rows_of(mamba_out)], axis=1)
    hidden = values + dot(joined, w_out)
    normed_ff, pull_ff = jax.vjp(lambda v, g: low(normalize(v, g)), hidden, gain_all[D : 2 * D])
    normed_ff_low = rows_of(normed_ff)
    activated, pull_active = jax.vjp(lambda g: activation(g, low), dot(normed_ff_low, w_up))
    activated_low = rows_of(activated)
    output = (hidden + dot(activated_low, w_down)).astype(jnp.bfloat16)

    moving = Reductions(axes)
    cot = jnp.where(valid[:, None], cotangent, jnp.zeros_like(cotangent))
    (up_cot,) = pull_active(dot_right(cot, w_down))
    up_cot = rows_of(up_cot)
    moving.add("down", dot_left(activated_low, cot), paired=True)
    (up_cot,) = moving.step([up_cot])
    moving.add("up", dot_left(normed_ff_low, up_cot), paired=True)
    (ff_cot,) = moving.step([dot_right(up_cot, w_up)])
    hidden_part, gain_ff = pull_ff(ff_cot)
    hidden_cot = cot.astype(jnp.float32) + hidden_part
    hidden_low = rows_of(hidden_cot)
    moving.add("out", dot_left(joined, hidden_low), paired=True)
    (joined_cot,) = moving.step([dot_right(hidden_low, w_out)])
    scan_cot, gate_cot, gain_scan = pull_gating(joined_cot[:, context_width:])
    (qkv_cot,) = pull_context(joined_cot[:, :context_width])
    side_cot = jnp.concatenate([rows_of(qkv_cot), rows_of(gate_cot)], axis=1)
    moving.add("side", dot_left(normed_low, side_cot))
    (scan_cot,) = moving.step([scan_cot])
    conv_out_cot, dstep, dcum, dskip = scan_backward(
        scan_cot, scan_out, conv_low, step_size, cumulative, head_params, segment
    )
    step_cot, head_grad = pull_steps((dstep, dcum))
    head_grad = head_grad.at[2].add(dskip)
    (conv_out_cot,) = moving.step([conv_out_cot])
    conv_cot, taps_grad = pull_conv(conv_out_cot)
    conv_cot = rows_of(
        jnp.concatenate(
            [conv_cot, step_cot, jnp.zeros((tokens.shape[0], STEP_LANES - MH), jnp.float32)], axis=1
        )
    )
    (conv_cot,) = moving.step([conv_cot])
    normed_cot = dot_right(side_cot, w_side) + dot_right(conv_cot, w_conv)
    tokens_part, gain_in = pull_norm(normed_cot)
    token_grad = hidden_cot + tokens_part
    gains_grad = jnp.concatenate([gain_in, gain_ff, gain_scan])
    owners = lax.axis_size(axes[1])
    moving.add(
        "conv",
        with_vectors(dot_left(normed_low, conv_cot), gains_grad, taps_grad, head_grad, owners),
    )
    if tuned(axes):
        moving.interleave("conv", "side")
    return output, token_grad, moving.finish()


def on_device(
    axes,
    tokens,
    cotangent,
    seq_lengths,
    mixer_in,
    mixer_in_mean,
    mixer_in_square,
    mixer_out,
    mixer_out_mean,
    mixer_out_square,
    swiglu_in,
    swiglu_in_mean,
    swiglu_in_square,
    swiglu_out,
    swiglu_out_mean,
    swiglu_out_square,
    gains,
    gains_mean,
    gains_square,
    conv_kernel,
    conv_kernel_mean,
    conv_kernel_square,
    head_params,
    head_params_mean,
    head_params_square,
):
    weights = gather_weights(axes, mixer_in, mixer_out, swiglu_in, swiglu_out, gains, conv_kernel)
    output, token_grad, sums = forward_backward(
        axes, tokens, cotangent, seq_lengths[0], weights, head_params
    )
    own_gains, own_taps, head_grad = split_vectors(
        sums["conv"], gains.shape[0], conv_kernel.shape[1], head_params.shape
    )
    matrix = jnp.concatenate([sums["side"].T, sums["conv"][:, : CONV + MH].T], axis=0)
    owned = (
        matrix.astype(jnp.float32),
        sums["out"].astype(jnp.float32),
        sums["up"].astype(jnp.float32),
        sums["down"].astype(jnp.float32),
        own_gains,
        own_taps,
    )
    masters = (mixer_in, mixer_out, swiglu_in, swiglu_out, gains, conv_kernel)
    means = (
        mixer_in_mean,
        mixer_out_mean,
        swiglu_in_mean,
        swiglu_out_mean,
        gains_mean,
        conv_kernel_mean,
    )
    squares = (
        mixer_in_square,
        mixer_out_square,
        swiglu_in_square,
        swiglu_out_square,
        gains_square,
        conv_kernel_square,
    )
    rates = (MATRIX_RATE, MATRIX_RATE, MATRIX_RATE, MATRIX_RATE, VECTOR_RATE, VECTOR_RATE)
    turned = adamw(mixer_in.T, mixer_in_mean.T, mixer_in_square.T, owned[0], rates[0])
    updated = [tuple(array.T for array in turned)] + [
        adamw(masters[index], means[index], squares[index], owned[index], rates[index])
        for index in range(1, 6)
    ]
    head_new = adamw(head_params, head_params_mean, head_params_square, head_grad, VECTOR_RATE)
    return (
        output,
        token_grad,
        updated[0][0],
        updated[0][1],
        updated[0][2],
        updated[1][0],
        updated[1][1],
        updated[1][2],
        updated[2][0],
        updated[2][1],
        updated[2][2],
        updated[3][0],
        updated[3][1],
        updated[3][2],
        updated[4][0],
        updated[4][1],
        updated[4][2],
        updated[5][0],
        updated[5][1],
        updated[5][2],
        head_new[0],
        head_new[1],
        head_new[2],
    )


def solution(mesh):
    rep, shard = ("rep",), ("shard",)
    if mesh.shape["rep"] == 4 and mesh.shape["shard"] == 8:
        rep, shard = ("x", "core"), ("z", "y")
        mesh = Mesh(mesh.devices.reshape(2, 2, 4, 2), rep + shard)
    rows, owned, across, copied = P(rep + shard, None), P(shard, None), P(None, shard), P()
    optimizer = (owned,) * 12 + (P(shard),) * 3 + (across,) * 3 + (copied,) * 3
    return jax.shard_map(
        functools.partial(on_device, (rep, shard)),
        mesh=mesh,
        in_specs=(rows, rows, rows) + optimizer,
        out_specs=(rows, rows) + optimizer,
        check_vma=False,
    )
```
